128 devices in a mesh: gx: 8 (over x, core), gy: 16 (over z, y).
Axes of the slice: x: 4, y: 4, z: 4, core: 2. Of those that a mesh axis runs over, the one named last changes fastest.
Arguments:
- estimate: float32 [2, 1024, 2048], P(None, 'gx', 'gy'), may hold values from 0.24 to 5.3
- views: bfloat16 [4, 2, 1024, 2048], P(None, None, 'gx', 'gy'), may hold values from 0.18 to 7
- psf_rows: float32 [4, 31], replicated, may hold values from 0.05 to 1
- psf_cols: float32 [4, 31], replicated, may hold values from 0.05 to 1
- shifts: int32 [4, 128], P(None, 'gx'), may hold values from 0 to 15, as said below
- codes: int32 [4, 128, 16], P(None, 'gx', 'gy'), may hold values from 0 to 15
Outputs:
- updated: float32 [2, 1024, 2048], P(None, 'gx', 'gy')
The draws below stay inside these ranges and needn't reach their ends.
Inputs may be any that keep to these rules, and one draw needn't show every extreme that they name: `shifts`: within each view and each group of 16 consecutive block rows that starts at a multiple of 16, no displacement occurs more than 2 times, and one occurs exactly 2 times.
All inputs are finite; a program needn't handle non-finite values.
Results may differ from the reference program's by a relative error of at most 0.0003.
Values sent between devices are 32-bit elements; how exact they have to be, the bound alone decides.
No kernel may reach another device: no remote copies, remote signals or barrier semaphores. Data moves between devices by JAX's collectives and lax.ppermute only.
A program may use at most 64 MiB of HBM per device.

```python
import math
import jax
import jax.numpy as jnp
from jax import lax

Z = 2
TR = 128
TW = 128
BR = 8
V = 4
TAPS = 31
ITERS = 2
NBR = 128
NR = 1024
NC = 2048
N_GY = 16


def banded_field(key, count, lowest, highest, planes, rows, cols):
    period_key, angle_key, phase_key, drift_key, height_key, sign_key = jax.random.split(key, 6)
    periods = jnp.exp(jax.random.uniform(period_key, (count,), jnp.float32, math.log(20.0), math.log(120.0)))
    angles = jax.random.uniform(angle_key, (count,), jnp.float32, 0.0, 2.0 * math.pi)
    phases = jax.random.uniform(phase_key, (count,), jnp.float32, 0.0, 2.0 * math.pi)
    drifts = jax.random.uniform(drift_key, (count,), jnp.float32, -0.4, 0.4)
    heights = jax.random.uniform(height_key, (count,), jnp.float32, lowest, highest)
    signs = jnp.where(jax.random.bernoulli(sign_key, 0.5, (count,)), 1.0, -1.0).astype(jnp.float32)
    plane_pos = jnp.arange(planes, dtype=jnp.float32)[:, None, None]
    row_pos = jnp.arange(rows, dtype=jnp.float32)[None, :, None]
    col_pos = jnp.arange(cols, dtype=jnp.float32)[None, None, :]
    total = jnp.zeros((planes, rows, cols), jnp.float32)
    for index in range(count):
        phase_arg = (row_pos * jnp.cos(angles[index]) + col_pos * jnp.sin(angles[index])) * (2.0 * math.pi / periods[index])
        phase_arg = phase_arg + phases[index] + drifts[index] * plane_pos
        total = total + signs[index] * heights[index] * jnp.tanh(5.0 * jnp.sin(phase_arg))
    return total


def draw_shifts(key, part):
    key = jax.random.fold_in(key, 7)
    groups = NC // TW
    tile_count = NR // TR
    blocks = TR // BR
    subkeys = jax.random.split(key, V * tile_count)
    pattern = jnp.concatenate([jnp.zeros((1,), jnp.int32), jnp.arange(blocks - 1, dtype=jnp.int32)]) % groups

    def draw_group(subkey):
        first_key, second_key = jax.random.split(subkey)
        column_order = jax.random.permutation(first_key, groups).astype(jnp.int32)
        slot_order = jax.random.permutation(second_key, blocks).astype(jnp.int32)
        return column_order[pattern[slot_order]]
    return jax.vmap(draw_group)(subkeys).reshape(V, tile_count * blocks).astype(jnp.int32)


def draw_estimate(key, part):
    shared = banded_field(key, 3, 0.2, 0.35, Z, NR, NC)
    key = jax.random.fold_in(key, 11)
    noise_key = jax.random.fold_in(key, 0)
    rough = jax.random.uniform(noise_key, (Z, NR, NC), jnp.float32, -0.35, 0.35)
    return jnp.exp(shared + rough).astype(jnp.float32)


def draw_views(key, part):
    shared = banded_field(key, 3, 0.2, 0.35, Z, NR, NC)
    key = jax.random.fold_in(key, 13)
    layers = []
    for view_id in range(V):
        view_key = jax.random.fold_in(key, view_id)
        own_key, noise_key = jax.random.split(view_key, 2)
        own = banded_field(own_key, 2, 0.2, 0.35, Z, NR, NC)
        rough = jax.random.uniform(noise_key, (Z, NR, NC), jnp.float32, -0.35, 0.35)
        layers.append(jnp.exp(0.6 * shared + own + rough))
    return jnp.stack(layers).astype(jnp.bfloat16)


def with_ends(drawn, rng, low, high):
    spot = [jax.random.randint(jax.random.fold_in(rng, axis), (), 0, length) for axis, length in enumerate(drawn.shape)]
    widest = drawn.shape.index(max(drawn.shape))
    next_to = spot[:widest] + [(spot[widest] + 1) % drawn.shape[widest]] + spot[widest + 1:]
    return drawn.at[tuple(spot)].set(low).at[tuple(next_to)].set(high)


def setup_inputs(seed: int = 0) -> dict:
    streams_of = jax.random.split(jax.random.key(seed), 7)
    estimate = draw_estimate(jax.random.fold_in(streams_of[6], 71), 0)
    views = draw_views(jax.random.fold_in(streams_of[6], 71), 0)
    psf_rows = jnp.clip(jnp.exp(jax.random.uniform(streams_of[2], (V, TAPS), jnp.float32, math.log(0.05), math.log(1.0))), 0.05, 1.0)
    psf_cols = jnp.clip(jnp.exp(jax.random.uniform(streams_of[3], (V, TAPS), jnp.float32, math.log(0.05), math.log(1.0))), 0.05, 1.0)
    shifts = draw_shifts(jax.random.fold_in(streams_of[6], 71), 0)
    codes = with_ends(jax.random.randint(streams_of[5], (V, NBR, N_GY), 0, 16), jax.random.fold_in(streams_of[5], 1), 0, 15).astype(jnp.int32)
    return {"estimate": estimate, "views": views, "psf_rows": psf_rows, "psf_cols": psf_cols, "shifts": shifts, "codes": codes}


def shift_in(values, fraction):
    last = values.shape[-1] - 1
    column = lax.broadcasted_iota(jnp.int32, values.shape, values.ndim - 1)
    following = jnp.concatenate([values[..., 1:], values[..., -1:]], axis=-1)
    return jnp.where(column < last, (1.0 - fraction) * values + fraction * following, values)


def shift_back(values, fraction):
    last = values.shape[-1] - 1
    column = lax.broadcasted_iota(jnp.int32, values.shape, values.ndim - 1)
    preceding = jnp.concatenate([jnp.zeros_like(values[..., :1]), values[..., :-1]], axis=-1)
    own_part = jnp.where(column < last, (1.0 - fraction) * values, values)
    return own_part + fraction * preceding


def smooth_rows(padded, taps, count):
    total = taps[0] * padded[..., 0:count, :]
    for offset in range(1, taps.shape[0]):
        total = total + taps[offset] * padded[..., offset:offset + count, :]
    return total


def smooth_cols(padded, taps, count):
    total = taps[0] * padded[..., 0:count]
    for offset in range(1, taps.shape[0]):
        total = total + taps[offset] * padded[..., offset:offset + count]
    return total


def blur_field(field, taps_rows, taps_cols):
    half = taps_rows.shape[0] // 2
    padded = jnp.pad(field, ((0, 0), (half, half), (0, 0)))
    rows_done = smooth_rows(padded, taps_rows, field.shape[1])
    padded = jnp.pad(rows_done, ((0, 0), (0, 0), (half, half)))
    return smooth_cols(padded, taps_cols, field.shape[2])


def reference(estimate, views, psf_rows, psf_cols, shifts, codes):
    groups = codes.shape[2]
    depth, total_rows, total_cols = estimate.shape
    tile_cols = total_cols // groups
    block_count = total_rows // BR
    kern_rows = psf_rows / jnp.sum(psf_rows, axis=1, keepdims=True)
    kern_cols = psf_cols / jnp.sum(psf_cols, axis=1, keepdims=True)
    peer_ids = jnp.arange(groups, dtype=jnp.int32)
    for sweep in range(ITERS):
        blocked = estimate.reshape(depth, block_count, BR, groups, tile_cols)
        summed = jnp.zeros(estimate.shape, jnp.float32)
        for view_id in range(V):
            fraction = (codes[view_id].astype(jnp.float32) / 16.0)[None, :, None, :, None]
            fetch = ((peer_ids[None, :] + shifts[view_id][:, None]) % groups).astype(jnp.int32)
            fetch_index = jnp.broadcast_to(fetch[None, :, None, :, None], blocked.shape)
            moved = jnp.take_along_axis(blocked, fetch_index, axis=3)
            view_est = shift_in(moved, fraction).reshape(depth, total_rows, total_cols)
            blurred = blur_field(view_est, kern_rows[view_id], kern_cols[view_id])
            ratio = views[view_id].astype(jnp.float32) / blurred
            back = blur_field(ratio, kern_rows[view_id][::-1], kern_cols[view_id][::-1])
            returned = shift_back(back.reshape(blocked.shape), fraction)
            home = ((peer_ids[None, :] - shifts[view_id][:, None]) % groups).astype(jnp.int32)
            home_index = jnp.broadcast_to(home[None, :, None, :, None], blocked.shape)
            summed = summed + jnp.take_along_axis(returned, home_index, axis=3).reshape(estimate.shape)
        estimate = estimate * (summed / V)
    return estimate
```

```python
import functools

import jax
import jax.numpy as jnp
import numpy as np
from jax import lax
from jax.experimental import pallas as pl
from jax.experimental.pallas import tpu as pltpu
from jax.sharding import PartitionSpec as P

ITERS = 2
V = 4
Z = 2
T = 128
ROWS = 16
GY = 16
GX = 8
CHUNKS = 64
META = 16
UNIT = ROWS * (1 + V) + 8
PERM = (0, 1, 2, 3, 7, 6, 5, 4)
SNAKE = PERM + tuple(8 + p for p in PERM)
AXES = ("gx", "gy")
F32 = jnp.float32
BF16 = jnp.bfloat16
VMEM = pl.BlockSpec(memory_space=pltpu.VMEM)
SMEM = pl.BlockSpec(memory_space=pltpu.SMEM)
PARAMS = pltpu.CompilerParams(vmem_limit_bytes=48 * 1024 * 1024)


def device_of(core, chunk):
    place = (chunk % 16 + 8 * core) % 16
    return (2 * (chunk // 16) + core) * GY + SNAKE.index(place)


FORWARD = [
    (device_of(c, q), device_of(c, (q + 1) % CHUNKS)) for c in range(2) for q in range(CHUNKS)
]
BACKWARD = [(b, a) for a, b in FORWARD]
SWAP = [((2 * x + c) * GY + g, (2 * x + 1 - c) * GY + g)
        for x in range(GX // 2) for c in range(2) for g in range(GY)]


def split(x):
    hi = x.astype(BF16)
    return hi, (x - hi.astype(F32)).astype(BF16)


def pack_kernel(core_ref, codes_ref, shifts_ref, est_ref, views_ref, keep_ref, send_ref):
    core = core_ref[0]
    lane = lax.broadcasted_iota(jnp.int32, (8, T), 1)
    for slot in range(8):
        chunk = PERM[slot]
        rows = pl.ds(chunk * ROWS, ROWS)
        meta = jnp.zeros((8, T), F32)
        for half in range(2):
            for v in range(V):
                code = codes_ref[v, 2 * chunk + half].astype(F32)
                shift = shifts_ref[v, 2 * chunk + half].astype(F32)
                meta = jnp.where(lane == half * V + v, code, meta)
                meta = jnp.where(lane == 8 + half * V + v, shift, meta)
        for ref, plane in ((keep_ref, core), (send_ref, 1 - core)):
            ref[slot, 0:ROWS, :] = est_ref[plane, rows, :]
            for v in range(V):
                ref[slot, pl.ds(ROWS * (1 + v), ROWS), :] = views_ref[v, plane, rows, :].astype(F32)
            ref[slot, pl.ds(ROWS * (1 + V), 8), :] = meta


def taps_kernel(cols_ref, rows_ref, band_ref, row_ref, back_ref):
    for v in range(V):
        for d in range(2):
            base = jnp.broadcast_to(cols_ref[2 * v + d : 2 * v + d + 1, :], (2 * T, 2 * T))
            turned = pltpu.roll(base, 0, 1, stride=1, stride_axis=0)[:, :T]
            hi, lo = split(turned)
            band_ref[v, d, 0 : 2 * T, :] = hi
            band_ref[v, d, 2 * T : 4 * T, :] = lo
            band_ref[v, d, 4 * T : 6 * T, :] = hi
        base = jnp.broadcast_to(rows_ref[2 * v : 2 * v + 1, :], (ROWS, T))
        hi, lo = split(pltpu.roll(base, 0, 1, stride=1, stride_axis=0)[:, : 3 * ROWS])
        row_ref[v] = jnp.concatenate([hi, hi, lo], axis=1)
        base = jnp.broadcast_to(rows_ref[2 * v + 1 : 2 * v + 2, :], (3 * ROWS, T))
        hi, lo = split(pltpu.roll(base, 0, 1, stride=1, stride_axis=0)[:, :ROWS])
        back_ref[v] = jnp.concatenate([hi, hi, lo], axis=1)


def column_pass(pieces, band):
    lane = lax.broadcasted_iota(jnp.int32, (ROWS, T), 1)
    turned = [pltpu.roll(p, T // 2, 1) for p in pieces]
    zero = jnp.zeros((ROWS, T), F32)
    turned = [zero] + turned + [zero]
    moved = [
        jnp.where(lane < T // 2, turned[j], turned[j + 1]) for j in range(len(pieces) + 1)
    ]
    his, los = zip(*[split(m) for m in moved])
    left = len(pieces)

    def windows(parts):
        return jnp.concatenate(
            [jnp.concatenate([parts[c], parts[c + 1]], axis=1) for c in range(left)], axis=0
        )

    hi, lo = windows(his), windows(los)
    return jnp.dot(
        jnp.concatenate([hi, hi, lo], axis=1), band, preferred_element_type=F32
    )


def step_kernel(
    meta_ref, flag_ref, before_ref, own_ref, after_ref, arrived_ref, band_ref, row_ref, back_ref,
    low_ref, mid_ref, high_ref, est2, slope2, view_u, total2,
):
    lane = lax.broadcasted_iota(jnp.int32, (GY, 8, T), 2)
    inner = jnp.where(lane < T - 1, 1.0 / 16.0, 0.0).astype(F32)
    for src, ref in enumerate((before_ref, own_ref, after_ref)):
        for half in range(2):
            b = 2 * src + half
            x = ref[0 : GY * ROWS, :].reshape(GY, ROWS, T)[:, 8 * half : 8 * half + 8, :]
            if src != 1:
                x = x * flag_ref[src // 2]
            d = (pltpu.roll(x, T - 1, 2) - x) * inner
            est2[b, 0:GY] = x
            est2[b, GY : 2 * GY] = x
            slope2[b, 0:GY] = d
            slope2[b, GY : 2 * GY] = d
    total2[...] = jnp.zeros(total2.shape, F32)
    inner8 = inner[0]
    for v in range(V):
        for src in range(3):
            parts = []
            for half in range(2):
                b = 2 * src + half
                shift = meta_ref[src * GY, 8 + half * V + v]
                x = est2[b, pl.ds(shift, GY)]
                d = slope2[b, pl.ds(shift, GY)]
                parts.append([
                    x[c] + meta_ref[src * GY + c, half * V + v].astype(F32) * d[c]
                    for c in range(GY)
                ])
            for c in range(GY):
                hi, lo = split(jnp.concatenate([parts[0][c], parts[1][c]], axis=0))
                cols = slice(T * c, T * c + T)
                view_u[v, ROWS * src : ROWS * src + ROWS, cols] = hi
                view_u[v, ROWS * (3 + src) : ROWS * (4 + src), cols] = lo
                view_u[v, ROWS * (6 + src) : ROWS * (7 + src), cols] = hi
        smooth = jnp.dot(row_ref[v], view_u[v], preferred_element_type=F32)
        blurred = column_pass([smooth[:, T * c : T * c + T] for c in range(GY)], band_ref[v, 0])
        ratio = [
            arrived_ref[c, ROWS * (1 + v) : ROWS * (2 + v), :]
            / blurred[ROWS * c : ROWS * c + ROWS, :]
            for c in range(GY)
        ]
        again = column_pass(ratio, band_ref[v, 1])
        his, los = zip(*[split(again[ROWS * c : ROWS * c + ROWS, :]) for c in range(GY)])
        hi, lo = jnp.concatenate(his, axis=1), jnp.concatenate(los, axis=1)
        spread = jnp.dot(
            back_ref[v], jnp.concatenate([hi, lo, hi], axis=0), preferred_element_type=F32
        )
        for b in range(6):
            src, half = b // 2, b % 2
            shift = meta_ref[src * GY, 8 + half * V + v]
            parts = []
            for c in range(GY):
                r = spread[8 * b : 8 * b + 8, T * c : T * c + T]
                g = r * inner8
                g = pltpu.roll(g, 1, 1) - g
                parts.append(r + meta_ref[src * GY + c, half * V + v].astype(F32) * g)
            total2[b, pl.ds(shift, GY)] += jnp.stack(parts)
    for src, ref in enumerate((low_ref, mid_ref, high_ref)):
        for half in range(2):
            b = 2 * src + half
            y = total2[b, 0:GY] + total2[b, GY : 2 * GY]
            for c in range(GY):
                ref[ROWS * c + 8 * half : ROWS * c + 8 * half + 8, :] = y[c]


def place(base, width, taps, at):
    left = at
    return jnp.pad(taps, ((0, 0), (left, width - left - taps.shape[1])))


def body(estimate, views, psf_rows, psf_cols, shifts, codes):
    core = lax.axis_index("gx") % 2
    group = lax.axis_index("gx") // 2
    gy = lax.axis_index("gy")
    within = gy % 4 + 4 * (gy // 4)
    within = jnp.where((gy // 4) % 2 == 0, within, 4 * (gy // 4) + 3 - gy % 4)
    chunk = group * 16 + (within + 8 * core) % 16
    flags = jnp.stack([chunk > 0, chunk < CHUNKS - 1]).astype(F32)

    unit = jax.ShapeDtypeStruct((8, UNIT, T), F32)
    keep, send = pl.pallas_call(
        pack_kernel,
        out_shape=(unit, unit),
        in_specs=[SMEM, SMEM, SMEM, VMEM, VMEM],
        out_specs=(VMEM, VMEM),
        compiler_params=PARAMS,
        name="pack",
    )(core.reshape(1), codes[:, :, 0], shifts, estimate, views)
    other = lax.ppermute(send, AXES, SWAP)

    rows_n = psf_rows / jnp.sum(psf_rows, axis=1, keepdims=True)
    cols_n = psf_cols / jnp.sum(psf_cols, axis=1, keepdims=True)
    col_base = jnp.stack(
        [place(None, 2 * T, cols_n[:, ::-1], 177), place(None, 2 * T, cols_n, 177)], axis=1
    ).reshape(2 * V, 2 * T)
    row_base = jnp.stack(
        [place(None, T, rows_n, 1), place(None, T, rows_n[:, ::-1], T - 31)], axis=1
    ).reshape(2 * V, T)
    band, row_mat, back_mat = pl.pallas_call(
        taps_kernel,
        out_shape=(
            jax.ShapeDtypeStruct((V, 2, 6 * T, T), BF16),
            jax.ShapeDtypeStruct((V, ROWS, 9 * ROWS), BF16),
            jax.ShapeDtypeStruct((V, 3 * ROWS, 3 * ROWS), BF16),
        ),
        in_specs=[VMEM, VMEM],
        out_specs=(VMEM, VMEM, VMEM),
        compiler_params=PARAMS,
        name="taps",
    )(col_base, row_base)

    arrived = lax.all_to_all(
        jnp.concatenate([keep, other], axis=0), "gy", split_axis=0, concat_axis=0, tiled=True
    )
    own = arrived[:, :ROWS, :].reshape(GY * ROWS, T)
    own_meta = arrived[:, ROWS * (1 + V), :]
    meta = None
    step = pl.pallas_call(
        step_kernel,
        out_shape=(jax.ShapeDtypeStruct((GY * ROWS, T), F32),) * 3,
        in_specs=[SMEM, SMEM] + [VMEM] * 7,
        out_specs=(VMEM,) * 3,
        scratch_shapes=[
            pltpu.VMEM((6, 2 * GY, 8, T), F32),
            pltpu.VMEM((6, 2 * GY, 8, T), F32),
            pltpu.VMEM((V, 9 * ROWS, GY * T), BF16),
            pltpu.VMEM((6, 2 * GY, 8, T), F32),
        ],
        compiler_params=PARAMS,
        name="step",
    )
    for sweep in range(ITERS):
        out = jnp.concatenate([own, own_meta], axis=0) if sweep == 0 else own
        before = lax.ppermute(out, AXES, FORWARD)
        after = lax.ppermute(out, AXES, BACKWARD)
        if sweep == 0:
            meta = jnp.concatenate(
                [before[GY * ROWS :, :META], own_meta[:, :META], after[GY * ROWS :, :META]], axis=0
            ).astype(jnp.int32)
        low, mid, high = step(meta, flags, before, own, after, arrived, band, row_mat, back_mat)
        from_after = lax.ppermute(low, AXES, BACKWARD)
        from_before = lax.ppermute(high, AXES, FORWARD)
        own = own * ((mid + from_before * flags[0] + from_after * flags[1]) * 0.25)
    home = lax.all_to_all(
        own.reshape(GY, ROWS, T), "gy", split_axis=0, concat_axis=0, tiled=True
    )
    mine, theirs = home[:8], home[8:]
    got = lax.ppermute(theirs, AXES, SWAP)

    def ordered(part):
        return jnp.concatenate([part[PERM.index(q)] for q in range(8)], axis=0)

    mine, got = ordered(mine), ordered(got)
    return jnp.where(core == 0, jnp.stack([mine, got]), jnp.stack([got, mine]))


def solution(mesh):
    placed = (
        P(None, "gx", "gy"),
        P(None, None, "gx", "gy"),
        P(),
        P(),
        P(None, "gx"),
        P(None, "gx", "gy"),
    )
    return jax.shard_map(
        body, mesh=mesh, in_specs=placed, out_specs=P(None, "gx", "gy"), check_vma=False
    )
```

```python
import jax
import jax.numpy as jnp
from jax import lax
from jax.experimental import pallas as pl
from jax.experimental.pallas import tpu as pltpu
from jax.sharding import PartitionSpec as P

ITERS = 2
V = 4
Z = 2
T = 128
ROWS = 16
GY = 16
GX = 8
CHUNKS = 64
META = 16
UNIT = ROWS * (1 + V) + 8
PERM = (0, 1, 2, 3, 7, 6, 5, 4)
SNAKE = PERM + tuple(8 + p for p in PERM)
AXES = ("gx", "gy")
F32 = jnp.float32
BF16 = jnp.bfloat16
VMEM = pl.BlockSpec(memory_space=pltpu.VMEM)
HBM = pl.BlockSpec(memory_space=pltpu.HBM)
SMEM = pl.BlockSpec(memory_space=pltpu.SMEM)
PARAMS = pltpu.CompilerParams(vmem_limit_bytes=48 * 1024 * 1024)


def device_of(core, chunk):
    group = chunk // 16
    within = chunk % 16 if group % 2 == 0 else 15 - chunk % 16
    return (2 * group + core) * GY + SNAKE.index((within + 8 * core) % 16)


def here():
    core, group = lax.axis_index("gx") % 2, lax.axis_index("gx") // 2
    row, col = lax.axis_index("gy") // 4, lax.axis_index("gy") % 4
    place = 4 * row + jnp.where(row % 2 == 0, col, 3 - col)
    within = (place + 8 * core) % 16
    odd = group % 2
    return core, odd, 16 * group + jnp.where(odd == 0, within, 15 - within)


def slot_chunk(slot, odd):
    return jnp.where(odd == 0, PERM[slot], 7 - PERM[slot])


FORWARD = [
    (device_of(c, q), device_of(c, (q + 1) % CHUNKS)) for c in range(2) for q in range(CHUNKS)
]
BACKWARD = [(b, a) for a, b in FORWARD]
SWAP = [((2 * x + c) * GY + g, (2 * x + 1 - c) * GY + g)
        for x in range(GX // 2) for c in range(2) for g in range(GY)]


def split(x):
    hi = x.astype(BF16)
    return hi, (x - hi.astype(F32)).astype(BF16)


def pack_kernel(
    codes_hbm, shifts_hbm, est_hbm, views_hbm, keep_ref, send_ref, codes_ref, shifts_ref, est, views, sems
):
    core, odd, _ = here()
    copies = [
        pltpu.make_async_copy(codes_hbm, codes_ref, sems.at[0]),
        pltpu.make_async_copy(shifts_hbm, shifts_ref, sems.at[1]),
        pltpu.make_async_copy(est_hbm, est, sems.at[2]),
        pltpu.make_async_copy(views_hbm, views, sems.at[3]),
    ]
    for copy in copies:
        copy.start()
    for copy in copies:
        copy.wait()
    lane = lax.broadcasted_iota(jnp.int32, (8, T), 1)
    for slot in range(8):
        chunk = slot_chunk(slot, odd)
        rows = pl.ds(pl.multiple_of(chunk * ROWS, ROWS), ROWS)
        meta = jnp.zeros((8, T), F32)
        for half in range(2):
            for v in range(V):
                code = codes_ref[v, 2 * chunk + half].astype(F32)
                shift = shifts_ref[v, 2 * chunk + half].astype(F32)
                meta = jnp.where(lane == half * V + v, code, meta)
                meta = jnp.where(lane == 8 + half * V + v, shift, meta)
        for ref, plane in ((keep_ref, core), (send_ref, 1 - core)):
            ref[slot, 0:ROWS, :] = est[plane, rows, :]
            for v in range(V):
                ref[slot, pl.ds(ROWS * (1 + v), ROWS), :] = views[v, plane, rows, :].astype(F32)
            ref[slot, pl.ds(ROWS * (1 + V), 8), :] = meta


def join_kernel(keep_ref, other_ref, out_hbm, sems):
    _, odd, _ = here()
    copies = [
        pltpu.make_async_copy(keep_ref, out_hbm.at[pl.ds(8 * odd, 8)], sems.at[0]),
        pltpu.make_async_copy(other_ref, out_hbm.at[pl.ds(8 - 8 * odd, 8)], sems.at[1]),
    ]
    for copy in copies:
        copy.start()
    for copy in copies:
        copy.wait()


def update_kernel(own_ref, mid_ref, low_ref, high_ref, out_ref):
    _, _, chunk = here()
    has_before = jnp.where(chunk > 0, 1.0, 0.0).astype(F32)
    has_after = jnp.where(chunk < CHUNKS - 1, 1.0, 0.0).astype(F32)
    total = mid_ref[...] + high_ref[...] * has_before + low_ref[...] * has_after
    out_ref[...] = own_ref[0 : GY * ROWS, :] * (total * 0.25)


def unpack_kernel(home_ref, got_ref, out_ref):
    core, odd, _ = here()
    for slot in range(8):
        rows = pl.ds(pl.multiple_of(slot_chunk(slot, odd) * ROWS, ROWS), ROWS)
        out_ref[core, rows, :] = home_ref[8 * odd + slot]
        out_ref[1 - core, rows, :] = got_ref[slot]


def taps_kernel(cols_ref, rows_ref, band_ref, row_ref, back_ref):
    for v in range(V):
        for d in range(2):
            base = jnp.broadcast_to(cols_ref[2 * v + d : 2 * v + d + 1, :], (2 * T, 2 * T))
            turned = pltpu.roll(base, 0, 1, stride=1, stride_axis=0)[:, :T]
            hi, lo = split(turned)
            band_ref[v, d, 0 : 2 * T, :] = hi
            band_ref[v, d, 2 * T : 4 * T, :] = lo
            band_ref[v, d, 4 * T : 6 * T, :] = hi
        base = jnp.broadcast_to(rows_ref[2 * v : 2 * v + 1, :], (ROWS, T))
        hi, lo = split(pltpu.roll(base, 0, 1, stride=1, stride_axis=0)[:, : 3 * ROWS])
        row_ref[v] = jnp.concatenate([hi, hi, lo], axis=1)
        base = jnp.broadcast_to(rows_ref[2 * v + 1 : 2 * v + 2, :], (3 * ROWS, T))
        hi, lo = split(pltpu.roll(base, 0, 1, stride=1, stride_axis=0)[:, :ROWS])
        back_ref[v] = jnp.concatenate([hi, hi, lo], axis=1)


def column_pass(pieces, band):
    lane = lax.broadcasted_iota(jnp.int32, (ROWS, T), 1)
    turned = [pltpu.roll(p, T // 2, 1) for p in pieces]
    zero = jnp.zeros((ROWS, T), F32)
    turned = [zero] + turned + [zero]
    moved = [
        jnp.where(lane < T // 2, turned[j], turned[j + 1]) for j in range(len(pieces) + 1)
    ]
    his, los = zip(*[split(m) for m in moved])
    left = len(pieces)

    def windows(parts):
        return jnp.concatenate(
            [jnp.concatenate([parts[c], parts[c + 1]], axis=1) for c in range(left)], axis=0
        )

    hi, lo = windows(his), windows(los)
    return jnp.dot(
        jnp.concatenate([hi, hi, lo], axis=1), band, preferred_element_type=F32
    )


def step_kernel(
    meta_ref, before_ref, own_ref, after_ref, arrived_ref, band_ref, row_ref, back_ref,
    low_ref, mid_ref, high_ref, est2, slope2, view_u, total2,
):
    _, _, here_chunk = here()
    inside = {0: here_chunk > 0, 2: here_chunk < CHUNKS - 1}
    lane = lax.broadcasted_iota(jnp.int32, (GY, 8, T), 2)
    inner = jnp.where(lane < T - 1, 1.0 / 16.0, 0.0).astype(F32)
    for src, ref in enumerate((before_ref, own_ref, after_ref)):
        for half in range(2):
            b = 2 * src + half
            x = ref[0 : GY * ROWS, :].reshape(GY, ROWS, T)[:, 8 * half : 8 * half + 8, :]
            if src != 1:
                x = x * jnp.where(inside[src], 1.0, 0.0).astype(F32)
            d = (pltpu.roll(x, T - 1, 2) - x) * inner
            est2[b, 0:GY] = x
            est2[b, GY : 2 * GY] = x
            slope2[b, 0:GY] = d
            slope2[b, GY : 2 * GY] = d
    total2[...] = jnp.zeros(total2.shape, F32)
    inner8 = inner[0]
    for v in range(V):
        for src in range(3):
            parts = []
            for half in range(2):
                b = 2 * src + half
                shift = meta_ref[src * GY, 8 + half * V + v]
                x = est2[b, pl.ds(shift, GY)]
                d = slope2[b, pl.ds(shift, GY)]
                parts.append([
                    x[c] + meta_ref[src * GY + c, half * V + v].astype(F32) * d[c]
                    for c in range(GY)
                ])
            for c in range(GY):
                hi, lo = split(jnp.concatenate([parts[0][c], parts[1][c]], axis=0))
                cols = slice(T * c, T * c + T)
                view_u[v, ROWS * src : ROWS * src + ROWS, cols] = hi
                view_u[v, ROWS * (3 + src) : ROWS * (4 + src), cols] = lo
                view_u[v, ROWS * (6 + src) : ROWS * (7 + src), cols] = hi
        smooth = jnp.dot(row_ref[v], view_u[v], preferred_element_type=F32)
        blurred = column_pass([smooth[:, T * c : T * c + T] for c in range(GY)], band_ref[v, 0])
        ratio = [
            arrived_ref[c, ROWS * (1 + v) : ROWS * (2 + v), :]
            / blurred[ROWS * c : ROWS * c + ROWS, :]
            for c in range(GY)
        ]
        again = column_pass(ratio, band_ref[v, 1])
        his, los = zip(*[split(again[ROWS * c : ROWS * c + ROWS, :]) for c in range(GY)])
        hi, lo = jnp.concatenate(his, axis=1), jnp.concatenate(los, axis=1)
        spread = jnp.dot(
            back_ref[v], jnp.concatenate([hi, lo, hi], axis=0), preferred_element_type=F32
        )
        for b in range(6):
            src, half = b // 2, b % 2
            shift = meta_ref[src * GY, 8 + half * V + v]
            parts = []
            for c in range(GY):
                r = spread[8 * b : 8 * b + 8, T * c : T * c + T]
                g = r * inner8
                g = pltpu.roll(g, 1, 1) - g
                parts.append(r + meta_ref[src * GY + c, half * V + v].astype(F32) * g)
            total2[b, pl.ds(shift, GY)] += jnp.stack(parts)
    for src, ref in enumerate((low_ref, mid_ref, high_ref)):
        for half in range(2):
            b = 2 * src + half
            y = total2[b, 0:GY] + total2[b, GY : 2 * GY]
            for c in range(GY):
                ref[ROWS * c + 8 * half : ROWS * c + 8 * half + 8, :] = y[c]


def place(base, width, taps, at):
    left = at
    return jnp.pad(taps, ((0, 0), (left, width - left - taps.shape[1])))


def body(estimate, views, psf_rows, psf_cols, shifts, codes):
    _, odd, _ = here()
    unit = jax.ShapeDtypeStruct((8, UNIT, T), F32)
    keep, send = pl.pallas_call(
        pack_kernel,
        out_shape=(unit, unit),
        in_specs=[HBM] * 4,
        out_specs=(VMEM, VMEM),
        scratch_shapes=[
            pltpu.SMEM((V, 2 * 8), jnp.int32),
            pltpu.SMEM((V, 2 * 8), jnp.int32),
            pltpu.VMEM((Z, T, T), F32),
            pltpu.VMEM((V, Z, T, T), BF16),
            pltpu.SemaphoreType.DMA((4,)),
        ],
        compiler_params=PARAMS,
        name="pack",
    )(codes[:, :, 0], shifts, estimate, views)
    other = lax.ppermute(send, AXES, SWAP)

    rows_n = psf_rows / jnp.sum(psf_rows, axis=1, keepdims=True)
    cols_n = psf_cols / jnp.sum(psf_cols, axis=1, keepdims=True)
    col_base = jnp.stack(
        [place(None, 2 * T, cols_n[:, ::-1], 177), place(None, 2 * T, cols_n, 177)], axis=1
    ).reshape(2 * V, 2 * T)
    row_base = jnp.stack(
        [place(None, T, rows_n, 1), place(None, T, rows_n[:, ::-1], T - 31)], axis=1
    ).reshape(2 * V, T)
    band, row_mat, back_mat = pl.pallas_call(
        taps_kernel,
        out_shape=(
            jax.ShapeDtypeStruct((V, 2, 6 * T, T), BF16),
            jax.ShapeDtypeStruct((V, ROWS, 9 * ROWS), BF16),
            jax.ShapeDtypeStruct((V, 3 * ROWS, 3 * ROWS), BF16),
        ),
        in_specs=[VMEM, VMEM],
        out_specs=(VMEM, VMEM, VMEM),
        compiler_params=PARAMS,
        name="taps",
    )(col_base, row_base)

    joined = pl.pallas_call(
        join_kernel,
        out_shape=jax.ShapeDtypeStruct((GY, UNIT, T), F32),
        in_specs=[VMEM, VMEM],
        out_specs=HBM,
        scratch_shapes=[pltpu.SemaphoreType.DMA((2,))],
        compiler_params=PARAMS,
        name="join",
    )(keep, other)
    arrived = lax.all_to_all(joined, "gy", split_axis=0, concat_axis=0, tiled=True)
    own = arrived[:, :ROWS, :].reshape(GY * ROWS, T)
    own_meta = arrived[:, ROWS * (1 + V), :]
    update = pl.pallas_call(
        update_kernel,
        out_shape=jax.ShapeDtypeStruct((GY * ROWS, T), F32),
        in_specs=[VMEM] * 4,
        out_specs=VMEM,
        compiler_params=PARAMS,
        name="update",
    )
    step = pl.pallas_call(
        step_kernel,
        out_shape=(jax.ShapeDtypeStruct((GY * ROWS, T), F32),) * 3,
        in_specs=[SMEM] + [VMEM] * 7,
        out_specs=(VMEM,) * 3,
        scratch_shapes=[
            pltpu.VMEM((6, 2 * GY, 8, T), F32),
            pltpu.VMEM((6, 2 * GY, 8, T), F32),
            pltpu.VMEM((V, 9 * ROWS, GY * T), BF16),
            pltpu.VMEM((6, 2 * GY, 8, T), F32),
        ],
        compiler_params=PARAMS,
        name="step",
    )
    for sweep in range(ITERS):
        out = jnp.concatenate([own, own_meta], axis=0) if sweep == 0 else own
        before = lax.ppermute(out, AXES, FORWARD)
        after = lax.ppermute(out, AXES, BACKWARD)
        if sweep == 0:
            meta = jnp.concatenate(
                [before[GY * ROWS :, :META], own_meta[:, :META], after[GY * ROWS :, :META]], axis=0
            ).astype(jnp.int32)
        low, mid, high = step(meta, before, own, after, arrived, band, row_mat, back_mat)
        from_after = lax.ppermute(low, AXES, BACKWARD)
        from_before = lax.ppermute(high, AXES, FORWARD)
        own = update(own, mid, from_after, from_before)
    home = lax.all_to_all(
        own.reshape(GY, ROWS, T), "gy", split_axis=0, concat_axis=0, tiled=True
    )
    got = lax.ppermute(lax.dynamic_slice_in_dim(home, 8 - 8 * odd, 8, 0), AXES, SWAP)
    return pl.pallas_call(
        unpack_kernel,
        out_shape=jax.ShapeDtypeStruct((Z, T, T), F32),
        in_specs=[VMEM, VMEM],
        out_specs=VMEM,
        compiler_params=PARAMS,
        name="unpack",
    )(home, got)


def solution(mesh):
    placed = (
        P(None, "gx", "gy"),
        P(None, None, "gx", "gy"),
        P(),
        P(),
        P(None, "gx"),
        P(None, "gx", "gy"),
    )
    return jax.shard_map(
        body, mesh=mesh, in_specs=placed, out_specs=P(None, "gx", "gy"), check_vma=False
    )
```

```python
import jax
import jax.numpy as jnp
from jax import lax
from jax.experimental import pallas as pl
from jax.experimental.pallas import tpu as pltpu
from jax.sharding import PartitionSpec as P

ITERS = 2
V = 4
Z = 2
T = 128
ROWS = 16
GY = 16
GX = 8
CHUNKS = 64
META = 16
UNIT = ROWS * (1 + V) + 8
AXES = ("gx", "gy")
F32 = jnp.float32
BF16 = jnp.bfloat16
VMEM = pl.BlockSpec(memory_space=pltpu.VMEM)
HBM = pl.BlockSpec(memory_space=pltpu.HBM)
SMEM = pl.BlockSpec(memory_space=pltpu.SMEM)
PARAMS = pltpu.CompilerParams(vmem_limit_bytes=48 * 1024 * 1024)


def device_of(plane, chunk):
    core, block = chunk % 2, chunk // 2
    group, tile, part = block // 8, block % 8 // 4, block % 4
    inner = (tile == 0) == (group % 2 == 0)
    row = (1 if inner else 0, 2 if inner else 3)[plane]
    return (2 * group + core) * GY + 4 * row + (part if tile == 0 else 3 - part)


def both_ways(pairs):
    return [(a, b) for a, b in pairs] + [(b, a) for a, b in pairs]


SWAP = both_ways([(2 * x * GY + g, (2 * x + 1) * GY + g) for x in range(GX // 2) for g in range(GY)])
PAIR = both_ways(
    [
        (device_of(p, q), device_of(p, q + 1))
        for p in range(Z) for q in range(1, CHUNKS - 1, 2)
    ]
    + [(device_of(0, q), device_of(1, q)) for q in (0, CHUNKS - 1)]
)


def own_tile_inner():
    core, group = lax.axis_index("gx") % 2, lax.axis_index("gx") // 2
    return core, (core + group) % 2 == 0


def here():
    core, group = lax.axis_index("gx") % 2, lax.axis_index("gx") // 2
    row, col = lax.axis_index("gy") // 4, lax.axis_index("gy") % 4
    inner = jnp.where((row == 1) | (row == 2), 1, 0)
    first_tile = (inner + group) % 2 == 1
    block = 8 * group + jnp.where(first_tile, col, 7 - col)
    paired = jnp.where(core == 0, block > 0, block < CHUNKS // 2 - 1)
    return core, jnp.where(paired, 1.0, 0.0).astype(F32)


def part_of(col, core):
    return jnp.where(core == 0, col, 3 - col)


def split(x):
    hi = x.astype(BF16)
    return hi, (x - hi.astype(F32)).astype(BF16)


def pack_kernel(
    codes_hbm, shifts_hbm, est_hbm, views_hbm, keep_ref, send_ref, codes_ref, shifts_ref, est, views, sems
):
    core, _ = own_tile_inner()
    copies = [
        pltpu.make_async_copy(codes_hbm, codes_ref, sems.at[0]),
        pltpu.make_async_copy(shifts_hbm, shifts_ref, sems.at[1]),
        pltpu.make_async_copy(est_hbm, est, sems.at[2]),
        pltpu.make_async_copy(views_hbm, views, sems.at[3]),
    ]
    for copy in copies:
        copy.start()
    for copy in copies:
        copy.wait()
    lane = lax.broadcasted_iota(jnp.int32, (8, T), 1)
    for slot in range(8):
        plane, col = slot // 4, slot % 4
        for ref, sub in ((keep_ref, core), (send_ref, 1 - core)):
            chunk = 2 * part_of(col, core) + sub
            rows = pl.ds(pl.multiple_of(chunk * ROWS, ROWS), ROWS)
            meta = jnp.zeros((8, T), F32)
            for half in range(2):
                for v in range(V):
                    code = codes_ref[v, 2 * chunk + half].astype(F32)
                    shift = shifts_ref[v, 2 * chunk + half].astype(F32)
                    meta = jnp.where(lane == half * V + v, code, meta)
                    meta = jnp.where(lane == 8 + half * V + v, shift, meta)
            ref[slot, 0:ROWS, :] = est[plane, rows, :]
            for v in range(V):
                ref[slot, pl.ds(ROWS * (1 + v), ROWS), :] = views[v, plane, rows, :].astype(F32)
            ref[slot, pl.ds(ROWS * (1 + V), 8), :] = meta


def join_kernel(keep_ref, other_ref, out_hbm, sems):
    _, inner = own_tile_inner()
    copies = []
    for i, (ref, near) in enumerate(((keep_ref, inner), (other_ref, jnp.logical_not(inner)))):
        first, second = jnp.where(near, 4, 0), jnp.where(near, 8, 12)
        copies.append(
            pltpu.make_async_copy(ref.at[0:4], out_hbm.at[pl.ds(first, 4)], sems.at[2 * i])
        )
        copies.append(
            pltpu.make_async_copy(ref.at[4:8], out_hbm.at[pl.ds(second, 4)], sems.at[2 * i + 1])
        )
    for copy in copies:
        copy.start()
    for copy in copies:
        copy.wait()


def update_kernel(own_ref, mid_ref, paired_ref, swapped_ref, out_ref):
    _, has_pair = here()
    total = mid_ref[...] + paired_ref[...] * has_pair + swapped_ref[...]
    out_ref[...] = own_ref[0 : GY * ROWS, :] * (total * 0.25)


def unpack_kernel(home_ref, got_ref, out_ref):
    core, inner = own_tile_inner()
    for slot in range(8):
        plane, col = slot // 4, slot % 4
        start = 2 * part_of(col, core)
        source = jnp.where(inner, 4 + slot, 12 * plane + col)
        for sub, value in ((core, home_ref[source]), (1 - core, got_ref[slot])):
            rows = pl.ds(pl.multiple_of((start + sub) * ROWS, ROWS), ROWS)
            out_ref[plane, rows, :] = value


def taps_kernel(cols_ref, rows_ref, band_ref, row_ref, back_ref):
    for v in range(V):
        for d in range(2):
            base = jnp.broadcast_to(cols_ref[2 * v + d : 2 * v + d + 1, :], (2 * T, 2 * T))
            turned = pltpu.roll(base, 0, 1, stride=1, stride_axis=0)[:, :T]
            hi, lo = split(turned)
            band_ref[v, d, 0 : 2 * T, :] = hi
            band_ref[v, d, 2 * T : 4 * T, :] = lo
            band_ref[v, d, 4 * T : 6 * T, :] = hi
        base = jnp.broadcast_to(rows_ref[2 * v : 2 * v + 1, :], (ROWS, T))
        hi, lo = split(pltpu.roll(base, 0, 1, stride=1, stride_axis=0)[:, : 3 * ROWS])
        row_ref[v] = jnp.concatenate([hi, hi, lo], axis=1)
        base = jnp.broadcast_to(rows_ref[2 * v + 1 : 2 * v + 2, :], (3 * ROWS, T))
        hi, lo = split(pltpu.roll(base, 0, 1, stride=1, stride_axis=0)[:, :ROWS])
        back_ref[v] = jnp.concatenate([hi, hi, lo], axis=1)


def column_pass(pieces, band):
    lane = lax.broadcasted_iota(jnp.int32, (ROWS, T), 1)
    turned = [pltpu.roll(p, T // 2, 1) for p in pieces]
    zero = jnp.zeros((ROWS, T), F32)
    turned = [zero] + turned + [zero]
    moved = [
        jnp.where(lane < T // 2, turned[j], turned[j + 1]) for j in range(len(pieces) + 1)
    ]
    his, los = zip(*[split(m) for m in moved])
    left = len(pieces)

    def windows(parts):
        return jnp.concatenate(
            [jnp.concatenate([parts[c], parts[c + 1]], axis=1) for c in range(left)], axis=0
        )

    hi, lo = windows(his), windows(los)
    return jnp.dot(
        jnp.concatenate([hi, hi, lo], axis=1), band, preferred_element_type=F32
    )


def step_kernel(
    meta_ref, paired_ref, own_ref, swapped_ref, arrived_ref, band_ref, row_ref, back_ref,
    pair_ref, mid_ref, swap_ref, est2, slope2, view_u, total2,
):
    core, has_pair = here()
    first = core == 0
    bases = (jnp.where(first, 0, 2 * GY), GY, jnp.where(first, 2 * GY, 0))

    def own_block(ref, half):
        return ref[0 : GY * ROWS, :].reshape(GY, ROWS, T)[:, 8 * half : 8 * half + 8, :]

    lane = lax.broadcasted_iota(jnp.int32, (GY, 8, T), 2)
    inner = jnp.where(lane < T - 1, 1.0 / 16.0, 0.0).astype(F32)
    for half in range(2):
        paired = own_block(paired_ref, half) * has_pair
        swapped = own_block(swapped_ref, half)
        before, after = jnp.where(first, paired, swapped), jnp.where(first, swapped, paired)
        for src, x in enumerate((before, own_block(own_ref, half), after)):
            b = 2 * src + half
            d = (pltpu.roll(x, T - 1, 2) - x) * inner
            est2[b, 0:GY] = x
            est2[b, GY : 2 * GY] = x
            slope2[b, 0:GY] = d
            slope2[b, GY : 2 * GY] = d
    total2[...] = jnp.zeros(total2.shape, F32)
    inner8 = inner[0]
    for v in range(V):
        for src in range(3):
            parts = []
            for half in range(2):
                b = 2 * src + half
                shift = meta_ref[bases[src], 8 + half * V + v]
                x = est2[b, pl.ds(shift, GY)]
                d = slope2[b, pl.ds(shift, GY)]
                parts.append([
                    x[c] + meta_ref[bases[src] + c, half * V + v].astype(F32) * d[c]
                    for c in range(GY)
                ])
            for c in range(GY):
                hi, lo = split(jnp.concatenate([parts[0][c], parts[1][c]], axis=0))
                cols = slice(T * c, T * c + T)
                view_u[v, ROWS * src : ROWS * src + ROWS, cols] = hi
                view_u[v, ROWS * (3 + src) : ROWS * (4 + src), cols] = lo
                view_u[v, ROWS * (6 + src) : ROWS * (7 + src), cols] = hi
        smooth = jnp.dot(row_ref[v], view_u[v], preferred_element_type=F32)
        blurred = column_pass([smooth[:, T * c : T * c + T] for c in range(GY)], band_ref[v, 0])
        ratio = [
            arrived_ref[c, ROWS * (1 + v) : ROWS * (2 + v), :]
            / blurred[ROWS * c : ROWS * c + ROWS, :]
            for c in range(GY)
        ]
        again = column_pass(ratio, band_ref[v, 1])
        his, los = zip(*[split(again[ROWS * c : ROWS * c + ROWS, :]) for c in range(GY)])
        hi, lo = jnp.concatenate(his, axis=1), jnp.concatenate(los, axis=1)
        spread = jnp.dot(
            back_ref[v], jnp.concatenate([hi, lo, hi], axis=0), preferred_element_type=F32
        )
        for b in range(6):
            src, half = b // 2, b % 2
            shift = meta_ref[bases[src], 8 + half * V + v]
            parts = []
            for c in range(GY):
                r = spread[8 * b : 8 * b + 8, T * c : T * c + T]
                g = r * inner8
                g = pltpu.roll(g, 1, 1) - g
                parts.append(r + meta_ref[bases[src] + c, half * V + v].astype(F32) * g)
            total2[b, pl.ds(shift, GY)] += jnp.stack(parts)
    for half in range(2):
        low, mid, high = [
            total2[2 * src + half, 0:GY] + total2[2 * src + half, GY : 2 * GY] for src in range(3)
        ]
        pair, swap = jnp.where(first, low, high), jnp.where(first, high, low)
        for ref, y in ((pair_ref, pair), (mid_ref, mid), (swap_ref, swap)):
            for c in range(GY):
                ref[ROWS * c + 8 * half : ROWS * c + 8 * half + 8, :] = y[c]


def place(base, width, taps, at):
    left = at
    return jnp.pad(taps, ((0, 0), (left, width - left - taps.shape[1])))


def body(estimate, views, psf_rows, psf_cols, shifts, codes):
    _, inner = own_tile_inner()
    unit = jax.ShapeDtypeStruct((8, UNIT, T), F32)
    keep, send = pl.pallas_call(
        pack_kernel,
        out_shape=(unit, unit),
        in_specs=[HBM] * 4,
        out_specs=(VMEM, VMEM),
        scratch_shapes=[
            pltpu.SMEM((V, 2 * 8), jnp.int32),
            pltpu.SMEM((V, 2 * 8), jnp.int32),
            pltpu.VMEM((Z, T, T), F32),
            pltpu.VMEM((V, Z, T, T), BF16),
            pltpu.SemaphoreType.DMA((4,)),
        ],
        compiler_params=PARAMS,
        name="pack",
    )(codes[:, :, 0], shifts, estimate, views)
    other = lax.ppermute(send, AXES, SWAP)

    rows_n = psf_rows / jnp.sum(psf_rows, axis=1, keepdims=True)
    cols_n = psf_cols / jnp.sum(psf_cols, axis=1, keepdims=True)
    col_base = jnp.stack(
        [place(None, 2 * T, cols_n[:, ::-1], 177), place(None, 2 * T, cols_n, 177)], axis=1
    ).reshape(2 * V, 2 * T)
    row_base = jnp.stack(
        [place(None, T, rows_n, 1), place(None, T, rows_n[:, ::-1], T - 31)], axis=1
    ).reshape(2 * V, T)
    band, row_mat, back_mat = pl.pallas_call(
        taps_kernel,
        out_shape=(
            jax.ShapeDtypeStruct((V, 2, 6 * T, T), BF16),
            jax.ShapeDtypeStruct((V, ROWS, 9 * ROWS), BF16),
            jax.ShapeDtypeStruct((V, 3 * ROWS, 3 * ROWS), BF16),
        ),
        in_specs=[VMEM, VMEM],
        out_specs=(VMEM, VMEM, VMEM),
        compiler_params=PARAMS,
        name="taps",
    )(col_base, row_base)

    joined = pl.pallas_call(
        join_kernel,
        out_shape=jax.ShapeDtypeStruct((GY, UNIT, T), F32),
        in_specs=[VMEM, VMEM],
        out_specs=HBM,
        scratch_shapes=[pltpu.SemaphoreType.DMA((4,))],
        compiler_params=PARAMS,
        name="join",
    )(keep, other)
    arrived = lax.all_to_all(joined, "gy", split_axis=0, concat_axis=0, tiled=True)
    own = arrived[:, :ROWS, :].reshape(GY * ROWS, T)
    own_meta = arrived[:, ROWS * (1 + V), :]
    update = pl.pallas_call(
        update_kernel,
        out_shape=jax.ShapeDtypeStruct((GY * ROWS, T), F32),
        in_specs=[VMEM] * 4,
        out_specs=VMEM,
        compiler_params=PARAMS,
        name="update",
    )
    step = pl.pallas_call(
        step_kernel,
        out_shape=(jax.ShapeDtypeStruct((GY * ROWS, T), F32),) * 3,
        in_specs=[SMEM] + [VMEM] * 7,
        out_specs=(VMEM,) * 3,
        scratch_shapes=[
            pltpu.VMEM((6, 2 * GY, 8, T), F32),
            pltpu.VMEM((6, 2 * GY, 8, T), F32),
            pltpu.VMEM((V, 9 * ROWS, GY * T), BF16),
            pltpu.VMEM((6, 2 * GY, 8, T), F32),
        ],
        compiler_params=PARAMS,
        name="step",
    )
    for sweep in range(ITERS):
        out = jnp.concatenate([own, own_meta], axis=0) if sweep == 0 else own
        paired = lax.ppermute(out, AXES, PAIR)
        swapped = lax.ppermute(out, AXES, SWAP)
        if sweep == 0:
            meta = jnp.concatenate(
                [paired[GY * ROWS :, :META], own_meta[:, :META], swapped[GY * ROWS :, :META]], axis=0
            ).astype(jnp.int32)
        pair, mid, swap = step(meta, paired, own, swapped, arrived, band, row_mat, back_mat)
        own = update(own, mid, lax.ppermute(pair, AXES, PAIR), lax.ppermute(swap, AXES, SWAP))
    home = lax.all_to_all(
        own.reshape(GY, ROWS, T), "gy", split_axis=0, concat_axis=0, tiled=True
    )
    theirs = jnp.where(inner, jnp.concatenate([home[0:4], home[12:16]], axis=0), home[4:12])
    got = lax.ppermute(theirs, AXES, SWAP)
    return pl.pallas_call(
        unpack_kernel,
        out_shape=jax.ShapeDtypeStruct((Z, T, T), F32),
        in_specs=[VMEM, VMEM],
        out_specs=VMEM,
        compiler_params=PARAMS,
        name="unpack",
    )(home, got)


def solution(mesh):
    placed = (
        P(None, "gx", "gy"),
        P(None, None, "gx", "gy"),
        P(),
        P(),
        P(None, "gx"),
        P(None, "gx", "gy"),
    )
    return jax.shard_map(
        body, mesh=mesh, in_specs=placed, out_specs=P(None, "gx", "gy"), check_vma=False
    )
```

```python
import jax
import jax.numpy as jnp
from jax import lax
from jax.experimental import pallas as pl
from jax.experimental.pallas import tpu as pltpu
from jax.sharding import PartitionSpec as P

ITERS = 2
V = 4
Z = 2
T = 128
ROWS = 16
GY = 16
GX = 8
CHUNKS = 64
META = 16
UNIT = ROWS * (1 + V) + 8
AXES = ("gx", "gy")
F32 = jnp.float32
BF16 = jnp.bfloat16
VMEM = pl.BlockSpec(memory_space=pltpu.VMEM)
HBM = pl.BlockSpec(memory_space=pltpu.HBM)
SMEM = pl.BlockSpec(memory_space=pltpu.SMEM)
PARAMS = pltpu.CompilerParams(vmem_limit_bytes=48 * 1024 * 1024)


def device_of(plane, chunk):
    core, block = chunk % 2, chunk // 2
    group, tile, part = block // 8, block % 8 // 4, block % 4
    inner = (tile == 0) == (group % 2 == 0)
    row = (1 if inner else 0, 2 if inner else 3)[plane]
    return (2 * group + core) * GY + 4 * row + (part if tile == 0 else 3 - part)


def both_ways(pairs):
    return [(a, b) for a, b in pairs] + [(b, a) for a, b in pairs]


SWAP = both_ways([(2 * x * GY + g, (2 * x + 1) * GY + g) for x in range(GX // 2) for g in range(GY)])
PAIR = both_ways(
    [
        (device_of(p, q), device_of(p, q + 1))
        for p in range(Z) for q in range(1, CHUNKS - 1, 2)
    ]
    + [(device_of(0, q), device_of(1, q)) for q in (0, CHUNKS - 1)]
)


def own_tile_inner():
    core, group = lax.axis_index("gx") % 2, lax.axis_index("gx") // 2
    return core, (core + group) % 2 == 0


def here():
    core, group = lax.axis_index("gx") % 2, lax.axis_index("gx") // 2
    row, col = lax.axis_index("gy") // 4, lax.axis_index("gy") % 4
    inner = jnp.where((row == 1) | (row == 2), 1, 0)
    first_tile = (inner + group) % 2 == 1
    block = 8 * group + jnp.where(first_tile, col, 7 - col)
    paired = jnp.where(core == 0, block > 0, block < CHUNKS // 2 - 1)
    return core, jnp.where(paired, 1.0, 0.0).astype(F32)


def part_of(col, core):
    return jnp.where(core == 0, col, 3 - col)


def split(x):
    hi = x.astype(BF16)
    return hi, (x - hi.astype(F32)).astype(BF16)


def pack_kernel(
    codes_hbm, shifts_hbm, est_hbm, views_hbm, keep_ref, send_ref, codes_ref, shifts_ref, est, views, sems
):
    core, _ = own_tile_inner()
    copies = [
        pltpu.make_async_copy(codes_hbm, codes_ref, sems.at[0]),
        pltpu.make_async_copy(shifts_hbm, shifts_ref, sems.at[1]),
        pltpu.make_async_copy(est_hbm, est, sems.at[2]),
        pltpu.make_async_copy(views_hbm, views, sems.at[3]),
    ]
    for copy in copies:
        copy.start()
    for copy in copies:
        copy.wait()
    lane = lax.broadcasted_iota(jnp.int32, (8, T), 1)
    for slot in range(8):
        plane, col = slot // 4, slot % 4
        for ref, sub in ((keep_ref, core), (send_ref, 1 - core)):
            chunk = 2 * part_of(col, core) + sub
            rows = pl.ds(pl.multiple_of(chunk * ROWS, ROWS), ROWS)
            meta = jnp.zeros((8, T), F32)
            for half in range(2):
                for v in range(V):
                    code = codes_ref[v, 2 * chunk + half].astype(F32)
                    shift = shifts_ref[v, 2 * chunk + half].astype(F32)
                    meta = jnp.where(lane == half * V + v, code, meta)
                    meta = jnp.where(lane == 8 + half * V + v, shift, meta)
            ref[slot, 0:ROWS, :] = est[plane, rows, :]
            for v in range(V):
                ref[slot, pl.ds(ROWS * (1 + v), ROWS), :] = views[v, plane, rows, :].astype(F32)
            ref[slot, pl.ds(ROWS * (1 + V), 8), :] = meta


def join_kernel(keep_ref, other_ref, out_hbm, sems):
    _, inner = own_tile_inner()
    copies = []
    for i, (ref, near) in enumerate(((keep_ref, inner), (other_ref, jnp.logical_not(inner)))):
        first, second = jnp.where(near, 4, 0), jnp.where(near, 8, 12)
        copies.append(
            pltpu.make_async_copy(ref.at[0:4], out_hbm.at[pl.ds(first, 4)], sems.at[2 * i])
        )
        copies.append(
            pltpu.make_async_copy(ref.at[4:8], out_hbm.at[pl.ds(second, 4)], sems.at[2 * i + 1])
        )
    for copy in copies:
        copy.start()
    for copy in copies:
        copy.wait()


def update_kernel(own_ref, mid_ref, paired_ref, swapped_ref, out_ref):
    _, has_pair = here()
    total = mid_ref[...] + paired_ref[...] * has_pair + swapped_ref[...]
    out_ref[...] = own_ref[0 : GY * ROWS, :] * (total * 0.25)


def unpack_kernel(home_ref, got_ref, out_ref):
    core, inner = own_tile_inner()
    for slot in range(8):
        plane, col = slot // 4, slot % 4
        start = 2 * part_of(col, core)
        source = jnp.where(inner, 4 + slot, 12 * plane + col)
        for sub, value in ((core, home_ref[source]), (1 - core, got_ref[slot])):
            rows = pl.ds(pl.multiple_of((start + sub) * ROWS, ROWS), ROWS)
            out_ref[plane, rows, :] = value


def taps_kernel(cols_ref, rows_ref, band_ref, row_ref, back_ref):
    def turned(base, count, width):
        rows = jnp.broadcast_to(base, (count, base.shape[1]))
        return split(pltpu.roll(rows, 0, 1, stride=1, stride_axis=0)[:, :width])

    for v in range(V):
        for d in range(2):
            hi, lo = turned(cols_ref[2 * v + d : 2 * v + d + 1, :], 2 * T, T)
            band_ref[v, d, 0 : 2 * T, 0:T] = hi
            band_ref[v, d, 0 : 2 * T, T : 2 * T] = lo
            band_ref[v, d, 2 * T : 4 * T, 0:T] = hi
            band_ref[v, d, 2 * T : 4 * T, T : 2 * T] = jnp.zeros_like(lo)
        hi, lo = turned(rows_ref[2 * v : 2 * v + 1, :], ROWS, 3 * ROWS)
        row_ref[v, 0:ROWS] = jnp.concatenate([hi, hi], axis=1)
        row_ref[v, ROWS : 2 * ROWS] = jnp.concatenate([lo, jnp.zeros_like(lo)], axis=1)
        hi, lo = turned(rows_ref[2 * v + 1 : 2 * v + 2, :], 3 * ROWS, ROWS)
        back_ref[v] = jnp.concatenate([hi, hi, lo], axis=1)


def column_pass(pieces, band):
    lane = lax.broadcasted_iota(jnp.int32, (ROWS, T), 1)
    turned = [pltpu.roll(p, T // 2, 1) for p in pieces]
    zero = jnp.zeros((ROWS, T), F32)
    turned = [zero] + turned + [zero]
    moved = [
        jnp.where(lane < T // 2, turned[j], turned[j + 1]) for j in range(len(pieces) + 1)
    ]
    his, los = zip(*[split(m) for m in moved])
    windows = [
        jnp.concatenate([his[c], his[c + 1], los[c], los[c + 1]], axis=1)
        for c in range(len(pieces))
    ]
    both = jnp.dot(jnp.concatenate(windows, axis=0), band, preferred_element_type=F32)
    return both[:, :T] + both[:, T:]


def column_tiles(ref, v):
    return [ref[v, :, T * c : T * c + T] for c in range(GY)]


def step_kernel(
    meta_ref, paired_ref, own_ref, swapped_ref, arrived_ref, band_ref, row_ref, back_ref,
    pair_ref, mid_ref, swap_ref, est2, slope2, view_u, total2, smooth, ratio, again,
):
    core, has_pair = here()
    first = core == 0
    bases = (jnp.where(first, 0, 2 * GY), GY, jnp.where(first, 2 * GY, 0))

    def own_block(ref, half):
        return ref[0 : GY * ROWS, :].reshape(GY, ROWS, T)[:, 8 * half : 8 * half + 8, :]

    def code_of(v, src, half, c):
        return meta_ref[bases[src] + c, half * V + v].astype(F32)

    def shift_of(v, src, half):
        return meta_ref[bases[src], 8 + half * V + v]

    lane = lax.broadcasted_iota(jnp.int32, (GY, 8, T), 2)
    inner = jnp.where(lane < T - 1, 1.0 / 16.0, 0.0).astype(F32)
    inner8 = inner[0]
    for half in range(2):
        paired = own_block(paired_ref, half) * has_pair
        swapped = own_block(swapped_ref, half)
        before, after = jnp.where(first, paired, swapped), jnp.where(first, swapped, paired)
        for src, x in enumerate((before, own_block(own_ref, half), after)):
            b = 2 * src + half
            d = (pltpu.roll(x, T - 1, 2) - x) * inner
            est2[b, 0:GY] = x
            est2[b, GY : 2 * GY] = x
            slope2[b, 0:GY] = d
            slope2[b, GY : 2 * GY] = d
    total2[...] = jnp.zeros(total2.shape, F32)

    def gather(v):
        for src in range(3):
            parts = []
            for half in range(2):
                b = 2 * src + half
                shift = shift_of(v, src, half)
                x = est2[b, pl.ds(shift, GY)]
                d = slope2[b, pl.ds(shift, GY)]
                parts.append([x[c] + code_of(v, src, half, c) * d[c] for c in range(GY)])
            for c in range(GY):
                hi, lo = split(jnp.concatenate([parts[0][c], parts[1][c]], axis=0))
                cols = slice(T * c, T * c + T)
                view_u[v, ROWS * src : ROWS * src + ROWS, cols] = hi
                view_u[v, ROWS * (3 + src) : ROWS * (4 + src), cols] = lo

    def rows_in(v):
        both = jnp.dot(row_ref[v], view_u[v], preferred_element_type=F32)
        smooth[v] = both[:ROWS] + both[ROWS:]

    def cols_in(v):
        blurred = column_pass(column_tiles(smooth, v), band_ref[v, 0])
        for c in range(GY):
            ratio[v, :, T * c : T * c + T] = (
                arrived_ref[c, ROWS * (1 + v) : ROWS * (2 + v), :]
                / blurred[ROWS * c : ROWS * c + ROWS, :]
            )

    def cols_back(v):
        again[v] = column_pass(column_tiles(ratio, v), band_ref[v, 1])

    def rows_back(v):
        his, los = zip(*[split(again[v, ROWS * c : ROWS * c + ROWS, :]) for c in range(GY)])
        hi, lo = jnp.concatenate(his, axis=1), jnp.concatenate(los, axis=1)
        spread = jnp.dot(
            back_ref[v], jnp.concatenate([hi, lo, hi], axis=0), preferred_element_type=F32
        )
        for b in range(6):
            src, half = b // 2, b % 2
            parts = []
            for c in range(GY):
                r = spread[8 * b : 8 * b + 8, T * c : T * c + T]
                g = r * inner8
                g = pltpu.roll(g, 1, 1) - g
                parts.append(r + code_of(v, src, half, c) * g)
            total2[b, pl.ds(shift_of(v, src, half), GY)] += jnp.stack(parts)

    stages = (gather, rows_in, cols_in, cols_back, rows_back)
    for turn in range(V + len(stages) - 1):
        for i, stage in enumerate(stages):
            if 0 <= turn - i < V:
                stage(turn - i)
    for half in range(2):
        low, mid, high = [
            total2[2 * src + half, 0:GY] + total2[2 * src + half, GY : 2 * GY] for src in range(3)
        ]
        pair, swap = jnp.where(first, low, high), jnp.where(first, high, low)
        for ref, y in ((pair_ref, pair), (mid_ref, mid), (swap_ref, swap)):
            for c in range(GY):
                ref[ROWS * c + 8 * half : ROWS * c + 8 * half + 8, :] = y[c]


def place(taps, at, width):
    return jnp.pad(taps, ((0, 0), (at, width - at - taps.shape[1])))


def body(estimate, views, psf_rows, psf_cols, shifts, codes):
    _, inner = own_tile_inner()
    unit = jax.ShapeDtypeStruct((8, UNIT, T), F32)
    keep, send = pl.pallas_call(
        pack_kernel,
        out_shape=(unit, unit),
        in_specs=[HBM] * 4,
        out_specs=(VMEM, VMEM),
        scratch_shapes=[
            pltpu.SMEM((V, 2 * 8), jnp.int32),
            pltpu.SMEM((V, 2 * 8), jnp.int32),
            pltpu.VMEM((Z, T, T), F32),
            pltpu.VMEM((V, Z, T, T), BF16),
            pltpu.SemaphoreType.DMA((4,)),
        ],
        compiler_params=PARAMS,
        name="pack",
    )(
        *[
            pltpu.with_memory_space_constraint(a, pltpu.HBM)
            for a in (codes[:, :, 0], shifts, estimate, views)
        ]
    )
    other = lax.ppermute(send, AXES, SWAP)

    rows_n = psf_rows / jnp.sum(psf_rows, axis=1, keepdims=True)
    cols_n = psf_cols / jnp.sum(psf_cols, axis=1, keepdims=True)
    col_base = jnp.stack(
        [place(cols_n[:, ::-1], 177, 2 * T), place(cols_n, 177, 2 * T)], axis=1
    ).reshape(2 * V, 2 * T)
    row_base = jnp.stack(
        [place(rows_n, 1, T), place(rows_n[:, ::-1], T - 31, T)], axis=1
    ).reshape(2 * V, T)
    band, row_mat, back_mat = pl.pallas_call(
        taps_kernel,
        out_shape=(
            jax.ShapeDtypeStruct((V, 2, 4 * T, 2 * T), BF16),
            jax.ShapeDtypeStruct((V, 2 * ROWS, 6 * ROWS), BF16),
            jax.ShapeDtypeStruct((V, 3 * ROWS, 3 * ROWS), BF16),
        ),
        in_specs=[VMEM, VMEM],
        out_specs=(VMEM, VMEM, VMEM),
        compiler_params=PARAMS,
        name="taps",
    )(col_base, row_base)

    joined = pl.pallas_call(
        join_kernel,
        out_shape=jax.ShapeDtypeStruct((GY, UNIT, T), F32),
        in_specs=[VMEM, VMEM],
        out_specs=HBM,
        scratch_shapes=[pltpu.SemaphoreType.DMA((4,))],
        compiler_params=PARAMS,
        name="join",
    )(keep, other)
    arrived = lax.all_to_all(joined, "gy", split_axis=0, concat_axis=0, tiled=True)
    own = arrived[:, :ROWS, :].reshape(GY * ROWS, T)
    own_meta = arrived[:, ROWS * (1 + V), :]
    update = pl.pallas_call(
        update_kernel,
        out_shape=jax.ShapeDtypeStruct((GY * ROWS, T), F32),
        in_specs=[VMEM] * 4,
        out_specs=VMEM,
        compiler_params=PARAMS,
        name="update",
    )
    step = pl.pallas_call(
        step_kernel,
        out_shape=(jax.ShapeDtypeStruct((GY * ROWS, T), F32),) * 3,
        in_specs=[SMEM] + [VMEM] * 7,
        out_specs=(VMEM,) * 3,
        scratch_shapes=[
            pltpu.VMEM((6, 2 * GY, 8, T), F32),
            pltpu.VMEM((6, 2 * GY, 8, T), F32),
            pltpu.VMEM((V, 6 * ROWS, GY * T), BF16),
            pltpu.VMEM((6, 2 * GY, 8, T), F32),
            pltpu.VMEM((V, ROWS, GY * T), F32),
            pltpu.VMEM((V, ROWS, GY * T), F32),
            pltpu.VMEM((V, GY * ROWS, T), F32),
        ],
        compiler_params=PARAMS,
        name="step",
    )
    for sweep in range(ITERS):
        out = jnp.concatenate([own, own_meta], axis=0) if sweep == 0 else own
        paired = lax.ppermute(out, AXES, PAIR)
        swapped = lax.ppermute(out, AXES, SWAP)
        if sweep == 0:
            meta = jnp.concatenate(
                [paired[GY * ROWS :, :META], own_meta[:, :META], swapped[GY * ROWS :, :META]], axis=0
            ).astype(jnp.int32)
        pair, mid, swap = step(meta, paired, own, swapped, arrived, band, row_mat, back_mat)
        own = update(own, mid, lax.ppermute(pair, AXES, PAIR), lax.ppermute(swap, AXES, SWAP))
    home = lax.all_to_all(
        own.reshape(GY, ROWS, T), "gy", split_axis=0, concat_axis=0, tiled=True
    )
    theirs = jnp.where(inner, jnp.concatenate([home[0:4], home[12:16]], axis=0), home[4:12])
    got = lax.ppermute(theirs, AXES, SWAP)
    return pl.pallas_call(
        unpack_kernel,
        out_shape=jax.ShapeDtypeStruct((Z, T, T), F32),
        in_specs=[VMEM, VMEM],
        out_specs=VMEM,
        compiler_params=PARAMS,
        name="unpack",
    )(home, got)


def solution(mesh):
    placed = (
        P(None, "gx", "gy"),
        P(None, None, "gx", "gy"),
        P(),
        P(),
        P(None, "gx"),
        P(None, "gx", "gy"),
    )
    return jax.shard_map(
        body, mesh=mesh, in_specs=placed, out_specs=P(None, "gx", "gy"), check_vma=False
    )
```

```python
import jax
import jax.numpy as jnp
from jax import lax
from jax.experimental import pallas as pl
from jax.experimental.pallas import tpu as pltpu
from jax.sharding import PartitionSpec as P

ITERS = 2
V = 4
Z = 2
T = 128
ROWS = 16
GY = 16
GX = 8
CHUNKS = 64
META = 16
UNIT = ROWS * (1 + V) + 8
AXES = ("gx", "gy")
F32 = jnp.float32
BF16 = jnp.bfloat16
VMEM = pl.BlockSpec(memory_space=pltpu.VMEM)
COST = pl.CostEstimate(flops=1_000_000_000, bytes_accessed=4_000_000, transcendentals=0)
HBM = pl.BlockSpec(memory_space=pltpu.HBM)
SMEM = pl.BlockSpec(memory_space=pltpu.SMEM)
PARAMS = pltpu.CompilerParams(vmem_limit_bytes=48 * 1024 * 1024)


def device_of(plane, chunk):
    core, block = chunk % 2, chunk // 2
    group, tile, part = block // 8, block % 8 // 4, block % 4
    inner = (tile == 0) == (group % 2 == 0)
    row = (1 if inner else 0, 2 if inner else 3)[plane]
    return (2 * group + core) * GY + 4 * row + (part if tile == 0 else 3 - part)


def both_ways(pairs):
    return [(a, b) for a, b in pairs] + [(b, a) for a, b in pairs]


SWAP = both_ways([(2 * x * GY + g, (2 * x + 1) * GY + g) for x in range(GX // 2) for g in range(GY)])
PAIR = both_ways(
    [
        (device_of(p, q), device_of(p, q + 1))
        for p in range(Z) for q in range(1, CHUNKS - 1, 2)
    ]
    + [(device_of(0, q), device_of(1, q)) for q in (0, CHUNKS - 1)]
)


def own_tile_inner():
    core, group = lax.axis_index("gx") % 2, lax.axis_index("gx") // 2
    return core, (core + group) % 2 == 0


def here():
    core, group = lax.axis_index("gx") % 2, lax.axis_index("gx") // 2
    row, col = lax.axis_index("gy") // 4, lax.axis_index("gy") % 4
    inner = jnp.where((row == 1) | (row == 2), 1, 0)
    first_tile = (inner + group) % 2 == 1
    block = 8 * group + jnp.where(first_tile, col, 7 - col)
    paired = jnp.where(core == 0, block > 0, block < CHUNKS // 2 - 1)
    return core, jnp.where(paired, 1.0, 0.0).astype(F32)


def part_of(col, core):
    return jnp.where(core == 0, col, 3 - col)


def split(x):
    hi = x.astype(BF16)
    return hi, (x - hi.astype(F32)).astype(BF16)


def pack_kernel(
    codes_hbm, shifts_hbm, est_hbm, views_hbm, keep_ref, send_ref, codes_ref, shifts_ref, est, views, sems
):
    core, _ = own_tile_inner()
    copies = [
        pltpu.make_async_copy(codes_hbm, codes_ref, sems.at[0]),
        pltpu.make_async_copy(shifts_hbm, shifts_ref, sems.at[1]),
        pltpu.make_async_copy(est_hbm, est, sems.at[2]),
        pltpu.make_async_copy(views_hbm, views, sems.at[3]),
    ]
    for copy in copies:
        copy.start()
    for copy in copies:
        copy.wait()
    lane = lax.broadcasted_iota(jnp.int32, (8, T), 1)
    for slot in range(8):
        plane, col = slot // 4, slot % 4
        for ref, sub in ((keep_ref, core), (send_ref, 1 - core)):
            chunk = 2 * part_of(col, core) + sub
            rows = pl.ds(pl.multiple_of(chunk * ROWS, ROWS), ROWS)
            meta = jnp.zeros((8, T), F32)
            for half in range(2):
                for v in range(V):
                    code = codes_ref[v, 2 * chunk + half].astype(F32)
                    shift = shifts_ref[v, 2 * chunk + half].astype(F32)
                    meta = jnp.where(lane == half * V + v, code, meta)
                    meta = jnp.where(lane == 8 + half * V + v, shift, meta)
            ref[slot, 0:ROWS, :] = est[plane, rows, :]
            for v in range(V):
                ref[slot, pl.ds(ROWS * (1 + v), ROWS), :] = views[v, plane, rows, :].astype(F32)
            ref[slot, pl.ds(ROWS * (1 + V), 8), :] = meta


def join_kernel(keep_ref, other_ref, out_hbm, sems):
    _, inner = own_tile_inner()
    copies = []
    for i, (ref, near) in enumerate(((keep_ref, inner), (other_ref, jnp.logical_not(inner)))):
        first, second = jnp.where(near, 4, 0), jnp.where(near, 8, 12)
        copies.append(
            pltpu.make_async_copy(ref.at[0:4], out_hbm.at[pl.ds(first, 4)], sems.at[2 * i])
        )
        copies.append(
            pltpu.make_async_copy(ref.at[4:8], out_hbm.at[pl.ds(second, 4)], sems.at[2 * i + 1])
        )
    for copy in copies:
        copy.start()
    for copy in copies:
        copy.wait()


def inside_kernel(paired_ref, out_ref):
    _, has_pair = here()
    out_ref[...] = paired_ref[...] * has_pair


def update_kernel(own_ref, mid_ref, paired_ref, swapped_ref, out_ref):
    total = mid_ref[...] + paired_ref[...] + swapped_ref[...]
    out_ref[...] = own_ref[0 : GY * ROWS, :] * (total * 0.25)


def unpack_kernel(home_ref, got_ref, out_ref):
    core, inner = own_tile_inner()
    for slot in range(8):
        plane, col = slot // 4, slot % 4
        start = 2 * part_of(col, core)
        source = jnp.where(inner, 4 + slot, 12 * plane + col)
        for sub, value in ((core, home_ref[source]), (1 - core, got_ref[slot])):
            rows = pl.ds(pl.multiple_of((start + sub) * ROWS, ROWS), ROWS)
            out_ref[plane, rows, :] = value


def put_split(ref, v, pieces, stacked=False):
    axis = 0 if stacked else 1
    hi = jnp.concatenate([p[0] for p in pieces], axis=axis)
    lo = jnp.concatenate([p[1] for p in pieces], axis=axis)
    ref[v] = jnp.concatenate(
        [
            jnp.concatenate([hi, hi], axis=1),
            jnp.concatenate([lo, jnp.zeros_like(lo)], axis=1),
        ],
        axis=0,
    )


def taps_kernel(
    cols_ref, rows_ref, band_ref, pair_in_ref, near_in_ref, pair_back_ref, near_back_ref
):
    core, _ = own_tile_inner()

    def either(a, b):
        return tuple(jnp.where(core == 0, x, y) for x, y in zip(a, b))

    def turned(base, count, width):
        rows = jnp.broadcast_to(base, (count, base.shape[1]))
        return split(pltpu.roll(rows, 0, 1, stride=1, stride_axis=0)[:, :width])

    for v in range(V):
        for d in range(2):
            hi, lo = turned(cols_ref[2 * v + d : 2 * v + d + 1, :], 2 * T, T)
            band_ref[v, d, 0 : 2 * T, 0:T] = hi
            band_ref[v, d, 0 : 2 * T, T : 2 * T] = lo
            band_ref[v, d, 2 * T : 4 * T, 0:T] = hi
            band_ref[v, d, 2 * T : 4 * T, T : 2 * T] = jnp.zeros_like(lo)
        before, own, after = [
            turned(pltpu.roll(jnp.broadcast_to(rows_ref[2 * v : 2 * v + 1, :], (8, T)), (T - ROWS * i) % T, 1)[0:1], ROWS, ROWS) for i in range(3)
        ]
        put_split(pair_in_ref, v, [either(before, after)])
        put_split(near_in_ref, v, [own, either(after, before)])
        before, own, after = [
            turned(pltpu.roll(jnp.broadcast_to(rows_ref[2 * v + 1 : 2 * v + 2, :], (8, T)), ROWS * i, 1)[0:1], ROWS, ROWS) for i in range(3)
        ]
        put_split(pair_back_ref, v, [either(before, after)], stacked=True)
        put_split(near_back_ref, v, [own, either(after, before)], stacked=True)


def column_pass(pieces, band):
    lane = lax.broadcasted_iota(jnp.int32, (ROWS, T), 1)
    turned = [pltpu.roll(p, T // 2, 1) for p in pieces]
    zero = jnp.zeros((ROWS, T), F32)
    turned = [zero] + turned + [zero]
    moved = [
        jnp.where(lane < T // 2, turned[j], turned[j + 1]) for j in range(len(pieces) + 1)
    ]
    his, los = zip(*[split(m) for m in moved])
    windows = [
        jnp.concatenate([his[c], his[c + 1], los[c], los[c + 1]], axis=1)
        for c in range(len(pieces))
    ]
    both = jnp.dot(jnp.concatenate(windows, axis=0), band, preferred_element_type=F32)
    return both[:, :T] + both[:, T:]


def column_tiles(ref, v):
    return [ref[v, :, T * c : T * c + T] for c in range(GY)]


def own_block(ref, half):
    return ref[0 : GY * ROWS, :].reshape(GY, ROWS, T)[:, 8 * half : 8 * half + 8, :]


def inner_lanes():
    lane = lax.broadcasted_iota(jnp.int32, (8, T), 1)
    return jnp.where(lane < T - 1, 1.0 / 16.0, 0.0).astype(F32)


def put_twice(b, x, est2, slope2):
    d = (pltpu.roll(x, T - 1, 2) - x) * inner_lanes()
    for copy in range(2):
        est2[b, GY * copy : GY * copy + GY] = x
        slope2[b, GY * copy : GY * copy + GY] = d


def code_of(meta_ref, v, b, c):
    return meta_ref[GY * (b // 2) + c, b % 2 * V + v].astype(F32)


def shift_of(meta_ref, v, b):
    return meta_ref[GY * (b // 2), 8 + b % 2 * V + v]


def gather(v, meta_ref, est2, slope2, view_u):
    count = est2.shape[0] // 2
    for src in range(count):
        parts = []
        for b in (2 * src, 2 * src + 1):
            shift = shift_of(meta_ref, v, b)
            x = est2[b, pl.ds(shift, GY)]
            d = slope2[b, pl.ds(shift, GY)]
            parts.append([x[c] + code_of(meta_ref, v, b, c) * d[c] for c in range(GY)])
        for c in range(GY):
            hi, lo = split(jnp.concatenate([parts[0][c], parts[1][c]], axis=0))
            cols = slice(T * c, T * c + T)
            view_u[v, ROWS * src : ROWS * src + ROWS, cols] = hi
            view_u[v, ROWS * (count + src) : ROWS * (count + src + 1), cols] = lo


def product(weights, values):
    both = jnp.dot(weights, values, preferred_element_type=F32)
    return both[: both.shape[0] // 2] + both[both.shape[0] // 2 :]


def rows_back(v, meta_ref, back_ref, again, total2):
    his, los = zip(*[split(again[v, ROWS * c : ROWS * c + ROWS, :]) for c in range(GY)])
    values = jnp.concatenate(
        [jnp.concatenate(his, axis=1), jnp.concatenate(los, axis=1)], axis=0
    )
    spread = product(back_ref[v], values)
    inner = inner_lanes()
    for b in range(total2.shape[0]):
        parts = []
        for c in range(GY):
            r = spread[8 * b : 8 * b + 8, T * c : T * c + T]
            g = r * inner
            g = pltpu.roll(g, 1, 1) - g
            parts.append(r + code_of(meta_ref, v, b, c) * g)
        total2[b, pl.ds(shift_of(meta_ref, v, b), GY)] += jnp.stack(parts)


def put_joined(ref, src, total2):
    for half in range(2):
        b = 2 * src + half
        y = total2[b, 0:GY] + total2[b, GY : 2 * GY]
        for c in range(GY):
            ref[ROWS * c + 8 * half : ROWS * c + 8 * half + 8, :] = y[c]


def in_turn(stages):
    for turn in range(V + len(stages) - 1):
        for i, stage in enumerate(stages):
            if 0 <= turn - i < V:
                stage(turn - i)


def front_kernel(meta_ref, own_ref, swapped_ref, near_in_ref, smooth_ref, est2, slope2, view_u):
    for src, ref in enumerate((own_ref, swapped_ref)):
        for half in range(2):
            put_twice(2 * src + half, own_block(ref, half), est2, slope2)

    def rows_in(v):
        smooth_ref[v] = product(near_in_ref[v], view_u[v])

    in_turn((lambda v: gather(v, meta_ref, est2, slope2, view_u), rows_in))


def core_kernel(
    meta_ref, paired_ref, near_ref, arrived_ref, band_ref, pair_in_ref, pair_back_ref,
    pair_ref, again_ref, est2, slope2, view_u, total2, smooth, ratio,
):
    _, has_pair = here()
    for half in range(2):
        put_twice(half, own_block(paired_ref, half) * has_pair, est2, slope2)
    total2[...] = jnp.zeros(total2.shape, F32)

    def rows_in(v):
        smooth[v] = near_ref[v] + product(pair_in_ref[v], view_u[v])

    def cols_in(v):
        blurred = column_pass(column_tiles(smooth, v), band_ref[v, 0])
        for c in range(GY):
            ratio[v, :, T * c : T * c + T] = (
                arrived_ref[c, ROWS * (1 + v) : ROWS * (2 + v), :]
                / blurred[ROWS * c : ROWS * c + ROWS, :]
            )

    def cols_back(v):
        again_ref[v] = column_pass(column_tiles(ratio, v), band_ref[v, 1])

    in_turn((
        lambda v: gather(v, meta_ref, est2, slope2, view_u),
        rows_in,
        cols_in,
        cols_back,
        lambda v: rows_back(v, meta_ref, pair_back_ref, again_ref, total2),
    ))
    put_joined(pair_ref, 0, total2)


def tail_kernel(meta_ref, again_ref, near_back_ref, mid_ref, swap_ref, total2):
    total2[...] = jnp.zeros(total2.shape, F32)
    for v in range(V):
        rows_back(v, meta_ref, near_back_ref, again_ref, total2)
    put_joined(mid_ref, 0, total2)
    put_joined(swap_ref, 1, total2)


def place(taps, at, width):
    return jnp.pad(taps, ((0, 0), (at, width - at - taps.shape[1])))


def body(estimate, views, psf_rows, psf_cols, shifts, codes):
    _, inner = own_tile_inner()
    unit = jax.ShapeDtypeStruct((8, UNIT, T), F32)
    keep, send = pl.pallas_call(
        pack_kernel,
        out_shape=(unit, unit),
        in_specs=[HBM] * 4,
        out_specs=(VMEM, VMEM),
        scratch_shapes=[
            pltpu.SMEM((V, 2 * 8), jnp.int32),
            pltpu.SMEM((V, 2 * 8), jnp.int32),
            pltpu.VMEM((Z, T, T), F32),
            pltpu.VMEM((V, Z, T, T), BF16),
            pltpu.SemaphoreType.DMA((4,)),
        ],
        compiler_params=PARAMS,
        name="pack",
    )(
        *[
            pltpu.with_memory_space_constraint(a, pltpu.HBM)
            for a in (codes[:, :, 0], shifts, estimate, views)
        ]
    )
    other = lax.ppermute(send, AXES, SWAP)

    rows_n = psf_rows / jnp.sum(psf_rows, axis=1, keepdims=True)
    cols_n = psf_cols / jnp.sum(psf_cols, axis=1, keepdims=True)
    col_base = jnp.stack(
        [place(cols_n[:, ::-1], 177, 2 * T), place(cols_n, 177, 2 * T)], axis=1
    ).reshape(2 * V, 2 * T)
    row_base = jnp.stack(
        [place(rows_n, 1, T), place(rows_n[:, ::-1], T - 31, T)], axis=1
    ).reshape(2 * V, T)
    band, pair_in, near_in, pair_back, near_back = pl.pallas_call(
        taps_kernel,
        out_shape=(
            jax.ShapeDtypeStruct((V, 2, 4 * T, 2 * T), BF16),
            jax.ShapeDtypeStruct((V, 2 * ROWS, 2 * ROWS), BF16),
            jax.ShapeDtypeStruct((V, 2 * ROWS, 4 * ROWS), BF16),
            jax.ShapeDtypeStruct((V, 2 * ROWS, 2 * ROWS), BF16),
            jax.ShapeDtypeStruct((V, 4 * ROWS, 2 * ROWS), BF16),
        ),
        in_specs=[VMEM, VMEM],
        out_specs=(VMEM,) * 5,
        compiler_params=PARAMS,
        cost_estimate=COST,
        name="taps",
    )(col_base, row_base)

    joined = pl.pallas_call(
        join_kernel,
        out_shape=jax.ShapeDtypeStruct((GY, UNIT, T), F32),
        in_specs=[VMEM, VMEM],
        out_specs=HBM,
        scratch_shapes=[pltpu.SemaphoreType.DMA((4,))],
        compiler_params=PARAMS,
        name="join",
    )(keep, other)
    arrived = lax.all_to_all(joined, "gy", split_axis=0, concat_axis=0, tiled=True)
    own = arrived[:, :ROWS, :].reshape(GY * ROWS, T)
    own_meta = arrived[:, ROWS * (1 + V), :] + 0.0 * band[0, 0, :GY, :T].astype(F32)
    update = pl.pallas_call(
        update_kernel,
        out_shape=jax.ShapeDtypeStruct((GY * ROWS, T), F32),
        in_specs=[VMEM] * 4,
        out_specs=VMEM,
        compiler_params=PARAMS,
        name="update",
    )
    chunk = jax.ShapeDtypeStruct((GY * ROWS, T), F32)
    inside = pl.pallas_call(
        inside_kernel,
        out_shape=chunk,
        in_specs=[VMEM],
        out_specs=VMEM,
        compiler_params=PARAMS,
        cost_estimate=COST,
        name="inside",
    )
    doubled = [pltpu.VMEM((b, 2 * GY, 8, T), F32) for b in (2, 4)]
    front = pl.pallas_call(
        front_kernel,
        out_shape=jax.ShapeDtypeStruct((V, ROWS, GY * T), F32),
        in_specs=[SMEM] + [VMEM] * 3,
        out_specs=VMEM,
        scratch_shapes=[doubled[1], doubled[1], pltpu.VMEM((V, 4 * ROWS, GY * T), BF16)],
        compiler_params=PARAMS,
        cost_estimate=COST,
        name="front",
    )
    middle = pl.pallas_call(
        core_kernel,
        out_shape=(chunk, jax.ShapeDtypeStruct((V, GY * ROWS, T), F32)),
        in_specs=[SMEM] + [VMEM] * 6,
        out_specs=(VMEM, VMEM),
        scratch_shapes=[
            doubled[0],
            doubled[0],
            pltpu.VMEM((V, 2 * ROWS, GY * T), BF16),
            doubled[0],
            pltpu.VMEM((V, ROWS, GY * T), F32),
            pltpu.VMEM((V, ROWS, GY * T), F32),
        ],
        compiler_params=PARAMS,
        cost_estimate=COST,
        name="middle",
    )
    tail = pl.pallas_call(
        tail_kernel,
        out_shape=(chunk, chunk),
        in_specs=[SMEM] + [VMEM] * 2,
        out_specs=(VMEM, VMEM),
        scratch_shapes=[doubled[1]],
        compiler_params=PARAMS,
        cost_estimate=COST,
        name="tail",
    )
    for sweep in range(ITERS):
        out = jnp.concatenate([own, own_meta], axis=0) if sweep == 0 else own
        paired = lax.ppermute(out, AXES, PAIR)
        swapped = lax.ppermute(out, AXES, SWAP)
        if sweep == 0:
            near_meta = jnp.concatenate(
                [own_meta[:, :META], swapped[GY * ROWS :, :META]], axis=0
            ).astype(jnp.int32)
        near = front(near_meta, own, swapped, near_in)
        if sweep == 0:
            pair_meta = (paired[GY * ROWS :, :META] + 0.0 * near[0, :, :META]).astype(jnp.int32)
        pair, again = middle(pair_meta, paired, near, arrived, band, pair_in, pair_back)
        mid, swap = tail(near_meta, again, near_back)
        own = update(
            own, mid, inside(lax.ppermute(pair, AXES, PAIR)), lax.ppermute(swap, AXES, SWAP)
        )
    home = lax.all_to_all(
        own.reshape(GY, ROWS, T), "gy", split_axis=0, concat_axis=0, tiled=True
    )
    theirs = jnp.where(inner, jnp.concatenate([home[0:4], home[12:16]], axis=0), home[4:12])
    got = lax.ppermute(theirs, AXES, SWAP)
    return pl.pallas_call(
        unpack_kernel,
        out_shape=jax.ShapeDtypeStruct((Z, T, T), F32),
        in_specs=[VMEM, VMEM],
        out_specs=VMEM,
        compiler_params=PARAMS,
        name="unpack",
    )(home, got)


def solution(mesh):
    placed = (
        P(None, "gx", "gy"),
        P(None, None, "gx", "gy"),
        P(),
        P(),
        P(None, "gx"),
        P(None, "gx", "gy"),
    )
    return jax.shard_map(
        body, mesh=mesh, in_specs=placed, out_specs=P(None, "gx", "gy"), check_vma=False
    )
```

```python
import jax
import jax.numpy as jnp
from jax import lax
from jax.experimental import pallas as pl
from jax.experimental.pallas import tpu as pltpu
from jax.sharding import PartitionSpec as P

ITERS = 2
V = 4
Z = 2
T = 128
ROWS = 16
GY = 16
GX = 8
CHUNKS = 64
META = 16
UNIT = ROWS * (1 + V) + 8
AXES = ("gx", "gy")
F32 = jnp.float32
BF16 = jnp.bfloat16
VMEM = pl.BlockSpec(memory_space=pltpu.VMEM)
COST = pl.CostEstimate(flops=1_000_000_000, bytes_accessed=4_000_000, transcendentals=0)
HBM = pl.BlockSpec(memory_space=pltpu.HBM)
SMEM = pl.BlockSpec(memory_space=pltpu.SMEM)
PARAMS = pltpu.CompilerParams(vmem_limit_bytes=48 * 1024 * 1024)


def device_of(plane, chunk):
    core, block = chunk % 2, chunk // 2
    group, tile, part = block // 8, block % 8 // 4, block % 4
    inner = (tile == 0) == (group % 2 == 0)
    row = (1 if inner else 0, 2 if inner else 3)[plane]
    return (2 * group + core) * GY + 4 * row + (part if tile == 0 else 3 - part)


def both_ways(pairs):
    return [(a, b) for a, b in pairs] + [(b, a) for a, b in pairs]


SWAP = both_ways([(2 * x * GY + g, (2 * x + 1) * GY + g) for x in range(GX // 2) for g in range(GY)])
PAIR = both_ways(
    [
        (device_of(p, q), device_of(p, q + 1))
        for p in range(Z) for q in range(1, CHUNKS - 1, 2)
    ]
    + [(device_of(0, q), device_of(1, q)) for q in (0, CHUNKS - 1)]
)


def own_tile_inner():
    core, group = lax.axis_index("gx") % 2, lax.axis_index("gx") // 2
    return core, (core + group) % 2 == 0


def here():
    core, group = lax.axis_index("gx") % 2, lax.axis_index("gx") // 2
    row, col = lax.axis_index("gy") // 4, lax.axis_index("gy") % 4
    inner = jnp.where((row == 1) | (row == 2), 1, 0)
    first_tile = (inner + group) % 2 == 1
    block = 8 * group + jnp.where(first_tile, col, 7 - col)
    paired = jnp.where(core == 0, block > 0, block < CHUNKS // 2 - 1)
    return core, jnp.where(paired, 1.0, 0.0).astype(F32)


def part_of(col, core):
    return jnp.where(core == 0, col, 3 - col)


def split(x):
    hi = x.astype(BF16)
    return hi, (x - hi.astype(F32)).astype(BF16)


def pack(sub, out_ref, codes_hbm, shifts_hbm, est_hbm, views_hbm, codes_ref, shifts_ref, est, views, sems):
    core, _ = own_tile_inner()
    copies = [
        pltpu.make_async_copy(codes_hbm, codes_ref, sems.at[0]),
        pltpu.make_async_copy(shifts_hbm, shifts_ref, sems.at[1]),
        pltpu.make_async_copy(est_hbm.at[:, :, sub], est, sems.at[2]),
        pltpu.make_async_copy(views_hbm.at[:, :, :, sub], views, sems.at[3]),
    ]
    for copy in copies:
        copy.start()
    for copy in copies:
        copy.wait()
    lane = lax.broadcasted_iota(jnp.int32, (8, T), 1)
    for slot in range(8):
        plane, part = slot // 4, part_of(slot % 4, core)
        block = 4 * part + 2 * sub
        meta = jnp.zeros((8, T), F32)
        for half in range(2):
            for v in range(V):
                code = codes_ref[v, block + half].astype(F32)
                shift = shifts_ref[v, block + half].astype(F32)
                meta = jnp.where(lane == half * V + v, code, meta)
                meta = jnp.where(lane == 8 + half * V + v, shift, meta)
        out_ref[slot, 0:ROWS, :] = est[plane, part]
        for v in range(V):
            out_ref[slot, pl.ds(ROWS * (1 + v), ROWS), :] = views[v, plane, part].astype(F32)
        out_ref[slot, pl.ds(ROWS * (1 + V), 8), :] = meta


def place(ref, near, out_hbm, sems):
    first, second = jnp.where(near, 4, 0), jnp.where(near, 8, 12)
    copies = [
        pltpu.make_async_copy(ref.at[0:4], out_hbm.at[pl.ds(first, 4)], sems.at[0]),
        pltpu.make_async_copy(ref.at[4:8], out_hbm.at[pl.ds(second, 4)], sems.at[1]),
    ]
    for copy in copies:
        copy.start()
    for copy in copies:
        copy.wait()


def send_kernel(codes_hbm, shifts_hbm, est_hbm, views_hbm, send_ref, *scratch):
    core, _ = own_tile_inner()
    pack(1 - core, send_ref, codes_hbm, shifts_hbm, est_hbm, views_hbm, *scratch)


def keep_kernel(codes_hbm, shifts_hbm, est_hbm, views_hbm, out_hbm, kept, place_sems, *scratch):
    core, inner = own_tile_inner()
    pack(core, kept, codes_hbm, shifts_hbm, est_hbm, views_hbm, *scratch)
    place(kept, inner, out_hbm, place_sems)


def join_kernel(kept_hbm, other_ref, out_hbm, sems):
    _, inner = own_tile_inner()
    place(other_ref, jnp.logical_not(inner), out_hbm, sems)


def inside_kernel(paired_ref, out_ref):
    _, has_pair = here()
    out_ref[...] = paired_ref[...] * has_pair


def update_kernel(own_ref, mid_ref, paired_ref, swapped_ref, out_ref):
    total = mid_ref[...] + paired_ref[...] + swapped_ref[...]
    out_ref[...] = own_ref[0 : GY * ROWS, :] * (total * 0.25)


def unpack_kernel(home_ref, got_ref, out_ref):
    core, inner = own_tile_inner()
    for slot in range(8):
        plane, col = slot // 4, slot % 4
        start = 2 * part_of(col, core)
        source = jnp.where(inner, 4 + slot, 12 * plane + col)
        for sub, value in ((core, home_ref[source]), (1 - core, got_ref[slot])):
            rows = pl.ds(pl.multiple_of((start + sub) * ROWS, ROWS), ROWS)
            out_ref[plane, rows, :] = value


def put_split(ref, v, pieces, stacked=False):
    axis = 0 if stacked else 1
    hi = jnp.concatenate([p[0] for p in pieces], axis=axis)
    lo = jnp.concatenate([p[1] for p in pieces], axis=axis)
    ref[v] = jnp.concatenate(
        [
            jnp.concatenate([hi, hi], axis=1),
            jnp.concatenate([lo, jnp.zeros_like(lo)], axis=1),
        ],
        axis=0,
    )


def base_rows(psf_ref, width, at):
    taps = psf_ref[...]
    taps = taps / jnp.sum(taps, axis=1, keepdims=True)
    lane = lax.broadcasted_iota(jnp.int32, (V, width), 1)
    back, straight = jnp.zeros((V, width), F32), jnp.zeros((V, width), F32)
    count = taps.shape[1]
    for t in range(count):
        tap = jnp.broadcast_to(taps[:, t : t + 1], (V, width))
        back = jnp.where(lane == at[0] + count - 1 - t, tap, back)
        straight = jnp.where(lane == at[1] + t, tap, straight)
    return back, straight


def taps_kernel(
    psf_rows_ref, psf_cols_ref, band_ref, pair_in_ref, near_in_ref, pair_back_ref, near_back_ref
):
    core, _ = own_tile_inner()
    col_bases = base_rows(psf_cols_ref, 2 * T, (177, 177))
    back_base, row_base = base_rows(psf_rows_ref, T, (T - 31, 1))

    def either(a, b):
        return tuple(jnp.where(core == 0, x, y) for x, y in zip(a, b))

    def turned(base, count, width):
        rows = jnp.broadcast_to(base, (count, base.shape[1]))
        return split(pltpu.roll(rows, 0, 1, stride=1, stride_axis=0)[:, :width])

    for v in range(V):
        for d in range(2):
            hi, lo = turned(col_bases[d][v : v + 1], 2 * T, T)
            band_ref[v, d, 0 : 2 * T, 0:T] = hi
            band_ref[v, d, 0 : 2 * T, T : 2 * T] = lo
            band_ref[v, d, 2 * T : 4 * T, 0:T] = hi
            band_ref[v, d, 2 * T : 4 * T, T : 2 * T] = jnp.zeros_like(lo)
        before, own, after = [
            turned(pltpu.roll(jnp.broadcast_to(row_base[v : v + 1], (8, T)), (T - ROWS * i) % T, 1)[0:1], ROWS, ROWS) for i in range(3)
        ]
        put_split(pair_in_ref, v, [either(before, after)])
        put_split(near_in_ref, v, [own, either(after, before)])
        before, own, after = [
            turned(pltpu.roll(jnp.broadcast_to(back_base[v : v + 1], (8, T)), ROWS * i, 1)[0:1], ROWS, ROWS) for i in range(3)
        ]
        put_split(pair_back_ref, v, [either(before, after)], stacked=True)
        put_split(near_back_ref, v, [own, either(after, before)], stacked=True)


def column_pass(pieces, band):
    lane = lax.broadcasted_iota(jnp.int32, (ROWS, T), 1)
    turned = [pltpu.roll(p, T // 2, 1) for p in pieces]
    zero = jnp.zeros((ROWS, T), F32)
    turned = [zero] + turned + [zero]
    moved = [
        jnp.where(lane < T // 2, turned[j], turned[j + 1]) for j in range(len(pieces) + 1)
    ]
    his, los = zip(*[split(m) for m in moved])
    windows = [
        jnp.concatenate([his[c], his[c + 1], los[c], los[c + 1]], axis=1)
        for c in range(len(pieces))
    ]
    both = jnp.dot(jnp.concatenate(windows, axis=0), band, preferred_element_type=F32)
    return both[:, :T] + both[:, T:]


def column_tiles(ref, v):
    return [ref[v, :, T * c : T * c + T] for c in range(GY)]


def own_block(ref, half):
    return ref[0 : GY * ROWS, :].reshape(GY, ROWS, T)[:, 8 * half : 8 * half + 8, :]


def inner_lanes():
    lane = lax.broadcasted_iota(jnp.int32, (8, T), 1)
    return jnp.where(lane < T - 1, 1.0 / 16.0, 0.0).astype(F32)


def put_twice(b, x, est2, slope2):
    d = (pltpu.roll(x, T - 1, 2) - x) * inner_lanes()
    for copy in range(2):
        est2[b, GY * copy : GY * copy + GY] = x
        slope2[b, GY * copy : GY * copy + GY] = d


def code_of(meta_ref, v, b, c):
    return meta_ref[GY * (b // 2) + c, b % 2 * V + v].astype(F32)


def shift_of(meta_ref, v, b):
    return meta_ref[GY * (b // 2), 8 + b % 2 * V + v]


def gather(v, meta_ref, est2, slope2, view_u):
    count = est2.shape[0] // 2
    for src in range(count):
        parts = []
        for b in (2 * src, 2 * src + 1):
            shift = shift_of(meta_ref, v, b)
            x = est2[b, pl.ds(shift, GY)]
            d = slope2[b, pl.ds(shift, GY)]
            parts.append([x[c] + code_of(meta_ref, v, b, c) * d[c] for c in range(GY)])
        for c in range(GY):
            hi, lo = split(jnp.concatenate([parts[0][c], parts[1][c]], axis=0))
            cols = slice(T * c, T * c + T)
            view_u[v, ROWS * src : ROWS * src + ROWS, cols] = hi
            view_u[v, ROWS * (count + src) : ROWS * (count + src + 1), cols] = lo


def product(weights, values):
    both = jnp.dot(weights, values, preferred_element_type=F32)
    return both[: both.shape[0] // 2] + both[both.shape[0] // 2 :]


def rows_back(v, meta_ref, back_ref, again, total2):
    his, los = zip(*[split(again[v, ROWS * c : ROWS * c + ROWS, :]) for c in range(GY)])
    values = jnp.concatenate(
        [jnp.concatenate(his, axis=1), jnp.concatenate(los, axis=1)], axis=0
    )
    spread = product(back_ref[v], values)
    inner = inner_lanes()
    for b in range(total2.shape[0]):
        parts = []
        for c in range(GY):
            r = spread[8 * b : 8 * b + 8, T * c : T * c + T]
            g = r * inner
            g = pltpu.roll(g, 1, 1) - g
            parts.append(r + code_of(meta_ref, v, b, c) * g)
        total2[b, pl.ds(shift_of(meta_ref, v, b), GY)] += jnp.stack(parts)


def put_joined(ref, src, total2):
    for half in range(2):
        b = 2 * src + half
        y = total2[b, 0:GY] + total2[b, GY : 2 * GY]
        for c in range(GY):
            ref[ROWS * c + 8 * half : ROWS * c + 8 * half + 8, :] = y[c]


def in_turn(stages):
    for turn in range(V + len(stages) - 1):
        for i, stage in enumerate(stages):
            if 0 <= turn - i < V:
                stage(turn - i)


def front_kernel(meta_ref, own_ref, swapped_ref, near_in_ref, smooth_ref, est2, slope2, view_u):
    for src, ref in enumerate((own_ref, swapped_ref)):
        for half in range(2):
            put_twice(2 * src + half, own_block(ref, half), est2, slope2)

    def rows_in(v):
        smooth_ref[v] = product(near_in_ref[v], view_u[v])

    in_turn((lambda v: gather(v, meta_ref, est2, slope2, view_u), rows_in))


def core_kernel(
    meta_ref, paired_ref, near_ref, arrived_ref, band_ref, pair_in_ref, pair_back_ref,
    pair_ref, again_ref, est2, slope2, view_u, total2, smooth, ratio,
):
    _, has_pair = here()
    for half in range(2):
        put_twice(half, own_block(paired_ref, half) * has_pair, est2, slope2)
    total2[...] = jnp.zeros(total2.shape, F32)

    def rows_in(v):
        smooth[v] = near_ref[v] + product(pair_in_ref[v], view_u[v])

    def cols_in(v):
        blurred = column_pass(column_tiles(smooth, v), band_ref[v, 0])
        for c in range(GY):
            ratio[v, :, T * c : T * c + T] = (
                arrived_ref[c, ROWS * (1 + v) : ROWS * (2 + v), :]
                / blurred[ROWS * c : ROWS * c + ROWS, :]
            )

    def cols_back(v):
        again_ref[v] = column_pass(column_tiles(ratio, v), band_ref[v, 1])

    in_turn((
        lambda v: gather(v, meta_ref, est2, slope2, view_u),
        rows_in,
        cols_in,
        cols_back,
        lambda v: rows_back(v, meta_ref, pair_back_ref, again_ref, total2),
    ))
    put_joined(pair_ref, 0, total2)


def tail_kernel(meta_ref, again_ref, near_back_ref, mid_ref, swap_ref, total2):
    total2[...] = jnp.zeros(total2.shape, F32)
    for v in range(V):
        rows_back(v, meta_ref, near_back_ref, again_ref, total2)
    put_joined(mid_ref, 0, total2)
    put_joined(swap_ref, 1, total2)


def body(estimate, views, psf_rows, psf_cols, shifts, codes):
    _, inner = own_tile_inner()
    taken = [
        pltpu.with_memory_space_constraint(a, pltpu.HBM)
        for a in (
            codes[:, :, 0],
            shifts,
            estimate.reshape(Z, 4, 2, ROWS, T),
            views.reshape(V, Z, 4, 2, ROWS, T),
        )
    ]
    room = [
        pltpu.SMEM((V, 2 * 8), jnp.int32),
        pltpu.SMEM((V, 2 * 8), jnp.int32),
        pltpu.VMEM((Z, 4, ROWS, T), F32),
        pltpu.VMEM((V, Z, 4, ROWS, T), BF16),
        pltpu.SemaphoreType.DMA((4,)),
    ]
    two_sems = pltpu.SemaphoreType.DMA((2,))
    unit = jax.ShapeDtypeStruct((8, UNIT, T), F32)
    whole = jax.ShapeDtypeStruct((GY, UNIT, T), F32)
    send = pl.pallas_call(
        send_kernel,
        out_shape=unit,
        in_specs=[HBM] * 4,
        out_specs=VMEM,
        scratch_shapes=room,
        compiler_params=PARAMS,
        name="send",
    )(*taken)
    other = lax.ppermute(send, AXES, SWAP)
    kept = pl.pallas_call(
        keep_kernel,
        out_shape=whole,
        in_specs=[HBM] * 4,
        out_specs=HBM,
        scratch_shapes=[pltpu.VMEM((8, UNIT, T), F32), two_sems] + room,
        compiler_params=PARAMS,
        cost_estimate=COST,
        name="keep",
    )(*taken)
    joined = pl.pallas_call(
        join_kernel,
        out_shape=whole,
        in_specs=[HBM, VMEM],
        out_specs=HBM,
        scratch_shapes=[two_sems],
        input_output_aliases={0: 0},
        compiler_params=PARAMS,
        name="join",
    )(kept, other)

    band, pair_in, near_in, pair_back, near_back = pl.pallas_call(
        taps_kernel,
        out_shape=(
            jax.ShapeDtypeStruct((V, 2, 4 * T, 2 * T), BF16),
            jax.ShapeDtypeStruct((V, 2 * ROWS, 2 * ROWS), BF16),
            jax.ShapeDtypeStruct((V, 2 * ROWS, 4 * ROWS), BF16),
            jax.ShapeDtypeStruct((V, 2 * ROWS, 2 * ROWS), BF16),
            jax.ShapeDtypeStruct((V, 4 * ROWS, 2 * ROWS), BF16),
        ),
        in_specs=[VMEM, VMEM],
        out_specs=(VMEM,) * 5,
        compiler_params=PARAMS,
        cost_estimate=COST,
        name="taps",
    )(psf_rows, psf_cols)

    arrived = lax.all_to_all(joined, "gy", split_axis=0, concat_axis=0, tiled=True)
    own = arrived[:, :ROWS, :].reshape(GY * ROWS, T)
    own_meta = arrived[:, ROWS * (1 + V), :] + 0.0 * band[0, 0, :GY, :T].astype(F32)
    update = pl.pallas_call(
        update_kernel,
        out_shape=jax.ShapeDtypeStruct((GY * ROWS, T), F32),
        in_specs=[VMEM] * 4,
        out_specs=VMEM,
        compiler_params=PARAMS,
        name="update",
    )
    chunk = jax.ShapeDtypeStruct((GY * ROWS, T), F32)
    inside = pl.pallas_call(
        inside_kernel,
        out_shape=chunk,
        in_specs=[VMEM],
        out_specs=VMEM,
        compiler_params=PARAMS,
        cost_estimate=COST,
        name="inside",
    )
    doubled = [pltpu.VMEM((b, 2 * GY, 8, T), F32) for b in (2, 4)]
    front = pl.pallas_call(
        front_kernel,
        out_shape=jax.ShapeDtypeStruct((V, ROWS, GY * T), F32),
        in_specs=[SMEM] + [VMEM] * 3,
        out_specs=VMEM,
        scratch_shapes=[doubled[1], doubled[1], pltpu.VMEM((V, 4 * ROWS, GY * T), BF16)],
        compiler_params=PARAMS,
        cost_estimate=COST,
        name="front",
    )
    middle = pl.pallas_call(
        core_kernel,
        out_shape=(chunk, jax.ShapeDtypeStruct((V, GY * ROWS, T), F32)),
        in_specs=[SMEM] + [VMEM] * 6,
        out_specs=(VMEM, VMEM),
        scratch_shapes=[
            doubled[0],
            doubled[0],
            pltpu.VMEM((V, 2 * ROWS, GY * T), BF16),
            doubled[0],
            pltpu.VMEM((V, ROWS, GY * T), F32),
            pltpu.VMEM((V, ROWS, GY * T), F32),
        ],
        compiler_params=PARAMS,
        cost_estimate=COST,
        name="middle",
    )
    tail = pl.pallas_call(
        tail_kernel,
        out_shape=(chunk, chunk),
        in_specs=[SMEM] + [VMEM] * 2,
        out_specs=(VMEM, VMEM),
        scratch_shapes=[doubled[1]],
        compiler_params=PARAMS,
        cost_estimate=COST,
        name="tail",
    )
    for sweep in range(ITERS):
        out = jnp.concatenate([own, own_meta], axis=0) if sweep == 0 else own
        paired = lax.ppermute(out, AXES, PAIR)
        swapped = lax.ppermute(out, AXES, SWAP)
        if sweep == 0:
            near_meta = jnp.concatenate(
                [own_meta[:, :META], swapped[GY * ROWS :, :META]], axis=0
            ).astype(jnp.int32)
        near = front(near_meta, own, swapped, near_in)
        if sweep == 0:
            pair_meta = (paired[GY * ROWS :, :META] + 0.0 * near[0, :, :META]).astype(jnp.int32)
        pair, again = middle(pair_meta, paired, near, arrived, band, pair_in, pair_back)
        mid, swap = tail(near_meta, again, near_back)
        own = update(
            own, mid, inside(lax.ppermute(pair, AXES, PAIR)), lax.ppermute(swap, AXES, SWAP)
        )
    home = lax.all_to_all(
        own.reshape(GY, ROWS, T), "gy", split_axis=0, concat_axis=0, tiled=True
    )
    theirs = jnp.where(inner, jnp.concatenate([home[0:4], home[12:16]], axis=0), home[4:12])
    got = lax.ppermute(theirs, AXES, SWAP)
    return pl.pallas_call(
        unpack_kernel,
        out_shape=jax.ShapeDtypeStruct((Z, T, T), F32),
        in_specs=[VMEM, VMEM],
        out_specs=VMEM,
        compiler_params=PARAMS,
        name="unpack",
    )(home, got)


def solution(mesh):
    placed = (
        P(None, "gx", "gy"),
        P(None, None, "gx", "gy"),
        P(),
        P(),
        P(None, "gx"),
        P(None, "gx", "gy"),
    )
    return jax.shard_map(
        body, mesh=mesh, in_specs=placed, out_specs=P(None, "gx", "gy"), check_vma=False
    )
```

```python
import jax
import jax.numpy as jnp
from jax import lax
from jax.experimental import pallas as pl
from jax.experimental.pallas import tpu as pltpu
from jax.sharding import PartitionSpec as P

ITERS = 2
V = 4
Z = 2
T = 128
ROWS = 16
GY = 16
GX = 8
CHUNKS = 64
META = 16
UNIT = ROWS * (1 + V) + 8
AXES = ("gx", "gy")
F32 = jnp.float32
BF16 = jnp.bfloat16
VMEM = pl.BlockSpec(memory_space=pltpu.VMEM)
COST = pl.CostEstimate(flops=1_000_000_000, bytes_accessed=4_000_000, transcendentals=0)
HBM = pl.BlockSpec(memory_space=pltpu.HBM)
SMEM = pl.BlockSpec(memory_space=pltpu.SMEM)
PARAMS = pltpu.CompilerParams(vmem_limit_bytes=48 * 1024 * 1024)


def device_of(plane, chunk):
    core, block = chunk % 2, chunk // 2
    group, tile, part = block // 8, block % 8 // 4, block % 4
    inner = (tile == 0) == (group % 2 == 0)
    row = (1 if inner else 0, 2 if inner else 3)[plane]
    return (2 * group + core) * GY + 4 * row + (part if tile == 0 else 3 - part)


def both_ways(pairs):
    return [(a, b) for a, b in pairs] + [(b, a) for a, b in pairs]


SWAP = both_ways([(2 * x * GY + g, (2 * x + 1) * GY + g) for x in range(GX // 2) for g in range(GY)])
PAIR = both_ways(
    [
        (device_of(p, q), device_of(p, q + 1))
        for p in range(Z) for q in range(1, CHUNKS - 1, 2)
    ]
    + [(device_of(0, q), device_of(1, q)) for q in (0, CHUNKS - 1)]
)


def own_tile_inner():
    core, group = lax.axis_index("gx") % 2, lax.axis_index("gx") // 2
    return core, (core + group) % 2 == 0


def here():
    core, group = lax.axis_index("gx") % 2, lax.axis_index("gx") // 2
    row, col = lax.axis_index("gy") // 4, lax.axis_index("gy") % 4
    inner = jnp.where((row == 1) | (row == 2), 1, 0)
    first_tile = (inner + group) % 2 == 1
    block = 8 * group + jnp.where(first_tile, col, 7 - col)
    paired = jnp.where(core == 0, block > 0, block < CHUNKS // 2 - 1)
    return core, jnp.where(paired, 1.0, 0.0).astype(F32)


def part_of(col, core):
    return jnp.where(core == 0, col, 3 - col)


def split(x):
    hi = x.astype(BF16)
    return hi, (x - hi.astype(F32)).astype(BF16)


def pack(sub, slot_of, out_ref, codes_hbm, shifts_hbm, est_hbm, views_hbm, codes_ref, shifts_ref, est, views, sems):
    core, _ = own_tile_inner()
    copies = [
        pltpu.make_async_copy(codes_hbm, codes_ref, sems.at[0]),
        pltpu.make_async_copy(shifts_hbm, shifts_ref, sems.at[1]),
        pltpu.make_async_copy(est_hbm.at[:, :, sub], est, sems.at[2]),
        pltpu.make_async_copy(views_hbm.at[:, :, :, sub], views, sems.at[3]),
    ]
    for copy in copies:
        copy.start()
    for copy in copies:
        copy.wait()
    lane = lax.broadcasted_iota(jnp.int32, (8, T), 1)
    for slot in range(8):
        plane, part, at = slot // 4, part_of(slot % 4, core), slot_of(slot)
        block = 4 * part + 2 * sub
        meta = jnp.zeros((8, T), F32)
        for half in range(2):
            for v in range(V):
                code = codes_ref[v, block + half].astype(F32)
                shift = shifts_ref[v, block + half].astype(F32)
                meta = jnp.where(lane == half * V + v, code, meta)
                meta = jnp.where(lane == 8 + half * V + v, shift, meta)
        out_ref[at, 0:ROWS, :] = est[plane, part]
        for v in range(V):
            out_ref[at, pl.ds(ROWS * (1 + v), ROWS), :] = views[v, plane, part].astype(F32)
        out_ref[at, pl.ds(ROWS * (1 + V), 8), :] = meta


def halves(near):
    return jnp.where(near, 4, 0), jnp.where(near, 8, 12)


def send_kernel(codes_hbm, shifts_hbm, est_hbm, views_hbm, send_ref, *scratch):
    core, _ = own_tile_inner()
    pack(1 - core, lambda slot: slot, send_ref, codes_hbm, shifts_hbm, est_hbm, views_hbm, *scratch)


def keep_kernel(codes_hbm, shifts_hbm, est_hbm, views_hbm, out_ref, *scratch):
    core, inner = own_tile_inner()
    starts = halves(inner)
    pack(
        core, lambda slot: starts[slot // 4] + slot % 4, out_ref,
        codes_hbm, shifts_hbm, est_hbm, views_hbm, *scratch,
    )


def join_kernel(kept_ref, other_ref, out_ref):
    _, inner = own_tile_inner()
    for i, start in enumerate(halves(jnp.logical_not(inner))):
        out_ref[pl.ds(start, 4)] = other_ref[4 * i : 4 * i + 4]


def lead_kernel(arrived_ref, out_ref):
    for c in range(GY):
        out_ref[ROWS * c : ROWS * c + ROWS, :] = arrived_ref[c, 0:ROWS, :]
        meta = arrived_ref[c, ROWS * (1 + V) : ROWS * (1 + V) + 1, :]
        out_ref[GY * ROWS + c : GY * ROWS + c + 1, :] = meta


def inside_kernel(paired_ref, out_ref):
    _, has_pair = here()
    out_ref[...] = paired_ref[...] * has_pair


def update_kernel(own_ref, mid_ref, paired_ref, swapped_ref, out_ref):
    total = mid_ref[...] + paired_ref[...] + swapped_ref[...]
    out_ref[...] = own_ref[0 : GY * ROWS, :] * (total * 0.25)


def theirs_kernel(home_ref, out_ref):
    _, inner = own_tile_inner()
    out_ref[0:4] = home_ref[pl.ds(jnp.where(inner, 0, 4), 4)]
    out_ref[4:8] = home_ref[pl.ds(jnp.where(inner, 12, 8), 4)]


def unpack_kernel(home_ref, got_ref, out_ref):
    core, inner = own_tile_inner()
    for slot in range(8):
        plane, col = slot // 4, slot % 4
        start = 2 * part_of(col, core)
        source = jnp.where(inner, 4 + slot, 12 * plane + col)
        for sub, value in ((core, home_ref[source]), (1 - core, got_ref[slot])):
            rows = pl.ds(pl.multiple_of((start + sub) * ROWS, ROWS), ROWS)
            out_ref[plane, rows, :] = value


def put_split(ref, v, pieces, stacked=False):
    axis = 0 if stacked else 1
    hi = jnp.concatenate([p[0] for p in pieces], axis=axis)
    lo = jnp.concatenate([p[1] for p in pieces], axis=axis)
    ref[v] = jnp.concatenate(
        [
            jnp.concatenate([hi, hi], axis=1),
            jnp.concatenate([lo, jnp.zeros_like(lo)], axis=1),
        ],
        axis=0,
    )


def base_rows(psf_ref, width, at):
    taps = psf_ref[...]
    taps = taps / jnp.sum(taps, axis=1, keepdims=True)
    lane = lax.broadcasted_iota(jnp.int32, (V, width), 1)
    back, straight = jnp.zeros((V, width), F32), jnp.zeros((V, width), F32)
    count = taps.shape[1]
    for t in range(count):
        tap = jnp.broadcast_to(taps[:, t : t + 1], (V, width))
        back = jnp.where(lane == at[0] + count - 1 - t, tap, back)
        straight = jnp.where(lane == at[1] + t, tap, straight)
    return back, straight


def taps_kernel(
    psf_rows_ref, psf_cols_ref, band_ref, pair_in_ref, near_in_ref, pair_back_ref, near_back_ref
):
    core, _ = own_tile_inner()
    col_bases = base_rows(psf_cols_ref, 2 * T, (177, 177))
    back_base, row_base = base_rows(psf_rows_ref, T, (T - 31, 1))

    def either(a, b):
        return tuple(jnp.where(core == 0, x, y) for x, y in zip(a, b))

    def turned(base, count, width):
        rows = jnp.broadcast_to(base, (count, base.shape[1]))
        return split(pltpu.roll(rows, 0, 1, stride=1, stride_axis=0)[:, :width])

    for v in range(V):
        for d in range(2):
            hi, lo = turned(col_bases[d][v : v + 1], 2 * T, T)
            band_ref[v, d, 0 : 2 * T, 0:T] = hi
            band_ref[v, d, 0 : 2 * T, T : 2 * T] = lo
            band_ref[v, d, 2 * T : 4 * T, 0:T] = hi
            band_ref[v, d, 2 * T : 4 * T, T : 2 * T] = jnp.zeros_like(lo)
        before, own, after = [
            turned(pltpu.roll(jnp.broadcast_to(row_base[v : v + 1], (8, T)), (T - ROWS * i) % T, 1)[0:1], ROWS, ROWS) for i in range(3)
        ]
        put_split(pair_in_ref, v, [either(before, after)])
        put_split(near_in_ref, v, [own, either(after, before)])
        before, own, after = [
            turned(pltpu.roll(jnp.broadcast_to(back_base[v : v + 1], (8, T)), ROWS * i, 1)[0:1], ROWS, ROWS) for i in range(3)
        ]
        put_split(pair_back_ref, v, [either(before, after)], stacked=True)
        put_split(near_back_ref, v, [own, either(after, before)], stacked=True)


def column_pass(pieces, band):
    lane = lax.broadcasted_iota(jnp.int32, (ROWS, T), 1)
    turned = [pltpu.roll(p, T // 2, 1) for p in pieces]
    zero = jnp.zeros((ROWS, T), F32)
    turned = [zero] + turned + [zero]
    moved = [
        jnp.where(lane < T // 2, turned[j], turned[j + 1]) for j in range(len(pieces) + 1)
    ]
    his, los = zip(*[split(m) for m in moved])
    windows = [
        jnp.concatenate([his[c], his[c + 1], los[c], los[c + 1]], axis=1)
        for c in range(len(pieces))
    ]
    both = jnp.dot(jnp.concatenate(windows, axis=0), band, preferred_element_type=F32)
    return both[:, :T] + both[:, T:]


def column_tiles(ref, v):
    return [ref[v, :, T * c : T * c + T] for c in range(GY)]


def own_block(ref, half):
    return ref[0 : GY * ROWS, :].reshape(GY, ROWS, T)[:, 8 * half : 8 * half + 8, :]


def inner_lanes():
    lane = lax.broadcasted_iota(jnp.int32, (8, T), 1)
    return jnp.where(lane < T - 1, 1.0 / 16.0, 0.0).astype(F32)


def put_twice(b, x, est2, slope2):
    d = (pltpu.roll(x, T - 1, 2) - x) * inner_lanes()
    for copy in range(2):
        est2[b, GY * copy : GY * copy + GY] = x
        slope2[b, GY * copy : GY * copy + GY] = d


def code_of(meta_ref, v, b, c):
    return meta_ref[GY * (b // 2) + c, b % 2 * V + v].astype(F32)


def shift_of(meta_ref, v, b):
    return meta_ref[GY * (b // 2), 8 + b % 2 * V + v]


def gather(v, meta_ref, est2, slope2, view_u):
    count = est2.shape[0] // 2
    for src in range(count):
        parts = []
        for b in (2 * src, 2 * src + 1):
            shift = shift_of(meta_ref, v, b)
            x = est2[b, pl.ds(shift, GY)]
            d = slope2[b, pl.ds(shift, GY)]
            parts.append([x[c] + code_of(meta_ref, v, b, c) * d[c] for c in range(GY)])
        for c in range(GY):
            hi, lo = split(jnp.concatenate([parts[0][c], parts[1][c]], axis=0))
            cols = slice(T * c, T * c + T)
            view_u[v, ROWS * src : ROWS * src + ROWS, cols] = hi
            view_u[v, ROWS * (count + src) : ROWS * (count + src + 1), cols] = lo


def product(weights, values):
    both = jnp.dot(weights, values, preferred_element_type=F32)
    return both[: both.shape[0] // 2] + both[both.shape[0] // 2 :]


def rows_back(v, meta_ref, back_ref, again, total2):
    his, los = zip(*[split(again[v, ROWS * c : ROWS * c + ROWS, :]) for c in range(GY)])
    values = jnp.concatenate(
        [jnp.concatenate(his, axis=1), jnp.concatenate(los, axis=1)], axis=0
    )
    spread = product(back_ref[v], values)
    inner = inner_lanes()
    for b in range(total2.shape[0]):
        parts = []
        for c in range(GY):
            r = spread[8 * b : 8 * b + 8, T * c : T * c + T]
            g = r * inner
            g = pltpu.roll(g, 1, 1) - g
            parts.append(r + code_of(meta_ref, v, b, c) * g)
        total2[b, pl.ds(shift_of(meta_ref, v, b), GY)] += jnp.stack(parts)


def put_joined(ref, src, total2):
    for half in range(2):
        b = 2 * src + half
        y = total2[b, 0:GY] + total2[b, GY : 2 * GY]
        for c in range(GY):
            ref[ROWS * c + 8 * half : ROWS * c + 8 * half + 8, :] = y[c]


def in_turn(stages):
    for turn in range(V + len(stages) - 1):
        for i, stage in enumerate(stages):
            if 0 <= turn - i < V:
                stage(turn - i)


def front_kernel(meta_ref, own_ref, swapped_ref, near_in_ref, smooth_ref, est2, slope2, view_u):
    for src, ref in enumerate((own_ref, swapped_ref)):
        for half in range(2):
            put_twice(2 * src + half, own_block(ref, half), est2, slope2)

    def rows_in(v):
        smooth_ref[v] = product(near_in_ref[v], view_u[v])

    in_turn((lambda v: gather(v, meta_ref, est2, slope2, view_u), rows_in))


def core_kernel(
    meta_ref, paired_ref, near_ref, arrived_ref, band_ref, pair_in_ref, pair_back_ref,
    pair_ref, again_ref, est2, slope2, view_u, total2, smooth, ratio,
):
    _, has_pair = here()
    for half in range(2):
        put_twice(half, own_block(paired_ref, half) * has_pair, est2, slope2)
    total2[...] = jnp.zeros(total2.shape, F32)

    def rows_in(v):
        smooth[v] = near_ref[v] + product(pair_in_ref[v], view_u[v])

    def cols_in(v):
        blurred = column_pass(column_tiles(smooth, v), band_ref[v, 0])
        for c in range(GY):
            ratio[v, :, T * c : T * c + T] = (
                arrived_ref[c, ROWS * (1 + v) : ROWS * (2 + v), :]
                / blurred[ROWS * c : ROWS * c + ROWS, :]
            )

    def cols_back(v):
        again_ref[v] = column_pass(column_tiles(ratio, v), band_ref[v, 1])

    in_turn((
        lambda v: gather(v, meta_ref, est2, slope2, view_u),
        rows_in,
        cols_in,
        cols_back,
        lambda v: rows_back(v, meta_ref, pair_back_ref, again_ref, total2),
    ))
    put_joined(pair_ref, 0, total2)


def tail_kernel(meta_ref, again_ref, near_back_ref, mid_ref, swap_ref, total2):
    total2[...] = jnp.zeros(total2.shape, F32)
    for v in range(V):
        rows_back(v, meta_ref, near_back_ref, again_ref, total2)
    put_joined(mid_ref, 0, total2)
    put_joined(swap_ref, 1, total2)


def all_to_all(blocks):
    blocks = pltpu.with_memory_space_constraint(blocks, pltpu.VMEM)
    return lax.all_to_all(blocks, "gy", split_axis=0, concat_axis=0, tiled=True)


def body(estimate, views, psf_rows, psf_cols, shifts, codes):
    _, inner = own_tile_inner()
    taken = [
        pltpu.with_memory_space_constraint(a, pltpu.HBM)
        for a in (
            codes[:, :, 0],
            shifts,
            estimate.reshape(Z, 4, 2, ROWS, T),
            views.reshape(V, Z, 4, 2, ROWS, T),
        )
    ]
    room = [
        pltpu.SMEM((V, 2 * 8), jnp.int32),
        pltpu.SMEM((V, 2 * 8), jnp.int32),
        pltpu.VMEM((Z, 4, ROWS, T), F32),
        pltpu.VMEM((V, Z, 4, ROWS, T), BF16),
        pltpu.SemaphoreType.DMA((4,)),
    ]
    unit = jax.ShapeDtypeStruct((8, UNIT, T), F32)
    whole = jax.ShapeDtypeStruct((GY, UNIT, T), F32)
    send = pl.pallas_call(
        send_kernel,
        out_shape=unit,
        in_specs=[HBM] * 4,
        out_specs=VMEM,
        scratch_shapes=room,
        compiler_params=PARAMS,
        name="send",
    )(*taken)
    other = lax.ppermute(send, AXES, SWAP)
    kept = pl.pallas_call(
        keep_kernel,
        out_shape=whole,
        in_specs=[HBM] * 4,
        out_specs=VMEM,
        scratch_shapes=room,
        compiler_params=PARAMS,
        cost_estimate=COST,
        name="keep",
    )(*taken)
    joined = pl.pallas_call(
        join_kernel,
        out_shape=whole,
        in_specs=[VMEM, VMEM],
        out_specs=VMEM,
        input_output_aliases={0: 0},
        compiler_params=PARAMS,
        name="join",
    )(kept, other)

    band, pair_in, near_in, pair_back, near_back = pl.pallas_call(
        taps_kernel,
        out_shape=(
            jax.ShapeDtypeStruct((V, 2, 4 * T, 2 * T), BF16),
            jax.ShapeDtypeStruct((V, 2 * ROWS, 2 * ROWS), BF16),
            jax.ShapeDtypeStruct((V, 2 * ROWS, 4 * ROWS), BF16),
            jax.ShapeDtypeStruct((V, 2 * ROWS, 2 * ROWS), BF16),
            jax.ShapeDtypeStruct((V, 4 * ROWS, 2 * ROWS), BF16),
        ),
        in_specs=[VMEM, VMEM],
        out_specs=(VMEM,) * 5,
        compiler_params=PARAMS,
        name="taps",
    )(psf_rows, psf_cols)

    arrived = all_to_all(joined)
    lead = pl.pallas_call(
        lead_kernel,
        out_shape=jax.ShapeDtypeStruct((GY * ROWS + GY, T), F32),
        in_specs=[VMEM],
        out_specs=VMEM,
        compiler_params=PARAMS,
        name="lead",
    )(arrived)
    own_meta = lead[GY * ROWS :, :META]
    update = pl.pallas_call(
        update_kernel,
        out_shape=jax.ShapeDtypeStruct((GY * ROWS, T), F32),
        in_specs=[VMEM] * 4,
        out_specs=VMEM,
        compiler_params=PARAMS,
        name="update",
    )
    chunk = jax.ShapeDtypeStruct((GY * ROWS, T), F32)
    inside = pl.pallas_call(
        inside_kernel,
        out_shape=chunk,
        in_specs=[VMEM],
        out_specs=VMEM,
        compiler_params=PARAMS,
        cost_estimate=COST,
        name="inside",
    )
    doubled = [pltpu.VMEM((b, 2 * GY, 8, T), F32) for b in (2, 4)]
    front = pl.pallas_call(
        front_kernel,
        out_shape=jax.ShapeDtypeStruct((V, ROWS, GY * T), F32),
        in_specs=[SMEM] + [VMEM] * 3,
        out_specs=VMEM,
        scratch_shapes=[doubled[1], doubled[1], pltpu.VMEM((V, 4 * ROWS, GY * T), BF16)],
        compiler_params=PARAMS,
        name="front",
    )
    middle = pl.pallas_call(
        core_kernel,
        out_shape=(chunk, jax.ShapeDtypeStruct((V, GY * ROWS, T), F32)),
        in_specs=[SMEM] + [VMEM] * 6,
        out_specs=(VMEM, VMEM),
        scratch_shapes=[
            doubled[0],
            doubled[0],
            pltpu.VMEM((V, 2 * ROWS, GY * T), BF16),
            doubled[0],
            pltpu.VMEM((V, ROWS, GY * T), F32),
            pltpu.VMEM((V, ROWS, GY * T), F32),
        ],
        compiler_params=PARAMS,
        cost_estimate=COST,
        name="middle",
    )
    tail = pl.pallas_call(
        tail_kernel,
        out_shape=(chunk, chunk),
        in_specs=[SMEM] + [VMEM] * 2,
        out_specs=(VMEM, VMEM),
        scratch_shapes=[doubled[1]],
        compiler_params=PARAMS,
        cost_estimate=COST,
        name="tail",
    )
    own = lead
    for sweep in range(ITERS):
        paired = lax.ppermute(own, AXES, PAIR)
        swapped = lax.ppermute(own, AXES, SWAP)
        if sweep == 0:
            near_meta = jnp.concatenate(
                [own_meta, swapped[GY * ROWS :, :META]], axis=0
            ).astype(jnp.int32)
        near = front(near_meta, own, swapped, near_in)
        if sweep == 0:
            pair_meta = (paired[GY * ROWS :, :META] + 0.0 * near[0, :, :META]).astype(jnp.int32)
        pair, again = middle(pair_meta, paired, near, arrived, band, pair_in, pair_back)
        mid, swap = tail(near_meta, again, near_back)
        own = update(
            own, mid, inside(lax.ppermute(pair, AXES, PAIR)), lax.ppermute(swap, AXES, SWAP)
        )
    home = all_to_all(own.reshape(GY, ROWS, T))
    theirs = pl.pallas_call(
        theirs_kernel,
        out_shape=jax.ShapeDtypeStruct((8, ROWS, T), F32),
        in_specs=[VMEM],
        out_specs=VMEM,
        compiler_params=PARAMS,
        name="theirs",
    )(home)
    got = lax.ppermute(theirs, AXES, SWAP)
    return pl.pallas_call(
        unpack_kernel,
        out_shape=jax.ShapeDtypeStruct((Z, T, T), F32),
        in_specs=[VMEM, VMEM],
        out_specs=VMEM,
        compiler_params=PARAMS,
        name="unpack",
    )(home, got)


def solution(mesh):
    placed = (
        P(None, "gx", "gy"),
        P(None, None, "gx", "gy"),
        P(),
        P(),
        P(None, "gx"),
        P(None, "gx", "gy"),
    )
    return jax.shard_map(
        body, mesh=mesh, in_specs=placed, out_specs=P(None, "gx", "gy"), check_vma=False
    )
```

```python
import jax
import jax.numpy as jnp
from jax import lax
from jax.experimental import pallas as pl
from jax.experimental.pallas import tpu as pltpu
from jax.sharding import PartitionSpec as P

ITERS = 2
V = 4
Z = 2
T = 128
ROWS = 16
GY = 16
GX = 8
CHUNKS = 64
META = 16
UNIT = ROWS * (1 + V) + 8
AXES = ("gx", "gy")
F32 = jnp.float32
BF16 = jnp.bfloat16
VMEM = pl.BlockSpec(memory_space=pltpu.VMEM)
COST = pl.CostEstimate(flops=1_000_000_000, bytes_accessed=4_000_000, transcendentals=0)
HBM = pl.BlockSpec(memory_space=pltpu.HBM)
SMEM = pl.BlockSpec(memory_space=pltpu.SMEM)
PARAMS = pltpu.CompilerParams(vmem_limit_bytes=48 * 1024 * 1024)


def device_of(plane, chunk):
    core, block = chunk % 2, chunk // 2
    group, tile, part = block // 8, block % 8 // 4, block % 4
    inner = (tile == 0) == (group % 2 == 0)
    row = (1 if inner else 0, 2 if inner else 3)[plane]
    return (2 * group + core) * GY + 4 * row + (part if tile == 0 else 3 - part)


def both_ways(pairs):
    return [(a, b) for a, b in pairs] + [(b, a) for a, b in pairs]


SWAP = both_ways([(2 * x * GY + g, (2 * x + 1) * GY + g) for x in range(GX // 2) for g in range(GY)])
PAIR = both_ways(
    [
        (device_of(p, q), device_of(p, q + 1))
        for p in range(Z) for q in range(1, CHUNKS - 1, 2)
    ]
    + [(device_of(0, q), device_of(1, q)) for q in (0, CHUNKS - 1)]
)


def own_tile_inner():
    core, group = lax.axis_index("gx") % 2, lax.axis_index("gx") // 2
    return core, (core + group) % 2 == 0


def here():
    core, group = lax.axis_index("gx") % 2, lax.axis_index("gx") // 2
    row, col = lax.axis_index("gy") // 4, lax.axis_index("gy") % 4
    inner = jnp.where((row == 1) | (row == 2), 1, 0)
    first_tile = (inner + group) % 2 == 1
    block = 8 * group + jnp.where(first_tile, col, 7 - col)
    paired = jnp.where(core == 0, block > 0, block < CHUNKS // 2 - 1)
    return core, jnp.where(paired, 1.0, 0.0).astype(F32)


def part_of(col, core):
    return jnp.where(core == 0, col, 3 - col)


def split(x):
    hi = x.astype(BF16)
    return hi, (x - hi.astype(F32)).astype(BF16)


def pack(sub, slot_of, out_ref, codes_hbm, shifts_hbm, est_hbm, views_hbm, codes_ref, shifts_ref, est, views, sems):
    core, _ = own_tile_inner()
    copies = [
        pltpu.make_async_copy(codes_hbm, codes_ref, sems.at[0]),
        pltpu.make_async_copy(shifts_hbm, shifts_ref, sems.at[1]),
        pltpu.make_async_copy(est_hbm.at[:, :, sub], est, sems.at[2]),
        pltpu.make_async_copy(views_hbm.at[:, :, :, sub], views, sems.at[3]),
    ]
    for copy in copies:
        copy.start()
    for copy in copies:
        copy.wait()
    lane = lax.broadcasted_iota(jnp.int32, (8, T), 1)
    for slot in range(8):
        plane, part, at = slot // 4, part_of(slot % 4, core), slot_of(slot)
        block = 4 * part + 2 * sub
        meta = jnp.zeros((8, T), F32)
        for half in range(2):
            for v in range(V):
                code = codes_ref[v, block + half].astype(F32)
                shift = shifts_ref[v, block + half].astype(F32)
                meta = jnp.where(lane == half * V + v, code, meta)
                meta = jnp.where(lane == 8 + half * V + v, shift, meta)
        out_ref[at, 0:ROWS, :] = est[plane, part]
        for v in range(V):
            out_ref[at, pl.ds(ROWS * (1 + v), ROWS), :] = views[v, plane, part].astype(F32)
        out_ref[at, pl.ds(ROWS * (1 + V), 8), :] = meta


def halves(near):
    return jnp.where(near, 4, 0), jnp.where(near, 8, 12)


def send_kernel(codes_hbm, shifts_hbm, est_hbm, views_hbm, send_ref, *scratch):
    core, _ = own_tile_inner()
    pack(1 - core, lambda slot: slot, send_ref, codes_hbm, shifts_hbm, est_hbm, views_hbm, *scratch)


def keep_kernel(codes_hbm, shifts_hbm, est_hbm, views_hbm, out_ref, *scratch):
    core, inner = own_tile_inner()
    starts = halves(inner)
    pack(
        core, lambda slot: starts[slot // 4] + slot % 4, out_ref,
        codes_hbm, shifts_hbm, est_hbm, views_hbm, *scratch,
    )


def join_kernel(kept_ref, other_ref, out_ref):
    _, inner = own_tile_inner()
    for i, start in enumerate(halves(jnp.logical_not(inner))):
        out_ref[pl.ds(start, 4)] = other_ref[4 * i : 4 * i + 4]


def lead_kernel(arrived_ref, out_ref):
    for c in range(GY):
        out_ref[ROWS * c : ROWS * c + ROWS, :] = arrived_ref[c, 0:ROWS, :]
        meta = arrived_ref[c, ROWS * (1 + V) : ROWS * (1 + V) + 1, :]
        out_ref[GY * ROWS + c : GY * ROWS + c + 1, :] = meta


def inside_kernel(paired_ref, out_ref):
    _, has_pair = here()
    out_ref[...] = paired_ref[...] * has_pair


def update_kernel(own_ref, mid_ref, paired_ref, swapped_ref, out_ref):
    total = mid_ref[...] + paired_ref[...] + swapped_ref[...]
    out_ref[...] = own_ref[0 : GY * ROWS, :] * (total * 0.25)


def theirs_kernel(home_ref, out_ref):
    _, inner = own_tile_inner()
    out_ref[0:4] = home_ref[pl.ds(jnp.where(inner, 0, 4), 4)]
    out_ref[4:8] = home_ref[pl.ds(jnp.where(inner, 12, 8), 4)]


def unpack_kernel(home_ref, got_ref, out_ref):
    core, inner = own_tile_inner()
    for slot in range(8):
        plane, col = slot // 4, slot % 4
        start = 2 * part_of(col, core)
        source = jnp.where(inner, 4 + slot, 12 * plane + col)
        for sub, value in ((core, home_ref[source]), (1 - core, got_ref[slot])):
            rows = pl.ds(pl.multiple_of((start + sub) * ROWS, ROWS), ROWS)
            out_ref[plane, rows, :] = value


def put_split(ref, v, pieces, stacked=False):
    axis = 0 if stacked else 1
    hi = jnp.concatenate([p[0] for p in pieces], axis=axis)
    lo = jnp.concatenate([p[1] for p in pieces], axis=axis)
    ref[v] = jnp.concatenate(
        [
            jnp.concatenate([hi, hi], axis=1),
            jnp.concatenate([lo, jnp.zeros_like(lo)], axis=1),
        ],
        axis=0,
    )


def base_rows(psf_ref, width, at):
    taps = psf_ref[...]
    taps = taps / jnp.sum(taps, axis=1, keepdims=True)
    lane = lax.broadcasted_iota(jnp.int32, (V, width), 1)
    back, straight = jnp.zeros((V, width), F32), jnp.zeros((V, width), F32)
    count = taps.shape[1]
    for t in range(count):
        tap = jnp.broadcast_to(taps[:, t : t + 1], (V, width))
        back = jnp.where(lane == at[0] + count - 1 - t, tap, back)
        straight = jnp.where(lane == at[1] + t, tap, straight)
    return back, straight


def taps_kernel(
    psf_rows_ref, psf_cols_ref, band_ref, pair_in_ref, near_in_ref, pair_back_ref, near_back_ref
):
    core, _ = own_tile_inner()
    col_bases = base_rows(psf_cols_ref, 2 * T, (177, 177))
    back_base, row_base = base_rows(psf_rows_ref, T, (T - 31, 1))

    def either(a, b):
        return tuple(jnp.where(core == 0, x, y) for x, y in zip(a, b))

    def turned(base, count, width):
        rows = jnp.broadcast_to(base, (count, base.shape[1]))
        return split(pltpu.roll(rows, 0, 1, stride=1, stride_axis=0)[:, :width])

    for v in range(V):
        for d in range(2):
            hi, lo = turned(col_bases[d][v : v + 1], 2 * T, T)
            band_ref[v, d, 0 : 2 * T, 0:T] = hi
            band_ref[v, d, 0 : 2 * T, T : 2 * T] = lo
            band_ref[v, d, 2 * T : 4 * T, 0:T] = hi
            band_ref[v, d, 2 * T : 4 * T, T : 2 * T] = jnp.zeros_like(lo)
        before, own, after = [
            turned(pltpu.roll(jnp.broadcast_to(row_base[v : v + 1], (8, T)), (T - ROWS * i) % T, 1)[0:1], ROWS, ROWS) for i in range(3)
        ]
        put_split(pair_in_ref, v, [either(before, after)])
        put_split(near_in_ref, v, [own, either(after, before)])
        before, own, after = [
            turned(pltpu.roll(jnp.broadcast_to(back_base[v : v + 1], (8, T)), ROWS * i, 1)[0:1], ROWS, ROWS) for i in range(3)
        ]
        put_split(pair_back_ref, v, [either(before, after)], stacked=True)
        put_split(near_back_ref, v, [own, either(after, before)], stacked=True)


def column_pass(pieces, band):
    lane = lax.broadcasted_iota(jnp.int32, (ROWS, T), 1)
    turned = [pltpu.roll(p, T // 2, 1) for p in pieces]
    zero = jnp.zeros((ROWS, T), F32)
    turned = [zero] + turned + [zero]
    moved = [
        jnp.where(lane < T // 2, turned[j], turned[j + 1]) for j in range(len(pieces) + 1)
    ]
    his, los = zip(*[split(m) for m in moved])
    done = []
    for half in range(2):
        windows = [
            jnp.concatenate([his[c], his[c + 1], los[c], los[c + 1]], axis=1)
            for c in range(half * len(pieces) // 2, (half + 1) * len(pieces) // 2)
        ]
        both = jnp.dot(jnp.concatenate(windows, axis=0), band, preferred_element_type=F32)
        done.append(both[:, :T] + both[:, T:])
    return jnp.concatenate(done, axis=0)


def column_tiles(ref, v):
    return [ref[v, :, T * c : T * c + T] for c in range(GY)]


def own_block(ref, half):
    return ref[0 : GY * ROWS, :].reshape(GY, ROWS, T)[:, 8 * half : 8 * half + 8, :]


def inner_lanes():
    lane = lax.broadcasted_iota(jnp.int32, (8, T), 1)
    return jnp.where(lane < T - 1, 1.0 / 16.0, 0.0).astype(F32)


def put_twice(b, x, est2, slope2):
    d = (pltpu.roll(x, T - 1, 2) - x) * inner_lanes()
    for copy in range(2):
        est2[b, GY * copy : GY * copy + GY] = x
        slope2[b, GY * copy : GY * copy + GY] = d


def code_of(meta_ref, v, b, c):
    return meta_ref[GY * (b // 2) + c, b % 2 * V + v].astype(F32)


def shift_of(meta_ref, v, b):
    return meta_ref[GY * (b // 2), 8 + b % 2 * V + v]


def gather(v, meta_ref, est2, slope2, view_u):
    count = est2.shape[0] // 2
    for src in range(count):
        parts = []
        for b in (2 * src, 2 * src + 1):
            shift = shift_of(meta_ref, v, b)
            x = est2[b, pl.ds(shift, GY)]
            d = slope2[b, pl.ds(shift, GY)]
            parts.append([x[c] + code_of(meta_ref, v, b, c) * d[c] for c in range(GY)])
        for c in range(GY):
            hi, lo = split(jnp.concatenate([parts[0][c], parts[1][c]], axis=0))
            cols = slice(T * c, T * c + T)
            view_u[v, ROWS * src : ROWS * src + ROWS, cols] = hi
            view_u[v, ROWS * (count + src) : ROWS * (count + src + 1), cols] = lo


def product(weights, values):
    both = jnp.dot(weights, values, preferred_element_type=F32)
    return both[: both.shape[0] // 2] + both[both.shape[0] // 2 :]


def rows_back(v, meta_ref, back_ref, again, total2):
    his, los = zip(*[split(again[v, ROWS * c : ROWS * c + ROWS, :]) for c in range(GY)])
    values = jnp.concatenate(
        [jnp.concatenate(his, axis=1), jnp.concatenate(los, axis=1)], axis=0
    )
    spread = product(back_ref[v], values)
    inner = inner_lanes()
    for b in range(total2.shape[0]):
        parts = []
        for c in range(GY):
            r = spread[8 * b : 8 * b + 8, T * c : T * c + T]
            g = r * inner
            g = pltpu.roll(g, 1, 1) - g
            parts.append(r + code_of(meta_ref, v, b, c) * g)
        total2[b, pl.ds(shift_of(meta_ref, v, b), GY)] += jnp.stack(parts)


def put_joined(ref, src, total2):
    for half in range(2):
        b = 2 * src + half
        y = total2[b, 0:GY] + total2[b, GY : 2 * GY]
        for c in range(GY):
            ref[ROWS * c + 8 * half : ROWS * c + 8 * half + 8, :] = y[c]


def for_views(stages):
    for stage in stages:
        for v in range(V):
            stage(v)


def front_kernel(meta_ref, own_ref, swapped_ref, near_in_ref, smooth_ref, est2, slope2, view_u):
    for src, ref in enumerate((own_ref, swapped_ref)):
        for half in range(2):
            put_twice(2 * src + half, own_block(ref, half), est2, slope2)

    def rows_in(v):
        smooth_ref[v] = product(near_in_ref[v], view_u[v])

    for_views((lambda v: gather(v, meta_ref, est2, slope2, view_u), rows_in))


def core_kernel(
    meta_ref, paired_ref, near_ref, arrived_ref, band_ref, pair_in_ref, pair_back_ref,
    pair_ref, again_ref, est2, slope2, view_u, total2, smooth, ratio,
):
    _, has_pair = here()
    for half in range(2):
        put_twice(half, own_block(paired_ref, half) * has_pair, est2, slope2)
    total2[...] = jnp.zeros(total2.shape, F32)

    def rows_in(v):
        smooth[v] = near_ref[v] + product(pair_in_ref[v], view_u[v])

    def cols_in(v):
        blurred = column_pass(column_tiles(smooth, v), band_ref[v, 0])
        for c in range(GY):
            ratio[v, :, T * c : T * c + T] = (
                arrived_ref[c, ROWS * (1 + v) : ROWS * (2 + v), :]
                / blurred[ROWS * c : ROWS * c + ROWS, :]
            )

    def cols_back(v):
        again_ref[v] = column_pass(column_tiles(ratio, v), band_ref[v, 1])

    for_views((
        lambda v: gather(v, meta_ref, est2, slope2, view_u),
        rows_in,
        cols_in,
        cols_back,
        lambda v: rows_back(v, meta_ref, pair_back_ref, again_ref, total2),
    ))
    put_joined(pair_ref, 0, total2)


def tail_kernel(meta_ref, again_ref, near_back_ref, mid_ref, swap_ref, total2):
    total2[...] = jnp.zeros(total2.shape, F32)
    for v in range(V):
        rows_back(v, meta_ref, near_back_ref, again_ref, total2)
    put_joined(mid_ref, 0, total2)
    put_joined(swap_ref, 1, total2)


def all_to_all(blocks):
    blocks = pltpu.with_memory_space_constraint(blocks, pltpu.VMEM)
    return lax.all_to_all(blocks, "gy", split_axis=0, concat_axis=0, tiled=True)


def body(estimate, views, psf_rows, psf_cols, shifts, codes):
    _, inner = own_tile_inner()
    taken = [
        pltpu.with_memory_space_constraint(a, pltpu.HBM)
        for a in (
            codes[:, :, 0],
            shifts,
            estimate.reshape(Z, 4, 2, ROWS, T),
            views.reshape(V, Z, 4, 2, ROWS, T),
        )
    ]
    room = [
        pltpu.SMEM((V, 2 * 8), jnp.int32),
        pltpu.SMEM((V, 2 * 8), jnp.int32),
        pltpu.VMEM((Z, 4, ROWS, T), F32),
        pltpu.VMEM((V, Z, 4, ROWS, T), BF16),
        pltpu.SemaphoreType.DMA((4,)),
    ]
    unit = jax.ShapeDtypeStruct((8, UNIT, T), F32)
    whole = jax.ShapeDtypeStruct((GY, UNIT, T), F32)
    send = pl.pallas_call(
        send_kernel,
        out_shape=unit,
        in_specs=[HBM] * 4,
        out_specs=VMEM,
        scratch_shapes=room,
        compiler_params=PARAMS,
        name="send",
    )(*taken)
    other = lax.ppermute(send, AXES, SWAP)
    kept = pl.pallas_call(
        keep_kernel,
        out_shape=whole,
        in_specs=[HBM] * 4,
        out_specs=VMEM,
        scratch_shapes=room,
        compiler_params=PARAMS,
        cost_estimate=COST,
        name="keep",
    )(*taken)
    joined = pl.pallas_call(
        join_kernel,
        out_shape=whole,
        in_specs=[VMEM, VMEM],
        out_specs=VMEM,
        input_output_aliases={0: 0},
        compiler_params=PARAMS,
        name="join",
    )(kept, other)

    band, pair_in, near_in, pair_back, near_back = pl.pallas_call(
        taps_kernel,
        out_shape=(
            jax.ShapeDtypeStruct((V, 2, 4 * T, 2 * T), BF16),
            jax.ShapeDtypeStruct((V, 2 * ROWS, 2 * ROWS), BF16),
            jax.ShapeDtypeStruct((V, 2 * ROWS, 4 * ROWS), BF16),
            jax.ShapeDtypeStruct((V, 2 * ROWS, 2 * ROWS), BF16),
            jax.ShapeDtypeStruct((V, 4 * ROWS, 2 * ROWS), BF16),
        ),
        in_specs=[VMEM, VMEM],
        out_specs=(VMEM,) * 5,
        compiler_params=PARAMS,
        name="taps",
    )(psf_rows, psf_cols)

    arrived = all_to_all(joined)
    lead = pl.pallas_call(
        lead_kernel,
        out_shape=jax.ShapeDtypeStruct((GY * ROWS + GY, T), F32),
        in_specs=[VMEM],
        out_specs=VMEM,
        compiler_params=PARAMS,
        name="lead",
    )(arrived)
    own_meta = lead[GY * ROWS :, :META]
    update = pl.pallas_call(
        update_kernel,
        out_shape=jax.ShapeDtypeStruct((GY * ROWS, T), F32),
        in_specs=[VMEM] * 4,
        out_specs=VMEM,
        compiler_params=PARAMS,
        name="update",
    )
    chunk = jax.ShapeDtypeStruct((GY * ROWS, T), F32)
    inside = pl.pallas_call(
        inside_kernel,
        out_shape=chunk,
        in_specs=[VMEM],
        out_specs=VMEM,
        compiler_params=PARAMS,
        cost_estimate=COST,
        name="inside",
    )
    doubled = [pltpu.VMEM((b, 2 * GY, 8, T), F32) for b in (2, 4)]
    front = pl.pallas_call(
        front_kernel,
        out_shape=jax.ShapeDtypeStruct((V, ROWS, GY * T), F32),
        in_specs=[SMEM] + [VMEM] * 3,
        out_specs=VMEM,
        scratch_shapes=[doubled[1], doubled[1], pltpu.VMEM((V, 4 * ROWS, GY * T), BF16)],
        compiler_params=PARAMS,
        name="front",
    )
    middle = pl.pallas_call(
        core_kernel,
        out_shape=(chunk, jax.ShapeDtypeStruct((V, GY * ROWS, T), F32)),
        in_specs=[SMEM] + [VMEM] * 6,
        out_specs=(VMEM, VMEM),
        scratch_shapes=[
            doubled[0],
            doubled[0],
            pltpu.VMEM((V, 2 * ROWS, GY * T), BF16),
            doubled[0],
            pltpu.VMEM((V, ROWS, GY * T), F32),
            pltpu.VMEM((V, ROWS, GY * T), F32),
        ],
        compiler_params=PARAMS,
        cost_estimate=COST,
        name="middle",
    )
    tail = pl.pallas_call(
        tail_kernel,
        out_shape=(chunk, chunk),
        in_specs=[SMEM] + [VMEM] * 2,
        out_specs=(VMEM, VMEM),
        scratch_shapes=[doubled[1]],
        compiler_params=PARAMS,
        cost_estimate=COST,
        name="tail",
    )
    own = lead
    for sweep in range(ITERS):
        paired = lax.ppermute(own, AXES, PAIR)
        swapped = lax.ppermute(own, AXES, SWAP)
        if sweep == 0:
            near_meta = jnp.concatenate(
                [own_meta, swapped[GY * ROWS :, :META]], axis=0
            ).astype(jnp.int32)
        near = front(near_meta, own, swapped, near_in)
        if sweep == 0:
            pair_meta = (paired[GY * ROWS :, :META] + 0.0 * near[0, :, :META]).astype(jnp.int32)
        pair, again = middle(pair_meta, paired, near, arrived, band, pair_in, pair_back)
        mid, swap = tail(near_meta, again, near_back)
        own = update(
            own, mid, inside(lax.ppermute(pair, AXES, PAIR)), lax.ppermute(swap, AXES, SWAP)
        )
    home = all_to_all(own.reshape(GY, ROWS, T))
    theirs = pl.pallas_call(
        theirs_kernel,
        out_shape=jax.ShapeDtypeStruct((8, ROWS, T), F32),
        in_specs=[VMEM],
        out_specs=VMEM,
        compiler_params=PARAMS,
        name="theirs",
    )(home)
    got = lax.ppermute(theirs, AXES, SWAP)
    return pl.pallas_call(
        unpack_kernel,
        out_shape=jax.ShapeDtypeStruct((Z, T, T), F32),
        in_specs=[VMEM, VMEM],
        out_specs=VMEM,
        compiler_params=PARAMS,
        name="unpack",
    )(home, got)


def solution(mesh):
    placed = (
        P(None, "gx", "gy"),
        P(None, None, "gx", "gy"),
        P(),
        P(),
        P(None, "gx"),
        P(None, "gx", "gy"),
    )
    return jax.shard_map(
        body, mesh=mesh, in_specs=placed, out_specs=P(None, "gx", "gy"), check_vma=False
    )
```

```python
import jax
import jax.numpy as jnp
from jax import lax
from jax.experimental import pallas as pl
from jax.experimental.pallas import tpu as pltpu
from jax.sharding import PartitionSpec as P

ITERS = 2
V = 4
Z = 2
T = 128
ROWS = 16
GY = 16
GX = 8
CHUNKS = 64
META = 16
UNIT = ROWS * (1 + V) + 8
AXES = ("gx", "gy")
F32 = jnp.float32
BF16 = jnp.bfloat16
VMEM = pl.BlockSpec(memory_space=pltpu.VMEM)
COST = pl.CostEstimate(flops=1_000_000_000, bytes_accessed=4_000_000, transcendentals=0)
HBM = pl.BlockSpec(memory_space=pltpu.HBM)
SMEM = pl.BlockSpec(memory_space=pltpu.SMEM)
PARAMS = pltpu.CompilerParams(vmem_limit_bytes=48 * 1024 * 1024)


def device_of(plane, chunk):
    core, block = chunk % 2, chunk // 2
    group, tile, part = block // 8, block % 8 // 4, block % 4
    inner = (tile == 0) == (group % 2 == 0)
    row = (1 if inner else 0, 2 if inner else 3)[plane]
    return (2 * group + core) * GY + 4 * row + (part if tile == 0 else 3 - part)


def both_ways(pairs):
    return [(a, b) for a, b in pairs] + [(b, a) for a, b in pairs]


SWAP = both_ways([(2 * x * GY + g, (2 * x + 1) * GY + g) for x in range(GX // 2) for g in range(GY)])
PAIR = both_ways(
    [
        (device_of(p, q), device_of(p, q + 1))
        for p in range(Z) for q in range(1, CHUNKS - 1, 2)
    ]
    + [(device_of(0, q), device_of(1, q)) for q in (0, CHUNKS - 1)]
)


CHIPS = [[(2 * x + c) * GY + g for c in range(2) for g in range(GY)] for x in range(GX // 2)]


def own_tile_inner():
    core, group = lax.axis_index("gx") % 2, lax.axis_index("gx") // 2
    return core, (core + group) % 2 == 0


def here():
    core, group = lax.axis_index("gx") % 2, lax.axis_index("gx") // 2
    row, col = lax.axis_index("gy") // 4, lax.axis_index("gy") % 4
    inner = jnp.where((row == 1) | (row == 2), 1, 0)
    first_tile = (inner + group) % 2 == 1
    block = 8 * group + jnp.where(first_tile, col, 7 - col)
    paired = jnp.where(core == 0, block > 0, block < CHUNKS // 2 - 1)
    return core, jnp.where(paired, 1.0, 0.0).astype(F32)


def part_of(col, core):
    return jnp.where(core == 0, col, 3 - col)


def split(x):
    hi = x.astype(BF16)
    return hi, (x - hi.astype(F32)).astype(BF16)


def pack(sub, slot_of, out_ref, codes_hbm, shifts_hbm, est_hbm, views_hbm, codes_ref, shifts_ref, est, views, sems):
    core, _ = own_tile_inner()
    copies = [
        pltpu.make_async_copy(codes_hbm, codes_ref, sems.at[0]),
        pltpu.make_async_copy(shifts_hbm, shifts_ref, sems.at[1]),
        pltpu.make_async_copy(est_hbm.at[:, :, sub], est, sems.at[2]),
        pltpu.make_async_copy(views_hbm.at[:, :, :, sub], views, sems.at[3]),
    ]
    for copy in copies:
        copy.start()
    for copy in copies:
        copy.wait()
    lane = lax.broadcasted_iota(jnp.int32, (8, T), 1)
    for slot in range(8):
        plane, part, at = slot // 4, part_of(slot % 4, core), slot_of(slot)
        block = 4 * part + 2 * sub
        meta = jnp.zeros((8, T), F32)
        for half in range(2):
            for v in range(V):
                code = codes_ref[v, block + half].astype(F32)
                shift = shifts_ref[v, block + half].astype(F32)
                meta = jnp.where(lane == half * V + v, code, meta)
                meta = jnp.where(lane == 8 + half * V + v, shift, meta)
        out_ref[at, 0:ROWS, :] = est[plane, part]
        for v in range(V):
            out_ref[at, pl.ds(ROWS * (1 + v), ROWS), :] = views[v, plane, part].astype(F32)
        out_ref[at, pl.ds(ROWS * (1 + V), 8), :] = meta


def halves(near):
    return jnp.where(near, 4, 0), jnp.where(near, 8, 12)


def send_kernel(codes_hbm, shifts_hbm, est_hbm, views_hbm, send_ref, *scratch):
    core, _ = own_tile_inner()
    pack(1 - core, lambda slot: slot, send_ref, codes_hbm, shifts_hbm, est_hbm, views_hbm, *scratch)


def keep_kernel(codes_hbm, shifts_hbm, est_hbm, views_hbm, out_ref, *scratch):
    core, inner = own_tile_inner()
    starts = halves(inner)
    pack(
        core, lambda slot: starts[slot // 4] + slot % 4, out_ref,
        codes_hbm, shifts_hbm, est_hbm, views_hbm, *scratch,
    )


def join_kernel(kept_ref, other_ref, out_ref):
    _, inner = own_tile_inner()
    for i, start in enumerate(halves(jnp.logical_not(inner))):
        out_ref[pl.ds(start, 4)] = other_ref[4 * i : 4 * i + 4]


def lead_kernel(arrived_ref, out_ref):
    for c in range(GY):
        out_ref[ROWS * c : ROWS * c + ROWS, :] = arrived_ref[c, 0:ROWS, :]
        meta = arrived_ref[c, ROWS * (1 + V) : ROWS * (1 + V) + 1, :]
        out_ref[GY * ROWS + c : GY * ROWS + c + 1, :] = meta


def inside_kernel(paired_ref, out_ref):
    _, has_pair = here()
    out_ref[...] = paired_ref[...] * has_pair


def update_kernel(own_ref, mid_ref, paired_ref, swapped_ref, out_ref):
    total = mid_ref[...] + paired_ref[...] + swapped_ref[...]
    out_ref[...] = own_ref[0 : GY * ROWS, :] * (total * 0.25)


def twice_kernel(own_ref, near_ref, paired_ref, swapped_ref, out_ref):
    for copy in range(2):
        update_kernel(
            own_ref, near_ref, paired_ref, swapped_ref,
            out_ref.at[GY * ROWS * copy : GY * ROWS * (copy + 1)],
        )


def unpack_kernel(home_ref, out_ref):
    core, inner = own_tile_inner()
    for slot in range(8):
        plane, col = slot // 4, slot % 4
        source = jnp.where(inner, 4 + slot, 12 * plane + col)
        for sub in range(2):
            at = (2 * part_of(col, core) + sub) * ROWS
            rows = pl.ds(pl.multiple_of(at, ROWS), ROWS)
            out_ref[plane, rows, :] = home_ref[GY * sub + source]


def put_split(ref, v, pieces, stacked=False):
    axis = 0 if stacked else 1
    hi = jnp.concatenate([p[0] for p in pieces], axis=axis)
    lo = jnp.concatenate([p[1] for p in pieces], axis=axis)
    ref[v] = jnp.concatenate(
        [
            jnp.concatenate([hi, hi], axis=1),
            jnp.concatenate([lo, jnp.zeros_like(lo)], axis=1),
        ],
        axis=0,
    )


def base_rows(psf_ref, width, at):
    taps = psf_ref[...]
    taps = taps / jnp.sum(taps, axis=1, keepdims=True)
    lane = lax.broadcasted_iota(jnp.int32, (V, width), 1)
    back, straight = jnp.zeros((V, width), F32), jnp.zeros((V, width), F32)
    count = taps.shape[1]
    for t in range(count):
        tap = jnp.broadcast_to(taps[:, t : t + 1], (V, width))
        back = jnp.where(lane == at[0] + count - 1 - t, tap, back)
        straight = jnp.where(lane == at[1] + t, tap, straight)
    return back, straight


def taps_kernel(
    psf_rows_ref, psf_cols_ref, band_ref, pair_in_ref, near_in_ref, pair_back_ref, near_back_ref
):
    core, _ = own_tile_inner()
    col_bases = base_rows(psf_cols_ref, 2 * T, (177, 177))
    back_base, row_base = base_rows(psf_rows_ref, T, (T - 31, 1))

    def either(a, b):
        return tuple(jnp.where(core == 0, x, y) for x, y in zip(a, b))

    def turned(base, count, width):
        rows = jnp.broadcast_to(base, (count, base.shape[1]))
        return split(pltpu.roll(rows, 0, 1, stride=1, stride_axis=0)[:, :width])

    for v in range(V):
        for d in range(2):
            hi, lo = turned(col_bases[d][v : v + 1], 2 * T, T)
            band_ref[v, d, 0 : 2 * T, 0:T] = hi
            band_ref[v, d, 0 : 2 * T, T : 2 * T] = lo
            band_ref[v, d, 2 * T : 4 * T, 0:T] = hi
            band_ref[v, d, 2 * T : 4 * T, T : 2 * T] = jnp.zeros_like(lo)
        before, own, after = [
            turned(pltpu.roll(jnp.broadcast_to(row_base[v : v + 1], (8, T)), (T - ROWS * i) % T, 1)[0:1], ROWS, ROWS) for i in range(3)
        ]
        put_split(pair_in_ref, v, [either(before, after)])
        put_split(near_in_ref, v, [own, either(after, before)])
        before, own, after = [
            turned(pltpu.roll(jnp.broadcast_to(back_base[v : v + 1], (8, T)), ROWS * i, 1)[0:1], ROWS, ROWS) for i in range(3)
        ]
        put_split(pair_back_ref, v, [either(before, after)], stacked=True)
        put_split(near_back_ref, v, [own, either(after, before)], stacked=True)


def column_pass(pieces, band):
    lane = lax.broadcasted_iota(jnp.int32, (ROWS, T), 1)
    turned = [pltpu.roll(p, T // 2, 1) for p in pieces]
    zero = jnp.zeros((ROWS, T), F32)
    turned = [zero] + turned + [zero]
    moved = [
        jnp.where(lane < T // 2, turned[j], turned[j + 1]) for j in range(len(pieces) + 1)
    ]
    his, los = zip(*[split(m) for m in moved])
    done = []
    for half in range(2):
        windows = [
            jnp.concatenate([his[c], his[c + 1], los[c], los[c + 1]], axis=1)
            for c in range(half * len(pieces) // 2, (half + 1) * len(pieces) // 2)
        ]
        both = jnp.dot(jnp.concatenate(windows, axis=0), band, preferred_element_type=F32)
        done.append(both[:, :T] + both[:, T:])
    return jnp.concatenate(done, axis=0)


def column_tiles(ref, v):
    return [ref[v, :, T * c : T * c + T] for c in range(GY)]


def own_block(ref, half):
    return ref[0 : GY * ROWS, :].reshape(GY, ROWS, T)[:, 8 * half : 8 * half + 8, :]


def inner_lanes():
    lane = lax.broadcasted_iota(jnp.int32, (8, T), 1)
    return jnp.where(lane < T - 1, 1.0 / 16.0, 0.0).astype(F32)


def put_twice(b, x, est2, slope2):
    d = (pltpu.roll(x, T - 1, 2) - x) * inner_lanes()
    for copy in range(2):
        est2[b, GY * copy : GY * copy + GY] = x
        slope2[b, GY * copy : GY * copy + GY] = d


def code_of(meta_ref, v, b, c):
    return meta_ref[GY * (b // 2) + c, b % 2 * V + v].astype(F32)


def shift_of(meta_ref, v, b):
    return meta_ref[GY * (b // 2), 8 + b % 2 * V + v]


def gather(v, meta_ref, est2, slope2, view_u):
    count = est2.shape[0] // 2
    for src in range(count):
        parts = []
        for b in (2 * src, 2 * src + 1):
            shift = shift_of(meta_ref, v, b)
            x = est2[b, pl.ds(shift, GY)]
            d = slope2[b, pl.ds(shift, GY)]
            parts.append([x[c] + code_of(meta_ref, v, b, c) * d[c] for c in range(GY)])
        for c in range(GY):
            hi, lo = split(jnp.concatenate([parts[0][c], parts[1][c]], axis=0))
            cols = slice(T * c, T * c + T)
            view_u[v, ROWS * src : ROWS * src + ROWS, cols] = hi
            view_u[v, ROWS * (count + src) : ROWS * (count + src + 1), cols] = lo


def product(weights, values):
    both = jnp.dot(weights, values, preferred_element_type=F32)
    return both[: both.shape[0] // 2] + both[both.shape[0] // 2 :]


def rows_back(v, meta_ref, back_ref, again, total2):
    his, los = zip(*[split(again[v, ROWS * c : ROWS * c + ROWS, :]) for c in range(GY)])
    values = jnp.concatenate(
        [jnp.concatenate(his, axis=1), jnp.concatenate(los, axis=1)], axis=0
    )
    spread = product(back_ref[v], values)
    inner = inner_lanes()
    for b in range(total2.shape[0]):
        parts = []
        for c in range(GY):
            r = spread[8 * b : 8 * b + 8, T * c : T * c + T]
            g = r * inner
            g = pltpu.roll(g, 1, 1) - g
            parts.append(r + code_of(meta_ref, v, b, c) * g)
        total2[b, pl.ds(shift_of(meta_ref, v, b), GY)] += jnp.stack(parts)


def put_joined(ref, src, total2):
    for half in range(2):
        b = 2 * src + half
        y = total2[b, 0:GY] + total2[b, GY : 2 * GY]
        for c in range(GY):
            ref[ROWS * c + 8 * half : ROWS * c + 8 * half + 8, :] = y[c]


def for_views(stages):
    for stage in stages:
        for v in range(V):
            stage(v)


def front_kernel(meta_ref, own_ref, swapped_ref, near_in_ref, smooth_ref, est2, slope2, view_u):
    for src, ref in enumerate((own_ref, swapped_ref)):
        for half in range(2):
            put_twice(2 * src + half, own_block(ref, half), est2, slope2)

    def rows_in(v):
        smooth_ref[v] = product(near_in_ref[v], view_u[v])

    for_views((lambda v: gather(v, meta_ref, est2, slope2, view_u), rows_in))


def core_kernel(
    meta_ref, paired_ref, near_ref, arrived_ref, band_ref, pair_in_ref, pair_back_ref,
    pair_ref, again_ref, est2, slope2, view_u, total2, smooth, ratio,
):
    _, has_pair = here()
    for half in range(2):
        put_twice(half, own_block(paired_ref, half) * has_pair, est2, slope2)
    total2[...] = jnp.zeros(total2.shape, F32)

    def rows_in(v):
        smooth[v] = near_ref[v] + product(pair_in_ref[v], view_u[v])

    def cols_in(v):
        blurred = column_pass(column_tiles(smooth, v), band_ref[v, 0])
        for c in range(GY):
            ratio[v, :, T * c : T * c + T] = (
                arrived_ref[c, ROWS * (1 + v) : ROWS * (2 + v), :]
                / blurred[ROWS * c : ROWS * c + ROWS, :]
            )

    def cols_back(v):
        again_ref[v] = column_pass(column_tiles(ratio, v), band_ref[v, 1])

    for_views((
        lambda v: gather(v, meta_ref, est2, slope2, view_u),
        rows_in,
        cols_in,
        cols_back,
        lambda v: rows_back(v, meta_ref, pair_back_ref, again_ref, total2),
    ))
    put_joined(pair_ref, 0, total2)


def tail_kernel(meta_ref, again_ref, near_back_ref, mid_ref, swap_ref, total2):
    total2[...] = jnp.zeros(total2.shape, F32)
    for v in range(V):
        rows_back(v, meta_ref, near_back_ref, again_ref, total2)
    put_joined(mid_ref, 0, total2)
    put_joined(swap_ref, 1, total2)


def all_to_all(blocks):
    blocks = pltpu.with_memory_space_constraint(blocks, pltpu.VMEM)
    return lax.all_to_all(blocks, "gy", split_axis=0, concat_axis=0, tiled=True)


def body(estimate, views, psf_rows, psf_cols, shifts, codes):
    _, inner = own_tile_inner()
    taken = [
        pltpu.with_memory_space_constraint(a, pltpu.HBM)
        for a in (
            codes[:, :, 0],
            shifts,
            estimate.reshape(Z, 4, 2, ROWS, T),
            views.reshape(V, Z, 4, 2, ROWS, T),
        )
    ]
    room = [
        pltpu.SMEM((V, 2 * 8), jnp.int32),
        pltpu.SMEM((V, 2 * 8), jnp.int32),
        pltpu.VMEM((Z, 4, ROWS, T), F32),
        pltpu.VMEM((V, Z, 4, ROWS, T), BF16),
        pltpu.SemaphoreType.DMA((4,)),
    ]
    unit = jax.ShapeDtypeStruct((8, UNIT, T), F32)
    whole = jax.ShapeDtypeStruct((GY, UNIT, T), F32)
    send = pl.pallas_call(
        send_kernel,
        out_shape=unit,
        in_specs=[HBM] * 4,
        out_specs=VMEM,
        scratch_shapes=room,
        compiler_params=PARAMS,
        name="send",
    )(*taken)
    other = lax.ppermute(send, AXES, SWAP)
    kept = pl.pallas_call(
        keep_kernel,
        out_shape=whole,
        in_specs=[HBM] * 4,
        out_specs=VMEM,
        scratch_shapes=room,
        compiler_params=PARAMS,
        cost_estimate=COST,
        name="keep",
    )(*taken)
    joined = pl.pallas_call(
        join_kernel,
        out_shape=whole,
        in_specs=[VMEM, VMEM],
        out_specs=VMEM,
        input_output_aliases={0: 0},
        compiler_params=PARAMS,
        name="join",
    )(kept, other)

    band, pair_in, near_in, pair_back, near_back = pl.pallas_call(
        taps_kernel,
        out_shape=(
            jax.ShapeDtypeStruct((V, 2, 4 * T, 2 * T), BF16),
            jax.ShapeDtypeStruct((V, 2 * ROWS, 2 * ROWS), BF16),
            jax.ShapeDtypeStruct((V, 2 * ROWS, 4 * ROWS), BF16),
            jax.ShapeDtypeStruct((V, 2 * ROWS, 2 * ROWS), BF16),
            jax.ShapeDtypeStruct((V, 4 * ROWS, 2 * ROWS), BF16),
        ),
        in_specs=[VMEM, VMEM],
        out_specs=(VMEM,) * 5,
        compiler_params=PARAMS,
        name="taps",
    )(psf_rows, psf_cols)

    arrived = all_to_all(joined)
    lead = pl.pallas_call(
        lead_kernel,
        out_shape=jax.ShapeDtypeStruct((GY * ROWS + GY, T), F32),
        in_specs=[VMEM],
        out_specs=VMEM,
        compiler_params=PARAMS,
        name="lead",
    )(arrived)
    own_meta = lead[GY * ROWS :, :META]
    update, update_twice = [
        pl.pallas_call(
            kernel,
            out_shape=jax.ShapeDtypeStruct((count * GY * ROWS, T), F32),
            in_specs=[VMEM] * 4,
            out_specs=VMEM,
            compiler_params=PARAMS,
            name=name,
        )
        for kernel, count, name in ((update_kernel, 1, "update"), (twice_kernel, 2, "last"))
    ]
    chunk = jax.ShapeDtypeStruct((GY * ROWS, T), F32)
    inside = pl.pallas_call(
        inside_kernel,
        out_shape=chunk,
        in_specs=[VMEM],
        out_specs=VMEM,
        compiler_params=PARAMS,
        cost_estimate=COST,
        name="inside",
    )
    doubled = [pltpu.VMEM((b, 2 * GY, 8, T), F32) for b in (2, 4)]
    front = pl.pallas_call(
        front_kernel,
        out_shape=jax.ShapeDtypeStruct((V, ROWS, GY * T), F32),
        in_specs=[SMEM] + [VMEM] * 3,
        out_specs=VMEM,
        scratch_shapes=[doubled[1], doubled[1], pltpu.VMEM((V, 4 * ROWS, GY * T), BF16)],
        compiler_params=PARAMS,
        name="front",
    )
    middle = pl.pallas_call(
        core_kernel,
        out_shape=(chunk, jax.ShapeDtypeStruct((V, GY * ROWS, T), F32)),
        in_specs=[SMEM] + [VMEM] * 6,
        out_specs=(VMEM, VMEM),
        scratch_shapes=[
            doubled[0],
            doubled[0],
            pltpu.VMEM((V, 2 * ROWS, GY * T), BF16),
            doubled[0],
            pltpu.VMEM((V, ROWS, GY * T), F32),
            pltpu.VMEM((V, ROWS, GY * T), F32),
        ],
        compiler_params=PARAMS,
        cost_estimate=COST,
        name="middle",
    )
    tail = pl.pallas_call(
        tail_kernel,
        out_shape=(chunk, chunk),
        in_specs=[SMEM] + [VMEM] * 2,
        out_specs=(VMEM, VMEM),
        scratch_shapes=[doubled[1]],
        compiler_params=PARAMS,
        cost_estimate=COST,
        name="tail",
    )
    own = lead
    for sweep in range(ITERS):
        paired = lax.ppermute(own, AXES, PAIR)
        swapped = lax.ppermute(own, AXES, SWAP)
        if sweep == 0:
            near_meta = jnp.concatenate(
                [own_meta, swapped[GY * ROWS :, :META]], axis=0
            ).astype(jnp.int32)
        near = front(near_meta, own, swapped, near_in)
        if sweep == 0:
            pair_meta = (paired[GY * ROWS :, :META] + 0.0 * near[0, :, :META]).astype(jnp.int32)
        pair, again = middle(pair_meta, paired, near, arrived, band, pair_in, pair_back)
        mid, swap = tail(near_meta, again, near_back)
        own = (update if sweep < ITERS - 1 else update_twice)(
            own, mid, inside(lax.ppermute(pair, AXES, PAIR)), lax.ppermute(swap, AXES, SWAP)
        )
    blocks = pltpu.with_memory_space_constraint(own.reshape(2 * GY, ROWS, T), pltpu.VMEM)
    home = lax.all_to_all(
        blocks, AXES, split_axis=0, concat_axis=0, tiled=True, axis_index_groups=CHIPS
    )
    return pl.pallas_call(
        unpack_kernel,
        out_shape=jax.ShapeDtypeStruct((Z, T, T), F32),
        in_specs=[VMEM],
        out_specs=VMEM,
        compiler_params=PARAMS,
        name="unpack",
    )(home)


def solution(mesh):
    placed = (
        P(None, "gx", "gy"),
        P(None, None, "gx", "gy"),
        P(),
        P(),
        P(None, "gx"),
        P(None, "gx", "gy"),
    )
    return jax.shard_map(
        body, mesh=mesh, in_specs=placed, out_specs=P(None, "gx", "gy"), check_vma=False
    )
```

```python
import jax
import jax.numpy as jnp
from jax import lax
from jax.experimental import pallas as pl
from jax.experimental.pallas import tpu as pltpu
from jax.sharding import PartitionSpec as P

ITERS = 2
V = 4
Z = 2
T = 128
ROWS = 16
GY = 16
GX = 8
CHUNKS = 64
META = 16
UNIT = ROWS * (1 + V) + 8
AXES = ("gx", "gy")
F32 = jnp.float32
BF16 = jnp.bfloat16
VMEM = pl.BlockSpec(memory_space=pltpu.VMEM)
COST = pl.CostEstimate(flops=1_000_000_000, bytes_accessed=4_000_000, transcendentals=0)
HBM = pl.BlockSpec(memory_space=pltpu.HBM)
SMEM = pl.BlockSpec(memory_space=pltpu.SMEM)
PARAMS = pltpu.CompilerParams(vmem_limit_bytes=48 * 1024 * 1024)


def device_of(plane, chunk):
    core, block = chunk % 2, chunk // 2
    group, tile, part = block // 8, block % 8 // 4, block % 4
    inner = (tile == 0) == (group % 2 == 0)
    row = (1 if inner else 0, 2 if inner else 3)[plane]
    return (2 * group + core) * GY + 4 * row + (part if tile == 0 else 3 - part)


def both_ways(pairs):
    return [(a, b) for a, b in pairs] + [(b, a) for a, b in pairs]


SWAP = both_ways([(2 * x * GY + g, (2 * x + 1) * GY + g) for x in range(GX // 2) for g in range(GY)])
PAIR = both_ways(
    [
        (device_of(p, q), device_of(p, q + 1))
        for p in range(Z) for q in range(1, CHUNKS - 1, 2)
    ]
    + [(device_of(0, q), device_of(1, q)) for q in (0, CHUNKS - 1)]
)


CHIPS = [[(2 * x + c) * GY + g for c in range(2) for g in range(GY)] for x in range(GX // 2)]


def own_tile_inner():
    core, group = lax.axis_index("gx") % 2, lax.axis_index("gx") // 2
    return core, (core + group) % 2 == 0


def here():
    core, group = lax.axis_index("gx") % 2, lax.axis_index("gx") // 2
    row, col = lax.axis_index("gy") // 4, lax.axis_index("gy") % 4
    inner = jnp.where((row == 1) | (row == 2), 1, 0)
    first_tile = (inner + group) % 2 == 1
    block = 8 * group + jnp.where(first_tile, col, 7 - col)
    paired = jnp.where(core == 0, block > 0, block < CHUNKS // 2 - 1)
    return core, jnp.where(paired, 1.0, 0.0).astype(F32)


def part_of(col, core):
    return jnp.where(core == 0, col, 3 - col)


def split(x):
    hi = x.astype(BF16)
    return hi, (x - hi.astype(F32)).astype(BF16)


def pack(sub, slot_of, out_ref, codes_hbm, shifts_hbm, est_hbm, views_hbm, codes_ref, shifts_ref, est, views, sems):
    core, _ = own_tile_inner()
    planes = [
        pltpu.make_async_copy(views_hbm.at[:, p, :, sub], views.at[:, p], sems.at[3 + p])
        for p in range(Z)
    ]
    copies = [
        pltpu.make_async_copy(codes_hbm, codes_ref, sems.at[0]),
        pltpu.make_async_copy(shifts_hbm, shifts_ref, sems.at[1]),
        pltpu.make_async_copy(est_hbm.at[:, :, sub], est, sems.at[2]),
    ]
    for copy in copies + planes:
        copy.start()
    for copy in copies:
        copy.wait()
    lane = lax.broadcasted_iota(jnp.int32, (8, T), 1)
    for slot in range(8):
        plane, part, at = slot // 4, part_of(slot % 4, core), slot_of(slot)
        block = 4 * part + 2 * sub
        meta = jnp.zeros((8, T), F32)
        for half in range(2):
            for v in range(V):
                code = codes_ref[v, block + half].astype(F32)
                shift = shifts_ref[v, block + half].astype(F32)
                meta = jnp.where(lane == half * V + v, code, meta)
                meta = jnp.where(lane == 8 + half * V + v, shift, meta)
        out_ref[at, 0:ROWS, :] = est[plane, part]
        out_ref[at, pl.ds(ROWS * (1 + V), 8), :] = meta
    for slot in range(8):
        plane, part, at = slot // 4, part_of(slot % 4, core), slot_of(slot)
        if slot % 4 == 0:
            planes[plane].wait()
        for v in range(V):
            out_ref[at, pl.ds(ROWS * (1 + v), ROWS), :] = views[v, plane, part].astype(F32)


def halves(near):
    return jnp.where(near, 4, 0), jnp.where(near, 8, 12)


def send_kernel(codes_hbm, shifts_hbm, est_hbm, views_hbm, send_ref, *scratch):
    core, _ = own_tile_inner()
    pack(1 - core, lambda slot: slot, send_ref, codes_hbm, shifts_hbm, est_hbm, views_hbm, *scratch)


def keep_kernel(codes_hbm, shifts_hbm, est_hbm, views_hbm, out_ref, *scratch):
    core, inner = own_tile_inner()
    starts = halves(inner)
    pack(
        core, lambda slot: starts[slot // 4] + slot % 4, out_ref,
        codes_hbm, shifts_hbm, est_hbm, views_hbm, *scratch,
    )


def join_kernel(kept_ref, other_ref, out_ref):
    _, inner = own_tile_inner()
    for i, start in enumerate(halves(jnp.logical_not(inner))):
        out_ref[pl.ds(start, 4)] = other_ref[4 * i : 4 * i + 4]


def lead_kernel(arrived_ref, out_ref):
    for c in range(GY):
        out_ref[ROWS * c : ROWS * c + ROWS, :] = arrived_ref[c, 0:ROWS, :]
        meta = arrived_ref[c, ROWS * (1 + V) : ROWS * (1 + V) + 1, :]
        out_ref[GY * ROWS + c : GY * ROWS + c + 1, :] = meta


def inside_kernel(paired_ref, out_ref):
    _, has_pair = here()
    out_ref[...] = paired_ref[...] * has_pair


def update_kernel(own_ref, mid_ref, paired_ref, swapped_ref, out_ref):
    total = mid_ref[...] + paired_ref[...] + swapped_ref[...]
    out_ref[...] = own_ref[0 : GY * ROWS, :] * (total * 0.25)


def twice_kernel(own_ref, near_ref, paired_ref, swapped_ref, out_ref):
    for copy in range(2):
        update_kernel(
            own_ref, near_ref, paired_ref, swapped_ref,
            out_ref.at[GY * ROWS * copy : GY * ROWS * (copy + 1)],
        )


def unpack_kernel(home_ref, out_ref):
    core, inner = own_tile_inner()
    for slot in range(8):
        plane, col = slot // 4, slot % 4
        source = jnp.where(inner, 4 + slot, 12 * plane + col)
        for sub in range(2):
            at = (2 * part_of(col, core) + sub) * ROWS
            rows = pl.ds(pl.multiple_of(at, ROWS), ROWS)
            out_ref[plane, rows, :] = home_ref[GY * sub + source]


def put_split(ref, v, pieces, stacked=False):
    axis = 0 if stacked else 1
    hi = jnp.concatenate([p[0] for p in pieces], axis=axis)
    lo = jnp.concatenate([p[1] for p in pieces], axis=axis)
    ref[v] = jnp.concatenate(
        [
            jnp.concatenate([hi, hi], axis=1),
            jnp.concatenate([lo, jnp.zeros_like(lo)], axis=1),
        ],
        axis=0,
    )


def base_rows(psf_ref, width, at):
    taps = psf_ref[...]
    taps = taps / jnp.sum(taps, axis=1, keepdims=True)
    lane = lax.broadcasted_iota(jnp.int32, (V, width), 1)
    back, straight = jnp.zeros((V, width), F32), jnp.zeros((V, width), F32)
    count = taps.shape[1]
    for t in range(count):
        tap = jnp.broadcast_to(taps[:, t : t + 1], (V, width))
        back = jnp.where(lane == at[0] + count - 1 - t, tap, back)
        straight = jnp.where(lane == at[1] + t, tap, straight)
    return back, straight


def taps_kernel(
    psf_rows_ref, psf_cols_ref, band_ref, pair_in_ref, near_in_ref, pair_back_ref, near_back_ref
):
    core, _ = own_tile_inner()
    col_bases = base_rows(psf_cols_ref, 2 * T, (177, 177))
    back_base, row_base = base_rows(psf_rows_ref, T, (T - 31, 1))

    def either(a, b):
        return tuple(jnp.where(core == 0, x, y) for x, y in zip(a, b))

    def turned(base, count, width):
        rows = jnp.broadcast_to(base, (count, base.shape[1]))
        return split(pltpu.roll(rows, 0, 1, stride=1, stride_axis=0)[:, :width])

    for v in range(V):
        for d in range(2):
            hi, lo = turned(col_bases[d][v : v + 1], 2 * T, T)
            band_ref[v, d, 0 : 2 * T, 0:T] = hi
            band_ref[v, d, 0 : 2 * T, T : 2 * T] = lo
            band_ref[v, d, 2 * T : 4 * T, 0:T] = hi
            band_ref[v, d, 2 * T : 4 * T, T : 2 * T] = jnp.zeros_like(lo)
        before, own, after = [
            turned(pltpu.roll(jnp.broadcast_to(row_base[v : v + 1], (8, T)), (T - ROWS * i) % T, 1)[0:1], ROWS, ROWS) for i in range(3)
        ]
        put_split(pair_in_ref, v, [either(before, after)])
        put_split(near_in_ref, v, [own, either(after, before)])
        before, own, after = [
            turned(pltpu.roll(jnp.broadcast_to(back_base[v : v + 1], (8, T)), ROWS * i, 1)[0:1], ROWS, ROWS) for i in range(3)
        ]
        put_split(pair_back_ref, v, [either(before, after)], stacked=True)
        put_split(near_back_ref, v, [own, either(after, before)], stacked=True)


def column_pass(pieces, band):
    lane = lax.broadcasted_iota(jnp.int32, (ROWS, T), 1)
    turned = [pltpu.roll(p, T // 2, 1) for p in pieces]
    zero = jnp.zeros((ROWS, T), F32)
    turned = [zero] + turned + [zero]
    moved = [
        jnp.where(lane < T // 2, turned[j], turned[j + 1]) for j in range(len(pieces) + 1)
    ]
    his, los = zip(*[split(m) for m in moved])
    done = []
    for half in range(2):
        windows = [
            jnp.concatenate([his[c], his[c + 1], los[c], los[c + 1]], axis=1)
            for c in range(half * len(pieces) // 2, (half + 1) * len(pieces) // 2)
        ]
        both = jnp.dot(jnp.concatenate(windows, axis=0), band, preferred_element_type=F32)
        done.append(both[:, :T] + both[:, T:])
    return jnp.concatenate(done, axis=0)


def column_tiles(ref, v):
    return [ref[v, :, T * c : T * c + T] for c in range(GY)]


def own_block(ref, half):
    return ref[0 : GY * ROWS, :].reshape(GY, ROWS, T)[:, 8 * half : 8 * half + 8, :]


def inner_lanes():
    lane = lax.broadcasted_iota(jnp.int32, (8, T), 1)
    return jnp.where(lane < T - 1, 1.0 / 16.0, 0.0).astype(F32)


def put_twice(b, x, est2, slope2):
    d = (pltpu.roll(x, T - 1, 2) - x) * inner_lanes()
    for copy in range(2):
        est2[b, GY * copy : GY * copy + GY] = x
        slope2[b, GY * copy : GY * copy + GY] = d


def code_of(meta_ref, v, b, c):
    return meta_ref[GY * (b // 2) + c, b % 2 * V + v].astype(F32)


def shift_of(meta_ref, v, b):
    return meta_ref[GY * (b // 2), 8 + b % 2 * V + v]


def gather(v, meta_ref, est2, slope2, view_u):
    count = est2.shape[0] // 2
    for src in range(count):
        parts = []
        for b in (2 * src, 2 * src + 1):
            shift = shift_of(meta_ref, v, b)
            x = est2[b, pl.ds(shift, GY)]
            d = slope2[b, pl.ds(shift, GY)]
            parts.append([x[c] + code_of(meta_ref, v, b, c) * d[c] for c in range(GY)])
        for c in range(GY):
            hi, lo = split(jnp.concatenate([parts[0][c], parts[1][c]], axis=0))
            cols = slice(T * c, T * c + T)
            view_u[v, ROWS * src : ROWS * src + ROWS, cols] = hi
            view_u[v, ROWS * (count + src) : ROWS * (count + src + 1), cols] = lo


def product(weights, values):
    both = jnp.dot(weights, values, preferred_element_type=F32)
    return both[: both.shape[0] // 2] + both[both.shape[0] // 2 :]


def rows_back(v, meta_ref, back_ref, again, total2):
    his, los = zip(*[split(again[v, ROWS * c : ROWS * c + ROWS, :]) for c in range(GY)])
    values = jnp.concatenate(
        [jnp.concatenate(his, axis=1), jnp.concatenate(los, axis=1)], axis=0
    )
    spread = product(back_ref[v], values)
    inner = inner_lanes()
    for b in range(total2.shape[0]):
        parts = []
        for c in range(GY):
            r = spread[8 * b : 8 * b + 8, T * c : T * c + T]
            g = r * inner
            g = pltpu.roll(g, 1, 1) - g
            parts.append(r + code_of(meta_ref, v, b, c) * g)
        total2[b, pl.ds(shift_of(meta_ref, v, b), GY)] += jnp.stack(parts)


def put_joined(ref, src, total2):
    for half in range(2):
        b = 2 * src + half
        y = total2[b, 0:GY] + total2[b, GY : 2 * GY]
        for c in range(GY):
            ref[ROWS * c + 8 * half : ROWS * c + 8 * half + 8, :] = y[c]


def for_views(stages):
    for stage in stages:
        for v in range(V):
            stage(v)


def front_kernel(meta_ref, own_ref, swapped_ref, near_in_ref, smooth_ref, est2, slope2, view_u):
    for src, ref in enumerate((own_ref, swapped_ref)):
        for half in range(2):
            put_twice(2 * src + half, own_block(ref, half), est2, slope2)

    def rows_in(v):
        smooth_ref[v] = product(near_in_ref[v], view_u[v])

    for_views((lambda v: gather(v, meta_ref, est2, slope2, view_u), rows_in))


def core_kernel(
    meta_ref, paired_ref, near_ref, arrived_ref, band_ref, pair_in_ref, pair_back_ref,
    pair_ref, again_ref, est2, slope2, view_u, total2, smooth, ratio,
):
    _, has_pair = here()
    for half in range(2):
        put_twice(half, own_block(paired_ref, half) * has_pair, est2, slope2)
    total2[...] = jnp.zeros(total2.shape, F32)

    def rows_in(v):
        smooth[v] = near_ref[v] + product(pair_in_ref[v], view_u[v])

    def cols_in(v):
        blurred = column_pass(column_tiles(smooth, v), band_ref[v, 0])
        for c in range(GY):
            ratio[v, :, T * c : T * c + T] = (
                arrived_ref[c, ROWS * (1 + v) : ROWS * (2 + v), :]
                / blurred[ROWS * c : ROWS * c + ROWS, :]
            )

    def cols_back(v):
        again_ref[v] = column_pass(column_tiles(ratio, v), band_ref[v, 1])

    for_views((
        lambda v: gather(v, meta_ref, est2, slope2, view_u),
        rows_in,
        cols_in,
        cols_back,
        lambda v: rows_back(v, meta_ref, pair_back_ref, again_ref, total2),
    ))
    put_joined(pair_ref, 0, total2)


def tail_kernel(meta_ref, again_ref, near_back_ref, mid_ref, swap_ref, total2):
    total2[...] = jnp.zeros(total2.shape, F32)
    for v in range(V):
        rows_back(v, meta_ref, near_back_ref, again_ref, total2)
    put_joined(mid_ref, 0, total2)
    put_joined(swap_ref, 1, total2)


def all_to_all(blocks):
    blocks = pltpu.with_memory_space_constraint(blocks, pltpu.VMEM)
    return lax.all_to_all(blocks, "gy", split_axis=0, concat_axis=0, tiled=True)


def body(estimate, views, psf_rows, psf_cols, shifts, codes):
    _, inner = own_tile_inner()
    taken = [
        pltpu.with_memory_space_constraint(a, pltpu.HBM)
        for a in (
            codes[:, :, 0],
            shifts,
            estimate.reshape(Z, 4, 2, ROWS, T),
            views.reshape(V, Z, 4, 2, ROWS, T),
        )
    ]
    room = [
        pltpu.SMEM((V, 2 * 8), jnp.int32),
        pltpu.SMEM((V, 2 * 8), jnp.int32),
        pltpu.VMEM((Z, 4, ROWS, T), F32),
        pltpu.VMEM((V, Z, 4, ROWS, T), BF16),
        pltpu.SemaphoreType.DMA((5,)),
    ]
    unit = jax.ShapeDtypeStruct((8, UNIT, T), F32)
    whole = jax.ShapeDtypeStruct((GY, UNIT, T), F32)
    send = pl.pallas_call(
        send_kernel,
        out_shape=unit,
        in_specs=[HBM] * 4,
        out_specs=VMEM,
        scratch_shapes=room,
        compiler_params=PARAMS,
        name="send",
    )(*taken)
    other = lax.ppermute(send, AXES, SWAP)
    kept = pl.pallas_call(
        keep_kernel,
        out_shape=whole,
        in_specs=[HBM] * 4,
        out_specs=VMEM,
        scratch_shapes=room,
        compiler_params=PARAMS,
        cost_estimate=COST,
        name="keep",
    )(*taken)
    joined = pl.pallas_call(
        join_kernel,
        out_shape=whole,
        in_specs=[VMEM, VMEM],
        out_specs=VMEM,
        input_output_aliases={0: 0},
        compiler_params=PARAMS,
        name="join",
    )(kept, other)

    band, pair_in, near_in, pair_back, near_back = pl.pallas_call(
        taps_kernel,
        out_shape=(
            jax.ShapeDtypeStruct((V, 2, 4 * T, 2 * T), BF16),
            jax.ShapeDtypeStruct((V, 2 * ROWS, 2 * ROWS), BF16),
            jax.ShapeDtypeStruct((V, 2 * ROWS, 4 * ROWS), BF16),
            jax.ShapeDtypeStruct((V, 2 * ROWS, 2 * ROWS), BF16),
            jax.ShapeDtypeStruct((V, 4 * ROWS, 2 * ROWS), BF16),
        ),
        in_specs=[VMEM, VMEM],
        out_specs=(VMEM,) * 5,
        compiler_params=PARAMS,
        name="taps",
    )(psf_rows, psf_cols)

    arrived = all_to_all(joined)
    lead = pl.pallas_call(
        lead_kernel,
        out_shape=jax.ShapeDtypeStruct((GY * ROWS + GY, T), F32),
        in_specs=[VMEM],
        out_specs=VMEM,
        compiler_params=PARAMS,
        name="lead",
    )(arrived)
    own_meta = lead[GY * ROWS :, :META]
    update, update_twice = [
        pl.pallas_call(
            kernel,
            out_shape=jax.ShapeDtypeStruct((count * GY * ROWS, T), F32),
            in_specs=[VMEM] * 4,
            out_specs=VMEM,
            compiler_params=PARAMS,
            name=name,
        )
        for kernel, count, name in ((update_kernel, 1, "update"), (twice_kernel, 2, "last"))
    ]
    chunk = jax.ShapeDtypeStruct((GY * ROWS, T), F32)
    inside = pl.pallas_call(
        inside_kernel,
        out_shape=chunk,
        in_specs=[VMEM],
        out_specs=VMEM,
        compiler_params=PARAMS,
        cost_estimate=COST,
        name="inside",
    )
    doubled = [pltpu.VMEM((b, 2 * GY, 8, T), F32) for b in (2, 4)]
    front = pl.pallas_call(
        front_kernel,
        out_shape=jax.ShapeDtypeStruct((V, ROWS, GY * T), F32),
        in_specs=[SMEM] + [VMEM] * 3,
        out_specs=VMEM,
        scratch_shapes=[doubled[1], doubled[1], pltpu.VMEM((V, 4 * ROWS, GY * T), BF16)],
        compiler_params=PARAMS,
        name="front",
    )
    middle = pl.pallas_call(
        core_kernel,
        out_shape=(chunk, jax.ShapeDtypeStruct((V, GY * ROWS, T), F32)),
        in_specs=[SMEM] + [VMEM] * 6,
        out_specs=(VMEM, VMEM),
        scratch_shapes=[
            doubled[0],
            doubled[0],
            pltpu.VMEM((V, 2 * ROWS, GY * T), BF16),
            doubled[0],
            pltpu.VMEM((V, ROWS, GY * T), F32),
            pltpu.VMEM((V, ROWS, GY * T), F32),
        ],
        compiler_params=PARAMS,
        cost_estimate=COST,
        name="middle",
    )
    tail = pl.pallas_call(
        tail_kernel,
        out_shape=(chunk, chunk),
        in_specs=[SMEM] + [VMEM] * 2,
        out_specs=(VMEM, VMEM),
        scratch_shapes=[doubled[1]],
        compiler_params=PARAMS,
        cost_estimate=COST,
        name="tail",
    )
    own = lead
    for sweep in range(ITERS):
        paired = lax.ppermute(own, AXES, PAIR)
        swapped = lax.ppermute(own, AXES, SWAP)
        if sweep == 0:
            near_meta = jnp.concatenate(
                [own_meta, swapped[GY * ROWS :, :META]], axis=0
            ).astype(jnp.int32)
        near = front(near_meta, own, swapped, near_in)
        if sweep == 0:
            pair_meta = (paired[GY * ROWS :, :META] + 0.0 * near[0, :, :META]).astype(jnp.int32)
        pair, again = middle(pair_meta, paired, near, arrived, band, pair_in, pair_back)
        mid, swap = tail(near_meta, again, near_back)
        own = (update if sweep < ITERS - 1 else update_twice)(
            own, mid, inside(lax.ppermute(pair, AXES, PAIR)), lax.ppermute(swap, AXES, SWAP)
        )
    blocks = pltpu.with_memory_space_constraint(own.reshape(2 * GY, ROWS, T), pltpu.VMEM)
    home = lax.all_to_all(
        blocks, AXES, split_axis=0, concat_axis=0, tiled=True, axis_index_groups=CHIPS
    )
    return pl.pallas_call(
        unpack_kernel,
        out_shape=jax.ShapeDtypeStruct((Z, T, T), F32),
        in_specs=[VMEM],
        out_specs=VMEM,
        compiler_params=PARAMS,
        name="unpack",
    )(home)


def solution(mesh):
    placed = (
        P(None, "gx", "gy"),
        P(None, None, "gx", "gy"),
        P(),
        P(),
        P(None, "gx"),
        P(None, "gx", "gy"),
    )
    return jax.shard_map(
        body, mesh=mesh, in_specs=placed, out_specs=P(None, "gx", "gy"), check_vma=False
    )
```

```python
import jax
import jax.numpy as jnp
from jax import lax
from jax.experimental import pallas as pl
from jax.experimental.pallas import tpu as pltpu
from jax.sharding import PartitionSpec as P

ITERS = 2
V = 4
Z = 2
T = 128
ROWS = 16
GY = 16
GX = 8
CHUNKS = 64
META = 16
UNIT = ROWS * (1 + V) + 8
AXES = ("gx", "gy")
F32 = jnp.float32
BF16 = jnp.bfloat16
VMEM = pl.BlockSpec(memory_space=pltpu.VMEM)
COST = pl.CostEstimate(flops=1_000_000_000, bytes_accessed=4_000_000, transcendentals=0)
HBM = pl.BlockSpec(memory_space=pltpu.HBM)
SMEM = pl.BlockSpec(memory_space=pltpu.SMEM)
PARAMS = pltpu.CompilerParams(vmem_limit_bytes=48 * 1024 * 1024)


def device_of(plane, chunk):
    core, block = chunk % 2, chunk // 2
    group, tile, part = block // 8, block % 8 // 4, block % 4
    inner = (tile == 0) == (group % 2 == 0)
    row = (1 if inner else 0, 2 if inner else 3)[plane]
    return (2 * group + core) * GY + 4 * row + (part if tile == 0 else 3 - part)


def both_ways(pairs):
    return [(a, b) for a, b in pairs] + [(b, a) for a, b in pairs]


SWAP = both_ways([(2 * x * GY + g, (2 * x + 1) * GY + g) for x in range(GX // 2) for g in range(GY)])
PAIR = both_ways(
    [
        (device_of(p, q), device_of(p, q + 1))
        for p in range(Z) for q in range(1, CHUNKS - 1, 2)
    ]
    + [(device_of(0, q), device_of(1, q)) for q in (0, CHUNKS - 1)]
)


CHIPS = [[(2 * x + c) * GY + g for c in range(2) for g in range(GY)] for x in range(GX // 2)]


def own_tile_inner():
    core, group = lax.axis_index("gx") % 2, lax.axis_index("gx") // 2
    return core, (core + group) % 2 == 0


def here():
    core, group = lax.axis_index("gx") % 2, lax.axis_index("gx") // 2
    row, col = lax.axis_index("gy") // 4, lax.axis_index("gy") % 4
    inner = jnp.where((row == 1) | (row == 2), 1, 0)
    first_tile = (inner + group) % 2 == 1
    block = 8 * group + jnp.where(first_tile, col, 7 - col)
    paired = jnp.where(core == 0, block > 0, block < CHUNKS // 2 - 1)
    return core, jnp.where(paired, 1.0, 0.0).astype(F32)


def part_of(col, core):
    return jnp.where(core == 0, col, 3 - col)


def split(x):
    hi = x.astype(BF16)
    return hi, (x - hi.astype(F32)).astype(BF16)


def pack(sub, slot_of, out_ref, codes_hbm, shifts_hbm, est_hbm, views_hbm, codes_ref, shifts_ref, est, views, sems):
    core, _ = own_tile_inner()
    copies = [
        pltpu.make_async_copy(codes_hbm, codes_ref, sems.at[0]),
        pltpu.make_async_copy(shifts_hbm, shifts_ref, sems.at[1]),
        pltpu.make_async_copy(est_hbm.at[:, :, sub], est, sems.at[2]),
        pltpu.make_async_copy(views_hbm.at[:, :, :, sub], views, sems.at[3]),
    ]
    for copy in copies:
        copy.start()
    for copy in copies:
        copy.wait()
    lane = lax.broadcasted_iota(jnp.int32, (8, T), 1)
    for slot in range(8):
        plane, part, at = slot // 4, part_of(slot % 4, core), slot_of(slot)
        block = 4 * part + 2 * sub
        meta = jnp.zeros((8, T), F32)
        for half in range(2):
            for v in range(V):
                code = codes_ref[v, block + half].astype(F32)
                shift = shifts_ref[v, block + half].astype(F32)
                meta = jnp.where(lane == half * V + v, code, meta)
                meta = jnp.where(lane == 8 + half * V + v, shift, meta)
        out_ref[at, 0:ROWS, :] = est[plane, part]
        for v in range(V):
            out_ref[at, pl.ds(ROWS * (1 + v), ROWS), :] = views[v, plane, part].astype(F32)
        out_ref[at, pl.ds(ROWS * (1 + V), 8), :] = meta


def halves(near):
    return jnp.where(near, 4, 0), jnp.where(near, 8, 12)


def send_kernel(codes_hbm, shifts_hbm, est_hbm, views_hbm, send_ref, *scratch):
    core, _ = own_tile_inner()
    pack(1 - core, lambda slot: slot, send_ref, codes_hbm, shifts_hbm, est_hbm, views_hbm, *scratch)


def keep_kernel(codes_hbm, shifts_hbm, est_hbm, views_hbm, out_ref, *scratch):
    core, inner = own_tile_inner()
    starts = halves(inner)
    pack(
        core, lambda slot: starts[slot // 4] + slot % 4, out_ref,
        codes_hbm, shifts_hbm, est_hbm, views_hbm, *scratch,
    )


def join_kernel(kept_ref, other_ref, out_ref):
    _, inner = own_tile_inner()
    for i, start in enumerate(halves(jnp.logical_not(inner))):
        out_ref[pl.ds(start, 4)] = other_ref[4 * i : 4 * i + 4]


def lead_kernel(arrived_ref, out_ref):
    for c in range(GY):
        out_ref[ROWS * c : ROWS * c + ROWS, :] = arrived_ref[c, 0:ROWS, :]
        meta = arrived_ref[c, ROWS * (1 + V) : ROWS * (1 + V) + 1, :]
        out_ref[GY * ROWS + c : GY * ROWS + c + 1, :] = meta


def inside_kernel(paired_ref, out_ref):
    _, has_pair = here()
    out_ref[...] = paired_ref[...] * has_pair


def update_kernel(own_ref, mid_ref, paired_ref, swapped_ref, out_ref):
    total = mid_ref[...] + paired_ref[...] + swapped_ref[...]
    out_ref[...] = own_ref[0 : GY * ROWS, :] * (total * 0.25)


def twice_kernel(own_ref, mid_ref, paired_ref, swapped_ref, out_ref):
    total = mid_ref[...] + paired_ref[...] + swapped_ref[...]
    updated = own_ref[0 : GY * ROWS, :] * (total * 0.25)
    for copy in range(2):
        out_ref[GY * ROWS * copy : GY * ROWS * (copy + 1), :] = updated


def unpack_kernel(home_ref, out_ref):
    core, inner = own_tile_inner()
    for slot in range(8):
        plane, col = slot // 4, slot % 4
        source = jnp.where(inner, 4 + slot, 12 * plane + col)
        for sub in range(2):
            at = (2 * part_of(col, core) + sub) * ROWS
            rows = pl.ds(pl.multiple_of(at, ROWS), ROWS)
            out_ref[plane, rows, :] = home_ref[GY * sub + source]


def put_split(ref, v, pieces, stacked=False):
    axis = 0 if stacked else 1
    hi = jnp.concatenate([p[0] for p in pieces], axis=axis)
    lo = jnp.concatenate([p[1] for p in pieces], axis=axis)
    ref[v] = jnp.concatenate(
        [
            jnp.concatenate([hi, hi], axis=1),
            jnp.concatenate([lo, jnp.zeros_like(lo)], axis=1),
        ],
        axis=0,
    )


def base_rows(psf_ref, width, at):
    taps = psf_ref[...]
    taps = taps / jnp.sum(taps, axis=1, keepdims=True)
    lane = lax.broadcasted_iota(jnp.int32, (V, width), 1)
    back, straight = jnp.zeros((V, width), F32), jnp.zeros((V, width), F32)
    count = taps.shape[1]
    for t in range(count):
        tap = jnp.broadcast_to(taps[:, t : t + 1], (V, width))
        back = jnp.where(lane == at[0] + count - 1 - t, tap, back)
        straight = jnp.where(lane == at[1] + t, tap, straight)
    return back, straight


def taps_kernel(
    psf_rows_ref, psf_cols_ref, band_ref, pair_in_ref, near_in_ref, pair_back_ref, near_back_ref
):
    core, _ = own_tile_inner()
    col_bases = base_rows(psf_cols_ref, 2 * T, (177, 177))
    back_base, row_base = base_rows(psf_rows_ref, T, (T - 31, 1))

    def either(a, b):
        return tuple(jnp.where(core == 0, x, y) for x, y in zip(a, b))

    def turned(base, count, width):
        rows = jnp.broadcast_to(base, (count, base.shape[1]))
        return split(pltpu.roll(rows, 0, 1, stride=1, stride_axis=0)[:, :width])

    for v in range(V):
        for d in range(2):
            hi, lo = turned(col_bases[d][v : v + 1], 2 * T, T)
            band_ref[v, d, 0 : 2 * T, 0:T] = hi
            band_ref[v, d, 0 : 2 * T, T : 2 * T] = lo
            band_ref[v, d, 2 * T : 4 * T, 0:T] = hi
            band_ref[v, d, 2 * T : 4 * T, T : 2 * T] = jnp.zeros_like(lo)
        before, own, after = [
            turned(pltpu.roll(jnp.broadcast_to(row_base[v : v + 1], (8, T)), (T - ROWS * i) % T, 1)[0:1], ROWS, ROWS) for i in range(3)
        ]
        put_split(pair_in_ref, v, [either(before, after)])
        put_split(near_in_ref, v, [own, either(after, before)])
        before, own, after = [
            turned(pltpu.roll(jnp.broadcast_to(back_base[v : v + 1], (8, T)), ROWS * i, 1)[0:1], ROWS, ROWS) for i in range(3)
        ]
        put_split(pair_back_ref, v, [either(before, after)], stacked=True)
        put_split(near_back_ref, v, [own, either(after, before)], stacked=True)


def column_pass(pieces, band):
    lane = lax.broadcasted_iota(jnp.int32, (ROWS, T), 1)
    turned = [pltpu.roll(p, T // 2, 1) for p in pieces]
    zero = jnp.zeros((ROWS, T), F32)
    turned = [zero] + turned + [zero]
    moved = [
        jnp.where(lane < T // 2, turned[j], turned[j + 1]) for j in range(len(pieces) + 1)
    ]
    his, los = zip(*[split(m) for m in moved])
    done = []
    for half in range(2):
        windows = [
            jnp.concatenate([his[c], his[c + 1], los[c], los[c + 1]], axis=1)
            for c in range(half * len(pieces) // 2, (half + 1) * len(pieces) // 2)
        ]
        both = jnp.dot(jnp.concatenate(windows, axis=0), band, preferred_element_type=F32)
        done.append(both[:, :T] + both[:, T:])
    return jnp.concatenate(done, axis=0)


def column_tiles(ref, v):
    return [ref[v, :, T * c : T * c + T] for c in range(GY)]


def own_block(ref, half):
    return ref[0 : GY * ROWS, :].reshape(GY, ROWS, T)[:, 8 * half : 8 * half + 8, :]


def inner_lanes():
    lane = lax.broadcasted_iota(jnp.int32, (8, T), 1)
    return jnp.where(lane < T - 1, 1.0 / 16.0, 0.0).astype(F32)


def put_twice(b, x, est2, slope2):
    d = (pltpu.roll(x, T - 1, 2) - x) * inner_lanes()
    for copy in range(2):
        est2[b, GY * copy : GY * copy + GY] = x
        slope2[b, GY * copy : GY * copy + GY] = d


def code_of(meta_ref, v, b, c):
    return meta_ref[GY * (b // 2) + c, b % 2 * V + v].astype(F32)


def shift_of(meta_ref, v, b):
    return meta_ref[GY * (b // 2), 8 + b % 2 * V + v]


def gather(v, meta_ref, est2, slope2, view_u):
    count = est2.shape[0] // 2
    for src in range(count):
        parts = []
        for b in (2 * src, 2 * src + 1):
            shift = shift_of(meta_ref, v, b)
            x = est2[b, pl.ds(shift, GY)]
            d = slope2[b, pl.ds(shift, GY)]
            parts.append([x[c] + code_of(meta_ref, v, b, c) * d[c] for c in range(GY)])
        for c in range(GY):
            hi, lo = split(jnp.concatenate([parts[0][c], parts[1][c]], axis=0))
            cols = slice(T * c, T * c + T)
            view_u[v, ROWS * src : ROWS * src + ROWS, cols] = hi
            view_u[v, ROWS * (count + src) : ROWS * (count + src + 1), cols] = lo


def product(weights, values):
    both = jnp.dot(weights, values, preferred_element_type=F32)
    return both[: both.shape[0] // 2] + both[both.shape[0] // 2 :]


def rows_back(v, meta_ref, back_ref, again, total2):
    his, los = zip(*[split(again[v, ROWS * c : ROWS * c + ROWS, :]) for c in range(GY)])
    values = jnp.concatenate(
        [jnp.concatenate(his, axis=1), jnp.concatenate(los, axis=1)], axis=0
    )
    spread = product(back_ref[v], values)
    inner = inner_lanes()
    for b in range(total2.shape[0]):
        parts = []
        for c in range(GY):
            r = spread[8 * b : 8 * b + 8, T * c : T * c + T]
            g = r * inner
            g = pltpu.roll(g, 1, 1) - g
            parts.append(r + code_of(meta_ref, v, b, c) * g)
        total2[b, pl.ds(shift_of(meta_ref, v, b), GY)] += jnp.stack(parts)


def put_joined(ref, src, total2):
    for half in range(2):
        b = 2 * src + half
        y = total2[b, 0:GY] + total2[b, GY : 2 * GY]
        for c in range(GY):
            ref[ROWS * c + 8 * half : ROWS * c + 8 * half + 8, :] = y[c]


def for_views(stages):
    for stage in stages:
        for v in range(V):
            stage(v)


def front_kernel(meta_ref, own_ref, swapped_ref, near_in_ref, smooth_ref, est2, slope2, view_u):
    for src, ref in enumerate((own_ref, swapped_ref)):
        for half in range(2):
            put_twice(2 * src + half, own_block(ref, half), est2, slope2)

    def rows_in(v):
        smooth_ref[v] = product(near_in_ref[v], view_u[v])

    for_views((lambda v: gather(v, meta_ref, est2, slope2, view_u), rows_in))


def core_kernel(
    meta_ref, paired_ref, near_ref, arrived_ref, band_ref, pair_in_ref, pair_back_ref,
    pair_ref, again_ref, est2, slope2, view_u, total2, smooth, ratio,
):
    _, has_pair = here()
    for half in range(2):
        put_twice(half, own_block(paired_ref, half) * has_pair, est2, slope2)
    total2[...] = jnp.zeros(total2.shape, F32)

    def rows_in(v):
        smooth[v] = near_ref[v] + product(pair_in_ref[v], view_u[v])

    def cols_in(v):
        blurred = column_pass(column_tiles(smooth, v), band_ref[v, 0])
        for c in range(GY):
            ratio[v, :, T * c : T * c + T] = (
                arrived_ref[c, ROWS * (1 + v) : ROWS * (2 + v), :]
                / blurred[ROWS * c : ROWS * c + ROWS, :]
            )

    def cols_back(v):
        again_ref[v] = column_pass(column_tiles(ratio, v), band_ref[v, 1])

    for_views((
        lambda v: gather(v, meta_ref, est2, slope2, view_u),
        rows_in,
        cols_in,
        cols_back,
        lambda v: rows_back(v, meta_ref, pair_back_ref, again_ref, total2),
    ))
    put_joined(pair_ref, 0, total2)


def tail_kernel(meta_ref, again_ref, near_back_ref, mid_ref, swap_ref, total2):
    total2[...] = jnp.zeros(total2.shape, F32)
    for v in range(V):
        rows_back(v, meta_ref, near_back_ref, again_ref, total2)
    put_joined(mid_ref, 0, total2)
    put_joined(swap_ref, 1, total2)


def all_to_all(blocks):
    blocks = pltpu.with_memory_space_constraint(blocks, pltpu.VMEM)
    return lax.all_to_all(blocks, "gy", split_axis=0, concat_axis=0, tiled=True)


def body(estimate, views, psf_rows, psf_cols, shifts, codes):
    _, inner = own_tile_inner()
    taken = [
        pltpu.with_memory_space_constraint(a, pltpu.HBM)
        for a in (
            codes[:, :, 0],
            shifts,
            estimate.reshape(Z, 4, 2, ROWS, T),
            views.reshape(V, Z, 4, 2, ROWS, T),
        )
    ]
    room = [
        pltpu.SMEM((V, 2 * 8), jnp.int32),
        pltpu.SMEM((V, 2 * 8), jnp.int32),
        pltpu.VMEM((Z, 4, ROWS, T), F32),
        pltpu.VMEM((V, Z, 4, ROWS, T), BF16),
        pltpu.SemaphoreType.DMA((4,)),
    ]
    unit = jax.ShapeDtypeStruct((8, UNIT, T), F32)
    whole = jax.ShapeDtypeStruct((GY, UNIT, T), F32)
    send = pl.pallas_call(
        send_kernel,
        out_shape=unit,
        in_specs=[HBM] * 4,
        out_specs=VMEM,
        scratch_shapes=room,
        compiler_params=PARAMS,
        name="send",
    )(*taken)
    other = lax.ppermute(send, AXES, SWAP)
    kept = pl.pallas_call(
        keep_kernel,
        out_shape=whole,
        in_specs=[HBM] * 4,
        out_specs=VMEM,
        scratch_shapes=room,
        compiler_params=PARAMS,
        cost_estimate=COST,
        name="keep",
    )(*taken)
    joined = pl.pallas_call(
        join_kernel,
        out_shape=whole,
        in_specs=[VMEM, VMEM],
        out_specs=VMEM,
        input_output_aliases={0: 0},
        compiler_params=PARAMS,
        name="join",
    )(kept, other)

    band, pair_in, near_in, pair_back, near_back = pl.pallas_call(
        taps_kernel,
        out_shape=(
            jax.ShapeDtypeStruct((V, 2, 4 * T, 2 * T), BF16),
            jax.ShapeDtypeStruct((V, 2 * ROWS, 2 * ROWS), BF16),
            jax.ShapeDtypeStruct((V, 2 * ROWS, 4 * ROWS), BF16),
            jax.ShapeDtypeStruct((V, 2 * ROWS, 2 * ROWS), BF16),
            jax.ShapeDtypeStruct((V, 4 * ROWS, 2 * ROWS), BF16),
        ),
        in_specs=[VMEM, VMEM],
        out_specs=(VMEM,) * 5,
        compiler_params=PARAMS,
        name="taps",
    )(psf_rows, psf_cols)

    arrived = all_to_all(joined)
    lead = pl.pallas_call(
        lead_kernel,
        out_shape=jax.ShapeDtypeStruct((GY * ROWS + GY, T), F32),
        in_specs=[VMEM],
        out_specs=VMEM,
        compiler_params=PARAMS,
        name="lead",
    )(arrived)
    own_meta = lead[GY * ROWS :, :META]
    update, update_twice = [
        pl.pallas_call(
            kernel,
            out_shape=jax.ShapeDtypeStruct((count * GY * ROWS, T), F32),
            in_specs=[VMEM] * 4,
            out_specs=VMEM,
            compiler_params=PARAMS,
            name=name,
        )
        for kernel, count, name in ((update_kernel, 1, "update"), (twice_kernel, 2, "last"))
    ]
    chunk = jax.ShapeDtypeStruct((GY * ROWS, T), F32)
    inside = pl.pallas_call(
        inside_kernel,
        out_shape=chunk,
        in_specs=[VMEM],
        out_specs=VMEM,
        compiler_params=PARAMS,
        cost_estimate=COST,
        name="inside",
    )
    doubled = [pltpu.VMEM((b, 2 * GY, 8, T), F32) for b in (2, 4)]
    front = pl.pallas_call(
        front_kernel,
        out_shape=jax.ShapeDtypeStruct((V, ROWS, GY * T), F32),
        in_specs=[SMEM] + [VMEM] * 3,
        out_specs=VMEM,
        scratch_shapes=[doubled[1], doubled[1], pltpu.VMEM((V, 4 * ROWS, GY * T), BF16)],
        compiler_params=PARAMS,
        name="front",
    )
    middle = pl.pallas_call(
        core_kernel,
        out_shape=(chunk, jax.ShapeDtypeStruct((V, GY * ROWS, T), F32)),
        in_specs=[SMEM] + [VMEM] * 6,
        out_specs=(VMEM, VMEM),
        scratch_shapes=[
            doubled[0],
            doubled[0],
            pltpu.VMEM((V, 2 * ROWS, GY * T), BF16),
            doubled[0],
            pltpu.VMEM((V, ROWS, GY * T), F32),
            pltpu.VMEM((V, ROWS, GY * T), F32),
        ],
        compiler_params=PARAMS,
        cost_estimate=COST,
        name="middle",
    )
    tail = pl.pallas_call(
        tail_kernel,
        out_shape=(chunk, chunk),
        in_specs=[SMEM] + [VMEM] * 2,
        out_specs=(VMEM, VMEM),
        scratch_shapes=[doubled[1]],
        compiler_params=PARAMS,
        cost_estimate=COST,
        name="tail",
    )
    own = lead
    for sweep in range(ITERS):
        paired = lax.ppermute(own, AXES, PAIR)
        swapped = lax.ppermute(own, AXES, SWAP)
        if sweep == 0:
            near_meta = jnp.concatenate(
                [own_meta, swapped[GY * ROWS :, :META]], axis=0
            ).astype(jnp.int32)
        near = front(near_meta, own, swapped, near_in)
        if sweep == 0:
            pair_meta = (paired[GY * ROWS :, :META] + 0.0 * near[0, :, :META]).astype(jnp.int32)
        pair, again = middle(pair_meta, paired, near, arrived, band, pair_in, pair_back)
        mid, swap = tail(near_meta, again, near_back)
        own = (update if sweep < ITERS - 1 else update_twice)(
            own, mid, inside(lax.ppermute(pair, AXES, PAIR)), lax.ppermute(swap, AXES, SWAP)
        )
    blocks = pltpu.with_memory_space_constraint(own.reshape(2 * GY, ROWS, T), pltpu.VMEM)
    home = lax.all_to_all(
        blocks, AXES, split_axis=0, concat_axis=0, tiled=True, axis_index_groups=CHIPS
    )
    return pl.pallas_call(
        unpack_kernel,
        out_shape=jax.ShapeDtypeStruct((Z, T, T), F32),
        in_specs=[VMEM],
        out_specs=VMEM,
        compiler_params=PARAMS,
        name="unpack",
    )(home)


def solution(mesh):
    placed = (
        P(None, "gx", "gy"),
        P(None, None, "gx", "gy"),
        P(),
        P(),
        P(None, "gx"),
        P(None, "gx", "gy"),
    )
    return jax.shard_map(
        body, mesh=mesh, in_specs=placed, out_specs=P(None, "gx", "gy"), check_vma=False
    )
```
